512 devices in a mesh: seq: 32 (over z, core), coarse: 4 (over y), exp: 4 (over x).
Axes of the slice: x: 4, y: 4, z: 16, core: 2. Of those that a mesh axis runs over, the one named last changes fastest.
Arguments:
- bytes_in: bfloat16 [4, 16384, 1024], P('exp', 'seq'), may hold values from -6 to 6
- norm_gain: float32 [1024], replicated, may hold values from 0.5 to 1.5
- qkv_weight: bfloat16 [3, 1024, 1024], P(None, None, 'coarse'), may hold values from -0.1875 to 0.1875
- gate_weight_enc: bfloat16 [2, 1024, 8], P(None, None, 'coarse'), may hold values from -0.1875 to 0.1875
- decay_rate: float32 [8], P('coarse'), may hold values from 0 to 0.05
- write_bias: float32 [8], P('coarse')
- head_gain: float32 [1024], P('coarse'), may hold values from 0.25 to 1.75
- boundaries: int32 [4, 16384], P('exp', 'seq'), may hold values from 0 to 1, as said below
- picks: int32 [4, 4096, 8], P('exp', ('seq', 'coarse')), may hold values from 0 to 127, as said below
- pick_gates: float32 [4, 4096, 8], P('exp', ('seq', 'coarse')), may hold values from 0.05 to 0.5
- extension: bfloat16 [1024], replicated, may hold values from -6 to 6
- expert_gate: bfloat16 [128, 2048, 512], P(('seq', 'exp'), 'coarse'), may hold values from -0.125 to 0.125
- expert_up: bfloat16 [128, 2048, 512], P(('seq', 'exp'), 'coarse'), may hold values from -0.125 to 0.125
- expert_down: bfloat16 [128, 512, 1024], P(('seq', 'exp'), None, 'coarse'), may hold values from -0.25 to 0.25
Outputs:
- mixed: bfloat16 [4, 16384, 1024], P('exp', 'seq', 'coarse')
The draws below stay inside these ranges and needn't reach their ends.
Inputs may be any that keep to these rules, and one draw needn't show every extreme that they name: Byte 0 of every sequence is a boundary. Each byte block holds 64 to 128 boundaries, and in every sequence some block holds exactly 128. `picks`: row b * 128 + s belongs to the s-th boundary of byte block b; rows past the block's number of boundaries are unused. Each row names 8 different experts. Within each aligned run of 32 rows no expert is named more than 2 times by used rows, and a run whose rows are all used names every expert exactly 2 times.
All inputs are finite; a program needn't handle non-finite values.
Results may differ from the reference program's by a relative error of at most 0.0063.
Values may be sent and summed in bfloat16 or wider, within the bound.
No kernel may reach another device: no remote copies, remote signals or barrier semaphores. Data moves between devices by JAX's collectives and lax.ppermute only.
A program may use at most 64 MiB of HBM per device.

```python
import jax
import jax.numpy as jnp
from jax import lax

D = 1024
HEADS = 8
HEAD_DIM = 128
D_MAIN = 2048
FF = 512
TOP = 8
BLOCK = 64
BYTE_DEV = 512
MOST = 128
SLOT_DEV = 32
EXPERTS = 128
CAP = 2
LENGTH = 16384
SEQS = 4
N_SEQ = 32
N_COARSE = 4


def pick_slow(key, slow_total):
    ordering = jax.random.permutation(key, HEADS)
    return ordering < slow_total


def draw_decay_rate(key, part):
    slow_heads = pick_slow(key, HEADS // 2)
    key = jax.random.fold_in(key, 3)
    first_key, second_key = jax.random.split(key)
    slow_rate = jax.random.uniform(first_key, (HEADS,), jnp.float32, 0.3, 1.2) / LENGTH
    fast_rate = jnp.exp(jax.random.uniform(second_key, (HEADS,), jnp.float32, jnp.log(1.0 / 50.0), jnp.log(1.0 / 20.0)))
    return jnp.where(slow_heads, slow_rate, fast_rate).astype(jnp.float32)


def draw_write_bias(key, part):
    slow_heads = pick_slow(key, HEADS // 2)
    key = jax.random.fold_in(key, 4)
    first_key, second_key = jax.random.split(key)
    slow_bias = jnp.log(64.0 / LENGTH) + jax.random.uniform(first_key, (HEADS,), jnp.float32, -0.3, 0.3)
    fast_bias = jax.random.uniform(second_key, (HEADS,), jnp.float32, -1.0, 1.0)
    return jnp.where(slow_heads, slow_bias, fast_bias).astype(jnp.float32)


def draw_boundaries(key, part):
    key = jax.random.fold_in(key, 7)
    count_key, full_key, order_key = jax.random.split(key, 3)
    block_total = SEQS * N_SEQ
    counts = jax.random.randint(count_key, (SEQS, N_SEQ), MOST // 2, MOST + 1)
    fullest = jax.random.randint(full_key, (SEQS, 1), 0, N_SEQ)
    counts = jnp.where(jnp.arange(N_SEQ)[None, :] == fullest, MOST, counts)
    ranking = jax.vmap(lambda block_key: jax.random.permutation(block_key, BYTE_DEV))(jax.random.split(order_key, block_total))
    ranking = ranking.reshape(SEQS, N_SEQ, BYTE_DEV)
    first_rank = ranking[:, :, :1]
    positions = jnp.arange(BYTE_DEV)[None, None, :]
    shifted = jnp.where(positions == 0, 0, jnp.where(ranking < first_rank, ranking + 1, ranking))
    ranking = jnp.where(jnp.arange(N_SEQ)[None, :, None] == 0, shifted, ranking)
    marked = (ranking < counts[:, :, None]).astype(jnp.int32)
    return marked.reshape(SEQS, N_SEQ * BYTE_DEV)


def draw_picks(key, part):
    key = jax.random.fold_in(key, 9)
    slot_key, turn_key, label_key = jax.random.split(key, 3)
    run_total = SEQS * N_SEQ * N_COARSE
    groups = EXPERTS // TOP
    slot_group = jax.vmap(lambda run_key: jax.random.permutation(run_key, SLOT_DEV))(jax.random.split(slot_key, run_total)) % groups
    rotation = jax.random.randint(turn_key, (run_total, SLOT_DEV, 1), 0, TOP)
    member = (jnp.arange(TOP)[None, None, :] + rotation) % TOP
    within = slot_group[:, :, None] + groups * member
    labels = jax.vmap(lambda run_key: jax.random.permutation(run_key, EXPERTS))(jax.random.split(label_key, run_total))
    chosen = jnp.take_along_axis(labels, within.reshape(run_total, SLOT_DEV * TOP), axis=1)
    return chosen.reshape(SEQS, N_SEQ * MOST, TOP).astype(jnp.int32)


def level_of(own_key, extent, cuts, smallest, top_value):
    loudness, own = 1.0, jax.random.fold_in(own_key, 6)
    for position, blocks in cuts:
        draws = jnp.exp(jax.random.uniform(jax.random.fold_in(own, position), (blocks,), jnp.float32, smallest / len(cuts), top_value / len(cuts)))
        loudness = loudness * jnp.repeat(draws, extent[position] // blocks).reshape([-1 if axis == position else 1 for axis in range(len(extent))])
    return loudness


def normal_values(own_key, shape, scale, limit, cuts=(), kind=jnp.bfloat16):
    values = jax.random.normal(own_key, shape, jnp.float32) * scale
    if len(cuts) > 0:
        values = level_of(own_key, shape, cuts, -0.22, 0.18) * values
    return jnp.clip(values, min=-limit, max=limit).astype(kind)


def setup_inputs(seed: int = 0) -> dict:
    key_of = jax.random.split(jax.random.key(seed), 15)
    return {
        "bytes_in": normal_values(key_of[0], (SEQS, LENGTH, D), 1.0, 6.0, ((0, 4), (1, 32))),
        "norm_gain": jnp.clip(1.0 + 0.1 * jax.random.normal(key_of[1], (D,), jnp.float32), 0.5, 1.5),
        "qkv_weight": normal_values(key_of[2], (3, D, D), D ** -0.5, 0.1875, ((2, 4),)),
        "gate_weight_enc": normal_values(key_of[3], (2, D, HEADS), D ** -0.5, 0.1875, ((2, 4),)),
        "decay_rate": draw_decay_rate(jax.random.fold_in(key_of[14], 71), 0),
        "write_bias": draw_write_bias(jax.random.fold_in(key_of[14], 71), 0),
        "head_gain": jnp.clip(1.0 + 0.15 * jax.random.normal(key_of[6], (D,), jnp.float32), 0.25, 1.75),
        "boundaries": draw_boundaries(jax.random.fold_in(key_of[14], 71), 0),
        "picks": draw_picks(jax.random.fold_in(key_of[14], 71), 0),
        "pick_gates": jnp.clip(0.05 + 0.45 * jax.random.uniform(key_of[9], (SEQS, N_SEQ * MOST, TOP), jnp.float32) ** level_of(key_of[9], (SEQS, N_SEQ * MOST, TOP), ((0, 4), (1, 128)), -0.2, 0.2), 0.05, 0.5),
        "extension": normal_values(key_of[10], (D_MAIN - D,), 1.0, 6.0),
        "expert_gate": normal_values(key_of[11], (EXPERTS, D_MAIN, FF), D_MAIN ** -0.5, 0.125, ((0, 128), (1, 4))),
        "expert_up": normal_values(key_of[12], (EXPERTS, D_MAIN, FF), D_MAIN ** -0.5, 0.125, ((0, 128), (1, 4))),
        "expert_down": normal_values(key_of[13], (EXPERTS, FF, D), FF ** -0.5, 0.25, ((0, 128), (2, 4))),
    }


precise = lax.Precision.HIGHEST

def block_terms(queries, key_vecs, write_rate, log_decay):
    block_len = write_rate.shape[-1]
    positions = jnp.arange(block_len)
    causal = positions[:, None] >= positions[None, :]
    strict = positions[:, None] > positions[None, :]
    cum_decay = jnp.cumsum(log_decay, axis=-1)
    gap_log = cum_decay[..., :, None] - cum_decay[..., None, :]
    decay_mat = jnp.where(causal, jnp.exp(jnp.where(causal, gap_log, 0.0)), 0.0)
    key_gram = jnp.einsum('...td,...sd->...ts', key_vecs, key_vecs, precision=precise)
    unit_lower = jnp.where(strict, write_rate[..., :, None] * decay_mat * key_gram, 0.0) + jnp.eye(block_len, dtype=jnp.float32)
    attend_mat = jnp.einsum('...td,...sd->...ts', queries, key_vecs, precision=precise) * decay_mat
    growth = jnp.exp(cum_decay)
    block_decay = growth[..., -1]
    key_decayed = key_vecs * jnp.exp(cum_decay[..., -1:] - cum_decay)[..., None]
    return (unit_lower, attend_mat, growth, key_decayed, block_decay)

def lower_solve(unit_lower, right_side):
    return lax.linalg.triangular_solve(unit_lower, right_side, left_side=True, lower=True, unit_diagonal=True)

def encode(byte_rows, norm_gain, qkv_weight, gate_weight_enc, decay_rate, write_bias, head_gain):
    byte_float = byte_rows.astype(jnp.float32)
    normed = (byte_float * lax.rsqrt(lax.optimization_barrier(jnp.mean(byte_float * byte_float, -1, keepdims=True)) + 1e-05) * norm_gain).astype(jnp.bfloat16)
    normed_float = normed.astype(jnp.float32)
    projected = jnp.einsum('td,cde->cte', normed_float, qkv_weight.astype(jnp.float32), precision=precise)
    linear_gates = jnp.einsum('td,cdh->cth', normed_float, gate_weight_enc.astype(jnp.float32), precision=precise)
    block_total = LENGTH // BLOCK

    def split_heads(array):
        return array.reshape(LENGTH, HEADS, HEAD_DIM).transpose(1, 0, 2).reshape(HEADS, block_total, BLOCK, HEAD_DIM)

    def unit_rows(array):
        heads_form = split_heads(jax.nn.silu(array))
        return heads_form * lax.rsqrt(lax.optimization_barrier(jnp.sum(heads_form * heads_form, -1, keepdims=True)) + 1e-06)

    def per_head(array):
        return array.T.reshape(HEADS, block_total, BLOCK)
    queries = unit_rows(projected[0])
    key_vecs = unit_rows(projected[1])
    values = split_heads(jax.nn.silu(projected[2]))
    write_rate = per_head(jax.nn.sigmoid(linear_gates[1] + write_bias[None, :]))
    log_decay = per_head(-decay_rate[None, :] * jax.nn.softplus(linear_gates[0]))
    unit_lower, attend_mat, growth, key_decayed, block_decay = block_terms(queries, key_vecs, write_rate, log_decay)

    def advance(carry_state, inputs):
        lower_b, attend_b, growth_b, decayed_b, scale_b, query_b, key_b, value_b, rate_b = inputs
        carried = jnp.einsum('htd,hde->hte', key_b, carry_state, precision=precise)
        update = lower_solve(lower_b, rate_b[..., None] * (value_b - growth_b[..., None] * carried))
        block_out = jnp.einsum('htd,hde->hte', growth_b[..., None] * query_b, carry_state, precision=precise)
        block_out = block_out + jnp.einsum('hts,hse->hte', attend_b, update, precision=precise)
        carry_state = scale_b[:, None, None] * carry_state + jnp.einsum('hsd,hse->hde', decayed_b, update, precision=precise)
        return (carry_state, block_out)
    stacked = tuple((jnp.moveaxis(array, 1, 0) for array in (unit_lower, attend_mat, growth, key_decayed, block_decay, queries, key_vecs, values, write_rate)))
    start_state = jnp.zeros((HEADS, HEAD_DIM, HEAD_DIM), jnp.float32)
    final_state, block_outs = lax.scan(advance, start_state, stacked)
    head_out = jnp.moveaxis(block_outs, 0, 1).reshape(HEADS, LENGTH, HEAD_DIM)
    head_norm = head_out * lax.rsqrt(lax.optimization_barrier(jnp.mean(head_out * head_out, -1, keepdims=True)) + 1e-06) * head_gain.reshape(HEADS, HEAD_DIM)[:, None, :]
    head_norm = head_norm.transpose(1, 0, 2).reshape(LENGTH, D).astype(jnp.bfloat16)
    return (byte_float + head_norm.astype(jnp.float32)).astype(jnp.bfloat16)

def reference(bytes_in, norm_gain, qkv_weight, gate_weight_enc, decay_rate, write_bias, head_gain, boundaries, picks, pick_gates, extension, expert_gate, expert_up, expert_down):
    hidden_bytes = lax.map(lambda seq_rows: encode(seq_rows, norm_gain, qkv_weight, gate_weight_enc, decay_rate, write_bias, head_gain), bytes_in)
    block_count = SEQS * N_SEQ
    byte_blocks = hidden_bytes.reshape(block_count, BYTE_DEV, D)
    bound_mask = boundaries.reshape(block_count, BYTE_DEV)
    bound_rank = jnp.cumsum(bound_mask, axis=1) - 1
    bound_count = lax.optimization_barrier(jnp.sum(bound_mask, axis=1))

    def slots_of(mask_row, rank_row):
        return jnp.zeros((MOST,), jnp.int32).at[jnp.where(mask_row == 1, rank_row, MOST)].set(jnp.arange(BYTE_DEV, dtype=jnp.int32), mode='drop')
    slot_pos = jax.vmap(slots_of)(bound_mask, bound_rank)
    stretch_rows = jnp.take_along_axis(byte_blocks, slot_pos[..., None], axis=1)
    tail_part = jnp.broadcast_to(extension, (block_count, MOST, D_MAIN - D))
    full_rows = jnp.concatenate([stretch_rows, tail_part], axis=-1)
    live_slots = jnp.arange(MOST)[None, :] < bound_count[:, None]
    quarter_count = block_count * N_COARSE
    quarter_rows = full_rows.reshape(quarter_count * SLOT_DEV, D_MAIN)
    live_quarter = live_slots.reshape(quarter_count, SLOT_DEV)
    expert_ids = picks.reshape(quarter_count, SLOT_DEV * TOP)
    live_flat = jnp.repeat(live_quarter, TOP, axis=1)

    def arrivals(ids_row, live_row):
        expert_hits = ((ids_row[:, None] == jnp.arange(EXPERTS)[None, :]) & live_row[:, None]).astype(jnp.int32)
        return lax.optimization_barrier(jnp.sum(expert_hits * (jnp.cumsum(expert_hits, axis=0) - 1), axis=1))
    arrival = jax.vmap(arrivals)(expert_ids, live_flat)
    column = (jnp.arange(quarter_count)[:, None] * CAP + arrival).astype(jnp.int32)
    row_index = (jnp.arange(quarter_count)[:, None] * SLOT_DEV + jnp.repeat(jnp.arange(SLOT_DEV), TOP)[None, :]).astype(jnp.int32)
    table = jnp.full((EXPERTS, quarter_count * CAP), quarter_count * SLOT_DEV, jnp.int32)
    table = table.at[jnp.where(live_flat, expert_ids, EXPERTS), column].set(row_index, mode='drop')
    flat_rows = jnp.concatenate([quarter_rows, jnp.zeros((1, D_MAIN), jnp.bfloat16)], axis=0)

    def expert_apply(operands):
        gate_w, up_w, down_w, index_row = operands
        rows_in = jnp.take(flat_rows, index_row, axis=0)
        gate_part = jnp.dot(rows_in.astype(jnp.float32), gate_w.astype(jnp.float32), preferred_element_type=jnp.float32)
        up_part = jnp.dot(rows_in.astype(jnp.float32), up_w.astype(jnp.float32), preferred_element_type=jnp.float32)
        expert_hidden = (jax.nn.silu(gate_part) * up_part).astype(jnp.bfloat16)
        return jnp.dot(expert_hidden.astype(jnp.float32), down_w.astype(jnp.float32), preferred_element_type=jnp.float32).astype(jnp.bfloat16)
    expert_value = lax.map(expert_apply, (expert_gate, expert_up, expert_down, table))
    gates_flat = pick_gates.reshape(quarter_count, SLOT_DEV * TOP)

    def combine_block(operands):
        ids_row, column_row, live_row, gate_row = operands
        picked = expert_value[jnp.where(live_row, ids_row, 0), column_row].astype(jnp.float32)
        weighted = jnp.where(live_row, gate_row, 0.0)[:, None] * picked
        return lax.optimization_barrier(jnp.sum(weighted.reshape(SLOT_DEV, TOP, D), axis=1))
    stretch_out = lax.map(combine_block, (expert_ids, column, live_flat, gates_flat)).reshape(block_count, MOST, D)
    last_rows = stretch_out[jnp.arange(block_count), bound_count - 1]
    previous = jnp.concatenate([jnp.zeros((1, D), jnp.float32), last_rows[:-1]], axis=0)
    previous = jnp.where((jnp.arange(block_count) % N_SEQ == 0)[:, None], 0.0, previous)
    lookup_rows = jnp.concatenate([stretch_out, previous[:, None, :]], axis=1)
    spread_rows = jnp.take_along_axis(lookup_rows, jnp.where(bound_rank < 0, MOST, bound_rank)[..., None], axis=1)
    mixed = (byte_blocks.astype(jnp.float32) + spread_rows).astype(jnp.bfloat16)
    return mixed.reshape(SEQS, LENGTH, D)
```

```python
import functools

import jax
import jax.numpy as jnp
from jax import lax
from jax.experimental import pallas as pl
from jax.experimental.pallas import tpu as pltpu
from jax.sharding import PartitionSpec as P

f32 = jnp.float32
bf16 = jnp.bfloat16
HALF = 256
GROUP = 4
VMEM_LIMIT = 48 * 1024 * 1024


def params():
    return pltpu.CompilerParams(vmem_limit_bytes=VMEM_LIMIT)


def whole(count):
    return [pl.BlockSpec(memory_space=pltpu.VMEM)] * count


def mm(a, b, dims=((1,), (0,))):
    return lax.dot_general(a, b, (dims, ((), ())), preferred_element_type=f32)


def split(x):
    high = x.astype(bf16)
    return high, (x - high.astype(f32)).astype(bf16)


def mm3(a, b, dims=((1,), (0,))):
    (ah, al), (bh, bl) = a, b
    return mm(ah, bh, dims) + (mm(ah, bl, dims) + mm(al, bh, dims))


def iota(shape, dim):
    return lax.broadcasted_iota(jnp.int32, shape, dim)


def as_row(column):
    size = column.shape[0]
    eye = iota((size, size), 0) == iota((size, size), 1)
    return jnp.sum(jnp.where(eye, column, 0.0), axis=0, keepdims=True)


def delta_kernel(
    x_ref, gain_ref, w_ref, gw_ref, rate_ref, bias_ref, ab_ref, q_ref, k_ref, sol_ref, cum_ref, low_h, low_l, inv
):
    rows = x_ref.shape[0]
    dim = HALF // 2
    x = x_ref[...].astype(f32)
    normed = (x * lax.rsqrt(jnp.mean(x * x, -1, keepdims=True) + 1e-05) * gain_ref[...]).astype(bf16)
    decay_in = mm(normed, gw_ref[0])
    write_in = mm(normed, gw_ref[1])
    write = jax.nn.sigmoid(write_in + bias_ref[...])
    soft = jnp.maximum(decay_in, 0.0) + jnp.log1p(jnp.exp(-jnp.abs(decay_in)))
    log_decay = -rate_ref[...] * soft
    tri = jnp.where(iota((rows, rows), 0) >= iota((rows, rows), 1), 1.0, 0.0).astype(bf16)
    part_h, rest = log_decay.astype(bf16), None
    rest = log_decay - part_h.astype(f32)
    part_m = rest.astype(bf16)
    part_l = (rest - part_m.astype(f32)).astype(bf16)
    cum = mm(tri, part_h) + (mm(tri, part_m) + mm(tri, part_l))
    cum_ref[...] = cum

    def act(index):
        value = mm(normed, w_ref[index])
        return value / (1.0 + jnp.exp(-value))

    q_all, k_all, v_all = act(0), act(1), act(2)
    strict = iota((HALF, HALF), 0) > iota((HALF, HALF), 1)
    keep = []
    for head in range(2):
        cols = slice(head * dim, (head + 1) * dim)
        q, k, v = q_all[:, cols], k_all[:, cols], v_all[:, cols]
        q = q * lax.rsqrt(jnp.sum(q * q, -1, keepdims=True) + 1e-06)
        k = k * lax.rsqrt(jnp.sum(k * k, -1, keepdims=True) + 1e-06)
        q_ref[:, cols] = q
        k_ref[:, cols] = k
        cum_col = cum[:, head : head + 1]
        cum_row = as_row(cum_col)
        beta = write[:, head : head + 1]
        kh, kl = split(k)
        cross = None
        for i, j in ((0, 0), (1, 1), (1, 0)):
            ri, rj = slice(i * HALF, (i + 1) * HALF), slice(j * HALF, (j + 1) * HALF)
            gram = mm3((kh[ri], kl[ri]), (kh[rj], kl[rj]), ((1,), (1,)))
            decay = jnp.exp(jnp.minimum(cum_col[ri] - cum_row[:, rj], 0.0))
            low = beta[ri] * decay * gram
            if i == j:
                low = jnp.where(strict, low, 0.0)
                low_h[2 * head + i], low_l[2 * head + i] = split(low)
                first = (iota((HALF, HALF), 0) >> 1) == (iota((HALF, HALF), 1) >> 1)
                eye = jnp.where(iota((HALF, HALF), 0) == iota((HALF, HALF), 1), 1.0, 0.0)
                inv[2 * head + i] = eye - jnp.where(first, low, 0.0)
            else:
                cross = split(low)
        right = jnp.concatenate([(beta * jnp.exp(cum_col)) * k, beta * v], axis=1)
        last = cum_col[rows - 1 : rows]
        keep.append((cross, right, k * jnp.exp(last - cum_col), jnp.exp(last)))

    def level(step, carry):
        r, c = iota((HALF, HALF), 0), iota((HALF, HALF), 1)
        above = ((r >> (step + 1)) == (c >> (step + 1))) & ((r >> step) > (c >> step))
        for m in range(4):
            t = inv[m]
            parts = split(t)
            zero = jnp.zeros((HALF, HALF), bf16)
            off = (jnp.where(above, low_h[m], zero), jnp.where(above, low_l[m], zero))
            inner = mm3(off, parts)
            inv[m] = t - mm3(parts, split(inner))
        return carry

    lax.fori_loop(1, 8, level, 0)
    for head in range(2):
        cross, right, k_end, scale = keep[head]
        first = mm3(split(inv[2 * head]), split(right[:HALF]))
        second = right[HALF:] - mm3(cross, split(first))
        second = mm3(split(inv[2 * head + 1]), split(second))
        solved = jnp.concatenate([first, second], axis=0)
        sol_ref[head] = solved
        ends = mm3(split(k_end), split(solved), ((0,), (0,)))
        eye = jnp.where(iota((dim, dim), 0) == iota((dim, dim), 1), 1.0, 0.0)
        ab_ref[head] = jnp.concatenate([scale * eye - ends[:, :dim], ends[:, dim:]], axis=1)


def local_kernel(q_ref, k_ref, sol_ref, cum_ref, map_ref, out_ref):
    dim = HALF // 2
    causal = iota((HALF, HALF), 0) >= iota((HALF, HALF), 1)
    for head in range(2):
        cols = slice(head * dim, (head + 1) * dim)
        q, k = q_ref[:, cols], k_ref[:, cols]
        cum_col = cum_ref[:, head : head + 1]
        cum_row = as_row(cum_col)
        (qh, ql), (kh, kl) = split(q), split(k)
        sh, sl = split(sol_ref[head])
        grown = jnp.exp(cum_col) * q
        for i in range(2):
            ri = slice(i * HALF, (i + 1) * HALF)
            total = None
            for j in range(i + 1):
                rj = slice(j * HALF, (j + 1) * HALF)
                attend = mm3((qh[ri], ql[ri]), (kh[rj], kl[rj]), ((1,), (1,)))
                attend = attend * jnp.exp(jnp.minimum(cum_col[ri] - cum_row[:, rj], 0.0))
                if i == j:
                    attend = jnp.where(causal, attend, 0.0)
                term = mm3(split(attend), (sh[rj], sl[rj]))
                total = term if total is None else total + term
            map_ref[head, ri] = grown[ri] - total[:, :dim]
            out_ref[head, ri] = total[:, dim:]


def compose(late, early):
    dim = late.shape[0]
    both = mm3(split(late[:, :dim]), split(early))
    return jnp.concatenate([both[:, :dim], both[:, dim:] + late[:, dim:]], axis=1)


def pair_kernel(core_ref, own_ref, got_ref, msg_ref, first_ref):
    dim = HALF // 2
    lead = core_ref[0] == 0
    own, got = own_ref[...], got_ref[...]
    early, late = jnp.where(lead, own, got), jnp.where(lead, got, own)
    first_ref[...] = early
    both = compose(late, early)
    eye = jnp.where(iota((dim, HALF), 0) == iota((dim, HALF), 1), 1.0, 0.0)
    msg_ref[...] = (both - eye).astype(bf16)


def group_kernel(place_ref, got_ref, before_ref, total_ref):
    dim = HALF // 2
    eye = jnp.where(iota((dim, HALF), 0) == iota((dim, HALF), 1), 1.0, 0.0)
    place = place_ref[0]
    running = eye
    before = eye
    for chip in range(GROUP):
        item = got_ref[chip].astype(f32) + eye
        running = item if chip == 0 else compose(item, running)
        if chip + 1 < GROUP:
            before = jnp.where(place == chip + 1, running, before)
    before_ref[...] = before
    total_ref[...] = running


def hop_kernel(total_ref, state_ref, out_ref):
    dim = HALF // 2
    moved = mm3(split(total_ref[:, :dim]), split(state_ref[...].astype(f32)))
    out_ref[...] = (moved + total_ref[:, dim:]).astype(bf16)


def enter_kernel(core_ref, before_ref, first_ref, state_ref, keep_ref, send_ref):
    dim = HALF // 2
    state = mm3(split(before_ref[:, :dim]), split(state_ref[...].astype(f32))) + before_ref[:, dim:]
    after = mm3(split(first_ref[:, :dim]), split(state)) + first_ref[:, dim:]
    lead = core_ref[0] == 0
    keep_ref[...] = jnp.where(lead, state, after)
    send_ref[...] = jnp.where(lead, after, state)


def finish_kernel(
    where_ref, map_ref, out_ref, keep_ref, got_ref, x_ref, gain_ref, mask_ref, rank_ref, hidden_ref, picked_ref
):
    dim = HALF // 2
    lead = where_ref[1] == 0
    keep, got = keep_ref[...], got_ref[...]
    states = (jnp.where(lead, keep, got), jnp.where(lead, got, keep))
    parts = []
    for head in range(2):
        out = out_ref[head] + mm3(split(map_ref[head]), split(states[head]))
        norm = out * lax.rsqrt(jnp.mean(out * out, -1, keepdims=True) + 1e-06)
        parts.append((norm * gain_ref[:, head * dim : (head + 1) * dim]).astype(bf16))
    normed = jnp.concatenate(parts, axis=1)
    hidden = (x_ref[...].astype(f32) + normed.astype(f32)).astype(bf16)
    hidden_ref[...] = hidden
    slots, rows = picked_ref.shape[0], hidden.shape[0]
    chosen = (iota((slots, rows), 0) == rank_ref[...]) & (mask_ref[...] == 1)
    picked_ref[...] = mm(jnp.where(chosen, 1.0, 0.0).astype(bf16), hidden).astype(bf16)


def route_kernel(where_ref, mask_ref, pick_ref, gate_ref, rank_ref, take_ref, weigh_ref):
    rows = mask_ref.shape[1]
    slots, top = pick_ref.shape
    total = take_ref.shape[1]
    mask = mask_ref[...]
    tri = jnp.where(iota((rows, rows), 0) <= iota((rows, rows), 1), 1.0, 0.0).astype(bf16)
    wide = jnp.broadcast_to(mask.astype(f32), (16, rows)).astype(bf16)
    rank_ref[...] = mm(wide, tri)[:1].astype(jnp.int32) - 1
    live = where_ref[0] * slots + iota((slots, total), 0) < jnp.sum(mask)
    column = iota((slots, total), 1)
    hit = jnp.zeros((slots, total), f32)
    weight = jnp.zeros((slots, total), f32)
    for pick in range(top):
        same = ((column >> 1) == pick_ref[:, pick : pick + 1]) & live
        hit = hit + jnp.where(same, 1.0, 0.0)
        weight = weight + jnp.where(same, gate_ref[:, pick : pick + 1], 0.0)
    earlier = jnp.where(iota((slots, slots), 0) > iota((slots, slots), 1), 1.0, 0.0).astype(bf16)
    arrival = mm(earlier, hit.astype(bf16)).astype(jnp.int32)
    here = (hit > 0.0) & (arrival == (column & 1))
    take_ref[...] = jnp.where(here, 1.0, 0.0).astype(bf16)
    weigh_ref[...] = jnp.where(here, weight, 0.0)


def dispatch_kernel(take_ref, got_ref, out_ref):
    take = take_ref[...]
    width = got_ref.shape[2]
    for part in range(got_ref.shape[0]):
        out_ref[:, part * width : (part + 1) * width] = mm(take, got_ref[part], ((0,), (0,))).astype(bf16)


def expert_kernel(rows_ref, weight_ref, ext_ref, out_ref):
    rows = rows_ref[...]
    depth = rows.shape[1]
    ext = jnp.broadcast_to(ext_ref[...].astype(f32), (16, depth)).astype(bf16)
    hidden = weight_ref.shape[0] // GROUP

    def part(start):
        cols = slice(start, start + hidden)
        offset = mm(ext, weight_ref[depth:, cols])[:1]
        return mm(rows, weight_ref[:depth, cols]) + offset

    gate, up = part(0), part(hidden)
    act = (gate / (1.0 + jnp.exp(-gate)) * up).astype(bf16)
    for c in range(GROUP):
        down = weight_ref[c * hidden : (c + 1) * hidden, 2 * hidden :]
        width = down.shape[1]
        out_ref[:, c * width : (c + 1) * width] = mm(act, down).astype(bf16)


def combine_kernel(weigh_ref, back_ref, out_ref):
    wh, wl = split(weigh_ref[...])
    width = out_ref.shape[2]
    for part in range(out_ref.shape[0]):
        back = back_ref[:, part * width : (part + 1) * width]
        out_ref[part] = mm(wh, back) + mm(wl, back)


def spread_kernel(hidden_ref, rank_ref, stretch_ref, prev_ref, out_ref):
    rows, slots = hidden_ref.shape[0], stretch_ref.shape[0]
    rank = rank_ref[...]
    chosen = jnp.where(iota((slots, rows), 0) == rank, 1.0, 0.0).astype(bf16)
    before = jnp.where(rank < 0, 1.0, 0.0)
    sh, sl = split(stretch_ref[...])
    spread = mm(chosen, sh, ((0,), (0,))) + mm(chosen, sl, ((0,), (0,)))
    size = rows
    eye = iota((size, size), 0) == iota((size, size), 1)
    before_col = jnp.sum(jnp.where(eye, before, 0.0), axis=1, keepdims=True)
    spread = jnp.where(before_col > 0.0, prev_ref[...], spread)
    out_ref[...] = (hidden_ref[...].astype(f32) + spread).astype(bf16)


def sds(shape, dtype):
    return jax.ShapeDtypeStruct(shape, dtype)


def call(kernel, outs, args, scalars=0, scratch=(), flops=10**8):
    smem = [pl.BlockSpec(memory_space=pltpu.SMEM)] * scalars
    return pl.pallas_call(
        kernel,
        out_shape=outs,
        in_specs=smem + whole(len(args) - scalars),
        out_specs=jax.tree.map(lambda _: pl.BlockSpec(memory_space=pltpu.VMEM), outs),
        scratch_shapes=list(scratch),
        compiler_params=params(),
        cost_estimate=pl.CostEstimate(flops=flops, bytes_accessed=10**6, transcendentals=0),
    )(*args)


def shards(
    bytes_in,
    norm_gain,
    qkv_weight,
    gate_weight_enc,
    decay_rate,
    write_bias,
    head_gain,
    boundaries,
    picks,
    pick_gates,
    extension,
    expert_gate,
    expert_up,
    expert_down,
):
    x = bytes_in[0]
    rows, width = x.shape
    dim = HALF // 2
    seq = lax.axis_index("seq")
    coarse = lax.axis_index("coarse")
    seq_total = lax.axis_size("seq")
    core = (seq % 2).astype(jnp.int32)
    place = ((seq // 2) % GROUP).astype(jnp.int32)
    local_slots = picks.shape[1]
    slot_total = local_slots * GROUP
    pair_total = local_slots * picks.shape[2]

    weights = jnp.concatenate([expert_gate[0], expert_up[0], expert_down[0]], axis=1)
    weights = lax.all_gather(weights, "coarse", axis=0, tiled=True)

    ab, q, k, solved, cum = call(
        delta_kernel,
        (
            sds((2, dim, HALF), f32),
            sds((rows, HALF), f32),
            sds((rows, HALF), f32),
            sds((2, rows, HALF), f32),
            sds((rows, 2), f32),
        ),
        (x, norm_gain[None], qkv_weight, gate_weight_enc, decay_rate[None], write_bias[None]),
        scratch=(
            pltpu.VMEM((4, HALF, HALF), bf16),
            pltpu.VMEM((4, HALF, HALF), bf16),
            pltpu.VMEM((4, HALF, HALF), f32),
        ),
        flops=2 * 10**9,
    )

    swap = [(i, i ^ 1) for i in range(seq_total)]
    own = lax.dynamic_index_in_dim(ab, core, 0, keepdims=False)
    give = lax.dynamic_index_in_dim(ab, 1 - core, 0, keepdims=False)
    got = lax.ppermute(give, "seq", swap)
    query_map, local_out = call(
        local_kernel,
        (sds((2, rows, dim), f32), sds((2, rows, dim), f32)),
        (q, k, solved, cum),
        flops=2 * 10**9,
    )
    spots = jnp.stack([coarse.astype(jnp.int32), core])
    rank, take, weigh = call(
        route_kernel,
        (sds((1, rows), jnp.int32), sds((local_slots, pair_total), bf16), sds((local_slots, pair_total), f32)),
        (spots, boundaries, picks[0], pick_gates[0]),
        scalars=1,
    )
    message, first = call(
        pair_kernel, (sds((dim, HALF), bf16), sds((dim, HALF), f32)), (core[None], own, got), scalars=1
    )
    stride = 2 * GROUP
    groups = [
        [stride * g + 2 * i + c for i in range(GROUP)] for g in range(seq_total // stride) for c in range(2)
    ]
    sent = jnp.broadcast_to(message[None], (GROUP, dim, HALF))
    chips = lax.all_to_all(sent, "seq", split_axis=0, concat_axis=0, tiled=True, axis_index_groups=groups)
    before, total = call(
        group_kernel, (sds((dim, HALF), f32), sds((dim, HALF), f32)), (place[None], chips), scalars=1
    )
    state = jnp.zeros((dim, dim), bf16)
    for hop in range(seq_total // stride - 1):
        if hop == 0:
            outgoing = total[:, dim:].astype(bf16)
        else:
            outgoing = call(hop_kernel, sds((dim, dim), bf16), (total, state))
        pairs = [(stride * hop + i, stride * (hop + 1) + i) for i in range(stride)]
        state = state + lax.ppermute(outgoing, "seq", pairs)
    keep, send = call(
        enter_kernel,
        (sds((dim, dim), f32), sds((dim, dim), f32)),
        (core[None], before, first, state),
        scalars=1,
    )
    other = lax.ppermute(send, "seq", swap)

    x_share = lax.dynamic_slice_in_dim(x, coarse * HALF, HALF, 1)
    hidden, picked = call(
        finish_kernel,
        (sds((rows, HALF), bf16), sds((slot_total, HALF), bf16)),
        (spots, query_map, local_out, keep, other, x_share, head_gain[None], boundaries, rank),
        scalars=1,
    )
    picked = lax.all_to_all(
        picked.reshape(GROUP, local_slots, HALF), "coarse", split_axis=0, concat_axis=0, tiled=True
    )
    outgoing = call(dispatch_kernel, sds((pair_total, width), bf16), (take, picked))
    experts = lax.axis_size(("seq", "exp"))
    capacity = pair_total // experts
    received = lax.all_to_all(
        outgoing.reshape(experts, capacity, width), ("seq", "exp"), split_axis=0, concat_axis=0, tiled=True
    )
    value = call(
        expert_kernel,
        sds((pair_total, width), bf16),
        (received.reshape(pair_total, width), weights, extension[None]),
    )
    returned = lax.all_to_all(
        value.reshape(experts, capacity, width), ("seq", "exp"), split_axis=0, concat_axis=0, tiled=True
    )
    stretch = call(
        combine_kernel,
        sds((GROUP, local_slots, HALF), f32),
        (weigh, returned.reshape(pair_total, width)),
    )
    stretch = lax.all_to_all(stretch, "coarse", split_axis=0, concat_axis=0, tiled=True)
    stretch = stretch.reshape(slot_total, HALF)
    last = lax.dynamic_slice_in_dim(stretch, rank[0, rows - 1], 1, 0)
    previous = lax.ppermute(last, "seq", [(i, i + 1) for i in range(seq_total - 1)])
    mixed = call(spread_kernel, sds((rows, HALF), bf16), (hidden, rank, stretch, previous))
    return mixed[None]


def solution(mesh):
    placed = (
        P("exp", "seq", None),
        P(),
        P(None, None, "coarse"),
        P(None, None, "coarse"),
        P("coarse"),
        P("coarse"),
        P("coarse"),
        P("exp", "seq"),
        P("exp", ("seq", "coarse"), None),
        P("exp", ("seq", "coarse"), None),
        P(),
        P(("seq", "exp"), "coarse", None),
        P(("seq", "exp"), "coarse", None),
        P(("seq", "exp"), None, "coarse"),
    )
    return jax.shard_map(
        shards, mesh=mesh, in_specs=placed, out_specs=P("exp", "seq", "coarse"), check_vma=False
    )
```

```python
import jax
import jax.numpy as jnp
from jax import lax
from jax.experimental import pallas as pl
from jax.experimental.pallas import tpu as pltpu
from jax.sharding import PartitionSpec as P

f32 = jnp.float32
bf16 = jnp.bfloat16
HALF = 256
GROUP = 4


def mm(a, b, dims=((1,), (0,))):
    return lax.dot_general(a, b, (dims, ((), ())), preferred_element_type=f32)


def split(x):
    high = x.astype(bf16)
    return high, (x - high.astype(f32)).astype(bf16)


def mm3(a, b, dims=((1,), (0,))):
    (ah, al), (bh, bl) = a, b
    return mm(ah, bh, dims) + (mm(ah, bl, dims) + mm(al, bh, dims))


def iota(shape, dim):
    return lax.broadcasted_iota(jnp.int32, shape, dim)


def as_row(column):
    size = column.shape[0]
    eye = iota((size, size), 0) == iota((size, size), 1)
    return jnp.sum(jnp.where(eye, column, 0.0), axis=0, keepdims=True)


def delta_kernel(
    spots_ref,
    x_far,
    gain_far,
    w_far,
    gw_far,
    rate_far,
    bias_far,
    egate_far,
    eup_far,
    edown_far,
    own_ref,
    give_ref,
    q_ref,
    k_ref,
    sol_ref,
    cum_ref,
    share_ref,
    weights_ref,
    x_ref,
    gain_ref,
    w_ref,
    gw_ref,
    rate_ref,
    bias_ref,
    low,
    inv,
    sems,
):
    rows = x_ref.shape[0]
    dim = HALF // 2
    pairs = [(x_far, x_ref), (gain_far, gain_ref), (gw_far, gw_ref), (rate_far, rate_ref), (bias_far, bias_ref)]
    pairs.append((w_far, w_ref))
    start = 0
    for far in (egate_far, eup_far, edown_far):
        size = far.shape[2]
        pairs.append((far.at[0], weights_ref.at[:, pl.ds(start, size)]))
        start += size
    moves = [pltpu.make_async_copy(a, b, sems.at[n]) for n, (a, b) in enumerate(pairs)]
    for move in moves:
        move.start()
    for move in moves[:5]:
        move.wait()
    first = pl.multiple_of(spots_ref[1] * HALF, HALF)
    moves.append(pltpu.make_async_copy(x_ref.at[:, pl.ds(first, HALF)], share_ref, sems.at[9]))
    moves[9].start()

    x = x_ref[...].astype(f32)
    normed = (x * lax.rsqrt(jnp.mean(x * x, -1, keepdims=True) + 1e-05) * gain_ref[...]).astype(bf16)
    linear = mm(normed, jnp.concatenate([gw_ref[0], gw_ref[1]], axis=0), ((1,), (1,)))
    decay_in, write_in = linear[:, :2], linear[:, 2:]
    write = jax.nn.sigmoid(write_in + bias_ref[...])
    soft = jnp.maximum(decay_in, 0.0) + jnp.log1p(jnp.exp(-jnp.abs(decay_in)))
    log_decay = -rate_ref[...] * soft
    tri = jnp.where(iota((rows, rows), 0) >= iota((rows, rows), 1), 1.0, 0.0).astype(bf16)
    part_h = log_decay.astype(bf16)
    rest = log_decay - part_h.astype(f32)
    part_m = rest.astype(bf16)
    part_l = (rest - part_m.astype(f32)).astype(bf16)
    sums = mm(tri, jnp.concatenate([part_h, part_m, part_l], axis=1))
    cum = sums[:, 0:2] + (sums[:, 2:4] + sums[:, 4:6])
    cum_ref[...] = cum

    moves[5].wait()

    def act(index):
        value = mm(normed, w_ref[index])
        return value / (1.0 + jnp.exp(-value))

    q_all, k_all, v_all = act(0), act(1), act(2)
    strict = iota((HALF, HALF), 0) > iota((HALF, HALF), 1)
    pair = (iota((dim, dim), 0) >> 1) == (iota((dim, dim), 1) >> 1)
    eye = jnp.where(iota((dim, dim), 0) == iota((dim, dim), 1), 1.0, 0.0)
    keep = []
    for head in range(2):
        cols = slice(head * dim, (head + 1) * dim)
        q, k, v = q_all[:, cols], k_all[:, cols], v_all[:, cols]
        q = q * lax.rsqrt(jnp.sum(q * q, -1, keepdims=True) + 1e-06)
        k = k * lax.rsqrt(jnp.sum(k * k, -1, keepdims=True) + 1e-06)
        q_ref[:, cols] = q
        k_ref[:, cols] = k
        cum_col = cum[:, head : head + 1]
        cum_row = as_row(cum_col)
        beta = write[:, head : head + 1]
        kh, kl = split(k)
        deep = jnp.concatenate([kh, kl], axis=1)
        twice = jnp.concatenate([kh, kh], axis=1)
        cross = None
        inner = []
        for i, j in ((0, 0), (1, 1), (1, 0)):
            ri, rj = slice(i * HALF, (i + 1) * HALF), slice(j * HALF, (j + 1) * HALF)
            gram = mm(deep[ri], twice[rj], ((1,), (1,))) + mm(kh[ri], kl[rj], ((1,), (1,)))
            lower = beta[ri] * jnp.exp(jnp.minimum(cum_col[ri] - cum_row[:, rj], 0.0)) * gram
            if i == j:
                lower = jnp.where(strict, lower, 0.0)
                for sub in range(2):
                    rs = slice(sub * dim, (sub + 1) * dim)
                    block = 4 * head + 2 * i + sub
                    part = lower[rs, rs]
                    low[block] = jnp.concatenate(split(part), axis=1)
                    inv[block] = eye - jnp.where(pair, part, 0.0)
                inner.append(jnp.concatenate(split(lower[dim:, :dim]), axis=1))
            else:
                cross = split(lower)
        right = jnp.concatenate([(beta * jnp.exp(cum_col)) * k, beta * v], axis=1)
        last = cum_col[rows - 1 : rows]
        keep.append((cross, inner, right, k * jnp.exp(last - cum_col), jnp.exp(last)))

    def packed(left, block):
        wide = jnp.concatenate(split(block), axis=1)
        out = mm(left, jnp.concatenate([wide, wide], axis=0))
        return out[:, :dim] + out[:, dim:]

    def level(step, carry):
        r, c = iota((dim, HALF), 0), iota((dim, HALF), 1) & (dim - 1)
        above = ((r >> (step + 1)) == (c >> (step + 1))) & ((r >> step) > (c >> step))
        zero = jnp.zeros((dim, HALF), bf16)
        blocks = [inv[m] for m in range(8)]
        inside = [packed(jnp.where(above, low[m], zero), blocks[m]) for m in range(8)]
        for m in range(8):
            inv[m] = blocks[m] - packed(jnp.concatenate(split(blocks[m]), axis=1), inside[m])
        return carry

    lax.fori_loop(1, 7, level, 0)
    for head in range(2):
        cross, inner, right, k_end, scale = keep[head]
        full = []
        for i in range(2):
            top, bottom = inv[4 * head + 2 * i], inv[4 * head + 2 * i + 1]
            corner = packed(jnp.concatenate(split(bottom), axis=1), packed(inner[i], top))
            upper = jnp.concatenate([top, jnp.zeros_like(top)], axis=1)
            full.append(split(jnp.concatenate([upper, jnp.concatenate([-corner, bottom], axis=1)], axis=0)))
        first = mm3(full[0], split(right[:HALF]))
        second = right[HALF:] - mm3(cross, split(first))
        second = mm3(full[1], split(second))
        solved = jnp.concatenate([first, second], axis=0)
        sol_ref[head] = solved
        ends = mm3(split(k_end), split(solved), ((0,), (0,)))
        keep[head] = jnp.concatenate([scale * eye - ends[:, :dim], ends[:, dim:]], axis=1)
    lead = spots_ref[0] == 0
    own_ref[...] = jnp.where(lead, keep[0], keep[1])
    give_ref[...] = jnp.where(lead, keep[1], keep[0])
    for move in moves[6:]:
        move.wait()


def local_kernel(q_ref, k_ref, sol_ref, cum_ref, both_ref, token_ref):
    token_ref[...] = jnp.zeros_like(token_ref)
    dim = HALF // 2
    causal = iota((HALF, HALF), 0) >= iota((HALF, HALF), 1)
    for head in range(2):
        cols = slice(head * dim, (head + 1) * dim)
        q, k = q_ref[:, cols], k_ref[:, cols]
        cum_col = cum_ref[:, head : head + 1]
        cum_row = as_row(cum_col)
        (qh, ql), (kh, kl) = split(q), split(k)
        sh, sl = split(sol_ref[head])
        grown = jnp.exp(cum_col) * q
        for i in range(2):
            ri = slice(i * HALF, (i + 1) * HALF)
            total = None
            for j in range(i + 1):
                rj = slice(j * HALF, (j + 1) * HALF)
                attend = mm3((qh[ri], ql[ri]), (kh[rj], kl[rj]), ((1,), (1,)))
                attend = attend * jnp.exp(jnp.minimum(cum_col[ri] - cum_row[:, rj], 0.0))
                if i == j:
                    attend = jnp.where(causal, attend, 0.0)
                term = mm3(split(attend), (sh[rj], sl[rj]))
                total = term if total is None else total + term
            both_ref[head, ri] = jnp.concatenate([grown[ri] - total[:, :dim], total[:, dim:]], axis=1)


def compose(late, early):
    dim = late.shape[0]
    both = mm3(split(late[:, :dim]), split(early))
    return jnp.concatenate([both[:, :dim], both[:, dim:] + late[:, dim:]], axis=1)


def pair_kernel(core_ref, own_ref, got_ref, msg_ref, first_ref):
    dim = HALF // 2
    lead = core_ref[0] == 0
    own, got = own_ref[...], got_ref[...]
    early, late = jnp.where(lead, own, got), jnp.where(lead, got, own)
    first_ref[...] = early
    eye = jnp.where(iota((dim, HALF), 0) == iota((dim, HALF), 1), 1.0, 0.0)
    message = (compose(late, early) - eye).astype(bf16)
    for chip in range(GROUP):
        msg_ref[chip] = message


def group_kernel(place_ref, got_ref, token_ref, before_ref, total_ref):
    del token_ref
    dim = HALF // 2
    eye = jnp.where(iota((dim, HALF), 0) == iota((dim, HALF), 1), 1.0, 0.0)
    place = place_ref[0]
    running = eye
    before = eye
    for chip in range(GROUP):
        item = got_ref[chip].astype(f32) + eye
        running = item if chip == 0 else compose(item, running)
        if chip + 1 < GROUP:
            before = jnp.where(place == chip + 1, running, before)
    before_ref[...] = before
    total_ref[...] = running


def hop_kernel(total_ref, state_ref, token_ref, out_ref):
    del token_ref
    dim = HALF // 2
    moved = mm3(split(total_ref[:, :dim]), split(state_ref[...].astype(f32)))
    out_ref[...] = (moved + total_ref[:, dim:]).astype(bf16)


def enter_kernel(core_ref, before_ref, first_ref, state_ref, pair_ref):
    dim = HALF // 2
    state = mm3(split(before_ref[:, :dim]), split(state_ref[...].astype(f32))) + before_ref[:, dim:]
    after = mm3(split(first_ref[:, :dim]), split(state)) + first_ref[:, dim:]
    lead = core_ref[0] == 0
    pair_ref[0] = jnp.where(lead, state, after)
    pair_ref[1] = jnp.where(lead, after, state)


def finish_kernel(
    core_ref,
    local_ref,
    own_ref,
    got_ref,
    x_ref,
    gain_ref,
    mask_ref,
    rank_ref,
    take_ref,
    left_far,
    right_far,
    hidden_ref,
    send_ref,
):
    del left_far, right_far
    dim = HALF // 2
    lead = core_ref[0] == 0
    keep, got = own_ref[0], got_ref[1]
    states = (jnp.where(lead, keep, got), jnp.where(lead, got, keep))
    parts = []
    for head in range(2):
        out = local_ref[head, :, dim:] + mm3(split(local_ref[head, :, :dim]), split(states[head]))
        norm = out * lax.rsqrt(jnp.mean(out * out, -1, keepdims=True) + 1e-06)
        parts.append((norm * gain_ref[:, head * dim : (head + 1) * dim]).astype(bf16))
    normed = jnp.concatenate(parts, axis=1)
    hidden = (x_ref[...].astype(f32) + normed.astype(f32)).astype(bf16)
    hidden_ref[...] = hidden
    quarters, _, slots = take_ref.shape
    count = send_ref.shape[0] // quarters
    chosen = (iota((quarters * slots, hidden.shape[0]), 0) == rank_ref[...]) & (mask_ref[...] == 1)
    picked = mm(jnp.where(chosen, 1.0, 0.0).astype(bf16), hidden).astype(bf16)
    for quarter in range(quarters):
        rows = picked[quarter * slots : (quarter + 1) * slots]
        taken = mm(take_ref[quarter], rows).astype(bf16)
        send_ref[quarter * count : (quarter + 1) * count] = taken.reshape(count, *send_ref.shape[1:])


def rank_kernel(mask_ref, rank_ref):
    rows = mask_ref.shape[1]
    tri = jnp.where(iota((rows, rows), 0) <= iota((rows, rows), 1), 1.0, 0.0).astype(bf16)
    wide = jnp.broadcast_to(mask_ref[...].astype(f32), (16, rows)).astype(bf16)
    rank_ref[...] = mm(wide, tri)[:1].astype(jnp.int32) - 1


def route_kernel(mask_ref, choice_ref, take_ref, weigh_ref, token_ref):
    token_ref[...] = jnp.zeros_like(token_ref)
    quarters, total, slots = take_ref.shape
    top = choice_ref.shape[1] // 2
    count = jnp.sum(mask_ref[...])
    line = iota((total, slots), 0)
    expert = (line >> 1).astype(f32)
    earlier = jnp.where(iota((slots, slots), 0) < iota((slots, slots), 1), 1.0, 0.0).astype(bf16)
    for quarter in range(quarters):
        live = quarter * slots + iota((total, slots), 1) < count
        hit = jnp.zeros((total, slots), f32)
        weight = jnp.zeros((total, slots), f32)
        for pick in range(top):
            same = (expert == choice_ref[quarter, pick : pick + 1, :slots]) & live
            hit = hit + jnp.where(same, 1.0, 0.0)
            weight = weight + jnp.where(same, choice_ref[quarter, top + pick : top + pick + 1, :slots], 0.0)
        arrival = mm(hit.astype(bf16), earlier).astype(jnp.int32)
        here = (hit > 0.0) & (arrival == (line & 1))
        take_ref[quarter] = jnp.where(here, 1.0, 0.0).astype(bf16)
        weigh_ref[quarter] = jnp.where(here, weight, 0.0)


def expert_part(coarse_ref, rows_ref, ext_ref, pieces, total, offset):
    width = rows_ref.shape[2]
    count = rows_ref.shape[0] // GROUP
    inner = total.shape[1]
    for ref, step, parts in pieces:
        c = lax.rem(coarse_ref[0] + step, GROUP)

        @pl.when(2 * c < GROUP)
        def _():
            for n, part in enumerate(parts):
                rows = rows_ref[pl.ds((2 * c + part) * count, count)].reshape(total.shape[0], width)
                total[...] += mm(rows, ref[n * width : (n + 1) * width, :inner])

        @pl.when(2 * c >= GROUP)
        def _():
            for n, part in enumerate(parts):
                ext = jnp.broadcast_to(ext_ref[2 * c + part - GROUP].astype(f32), (16, width)).astype(bf16)
                offset[...] += mm(ext, ref[n * width : (n + 1) * width, :inner])


def near_kernel(coarse_ref, rows_ref, ext_ref, own_ref, left_ref, right_ref, total_ref, offset_ref):
    total_ref[...] = jnp.zeros_like(total_ref)
    offset_ref[...] = jnp.zeros_like(offset_ref)
    pieces = ((own_ref, 0, (0, 1)), (left_ref, GROUP - 1, (0, 1)), (right_ref, 1, (0, 1)))
    expert_part(coarse_ref, rows_ref, ext_ref, pieces, total_ref, offset_ref)


def expert_kernel(
    coarse_ref,
    rows_ref,
    ext_ref,
    near_ref,
    near_offset_ref,
    own_ref,
    left_ref,
    right_ref,
    upper_ref,
    lower_ref,
    out_ref,
    total,
    offset,
):
    width = rows_ref.shape[2]
    count = rows_ref.shape[0] // GROUP
    inner = total.shape[1]
    hidden = inner // 2
    total[...] = near_ref[...]
    offset[...] = near_offset_ref[...]
    pieces = ((upper_ref, 2, (0,)), (lower_ref, 2, (1,)))
    expert_part(coarse_ref, rows_ref, ext_ref, pieces, total, offset)
    gate = total[:, :hidden] + offset[:1, :hidden]
    up = total[:, hidden:] + offset[:1, hidden:]
    act = (gate / (1.0 + jnp.exp(-gate)) * up).astype(bf16)

    def put(step, value):
        c = lax.rem(coarse_ref[0] + step, GROUP)
        out_ref[pl.ds(c * count, count)] = value.astype(bf16).reshape(count, *out_ref.shape[1:])

    for ref, step in ((own_ref, 0), (left_ref, GROUP - 1), (right_ref, 1)):
        put(step, mm(act, ref[:, inner:]))
    put(2, mm(act[:, :width], upper_ref[:, inner:]) + mm(act[:, width:], lower_ref[:, inner:]))


def combine_kernel(mask_ref, weigh_ref, back_ref, out_ref, last_ref):
    quarters, _, slots = weigh_ref.shape
    count, width = back_ref.shape[0] // quarters, back_ref.shape[2]
    bounds = jnp.sum(mask_ref[...])
    last = jnp.zeros(last_ref.shape, f32)
    for c in range(quarters):
        wh, wl = split(weigh_ref[c])
        back = back_ref[c * count : (c + 1) * count].reshape(weigh_ref.shape[1], width)
        part = mm(wh, back, ((0,), (0,))) + mm(wl, back, ((0,), (0,)))
        out_ref[c * slots : (c + 1) * slots] = part
        here = c * slots + iota((slots, 1), 0) == bounds - 1
        last = last + jnp.sum(jnp.where(here, part, 0.0), axis=0, keepdims=True)
    last_ref[...] = last


def spread_kernel(hidden_ref, rank_ref, stretch_ref, out_ref, before_ref):
    rows, slots = hidden_ref.shape[0], stretch_ref.shape[0]
    rank = rank_ref[...]
    chosen = jnp.where(iota((slots, rows), 0) == rank, 1.0, 0.0).astype(bf16)
    sh, sl = split(stretch_ref[...])
    spread = mm(chosen, sh, ((0,), (0,))) + mm(chosen, sl, ((0,), (0,)))
    eye = iota((rows, rows), 0) == iota((rows, rows), 1)
    before = jnp.sum(jnp.where(eye & (rank < 0), 1.0, 0.0), axis=1, keepdims=True)
    before_ref[...] = jnp.broadcast_to(before, before_ref.shape)
    out_ref[...] = (hidden_ref[...].astype(f32) + spread).astype(bf16)


def entry_kernel(hidden_ref, mixed_ref, before_ref, prev_ref, out_ref):
    entry = (hidden_ref[...].astype(f32) + prev_ref[...]).astype(bf16)
    out_ref[...] = jnp.where(before_ref[:, :1] > 0.0, entry, mixed_ref[...])


def sds(shape, dtype):
    return jax.ShapeDtypeStruct(shape, dtype)


def call(kernel, outs, args, scalars=0, scratch=(), flops=10**5, megabytes=16, far_in=(), far_out=()):
    def spec(far, index):
        space = pltpu.SMEM if index < 0 else pltpu.HBM if index in far else pltpu.VMEM
        return pl.BlockSpec(memory_space=space)

    many = isinstance(outs, tuple)
    places = tuple(spec(far_out, i) for i in range(len(outs))) if many else spec((), 0)
    return pl.pallas_call(
        kernel,
        out_shape=outs,
        in_specs=[spec(far_in, i - scalars) for i in range(len(args))],
        out_specs=places,
        scratch_shapes=list(scratch),
        compiler_params=pltpu.CompilerParams(vmem_limit_bytes=megabytes * 2**20),
        cost_estimate=pl.CostEstimate(flops=flops, bytes_accessed=flops // 100, transcendentals=0),
    )(*args)


def shards(
    bytes_in,
    norm_gain,
    qkv_weight,
    gate_weight_enc,
    decay_rate,
    write_bias,
    head_gain,
    boundaries,
    picks,
    pick_gates,
    extension,
    expert_gate,
    expert_up,
    expert_down,
):
    x = bytes_in[0]
    rows, width = x.shape
    dim = HALF // 2
    seq = lax.axis_index("seq")
    spot = lax.axis_index("coarse").astype(jnp.int32)[None]
    seq_total = lax.axis_size("seq")
    core = (seq % 2).astype(jnp.int32)[None]
    place = ((seq // 2) % GROUP).astype(jnp.int32)[None]
    local_slots = picks.shape[1]
    slot_total = local_slots * GROUP
    pair_total = local_slots * picks.shape[2]
    everywhere = ("coarse", "seq", "exp")

    def exchange(array, axes, **kwargs):
        return lax.all_to_all(array, axes, split_axis=0, concat_axis=0, tiled=True, **kwargs)

    choice = jnp.concatenate([picks[0].T.astype(f32), pick_gates[0].T], axis=0)
    choice = jnp.pad(choice, ((0, 0), (0, dim - local_slots)))
    choice = exchange(jnp.broadcast_to(choice[None], (GROUP, *choice.shape)), "coarse")

    depth, hidden_units = expert_gate.shape[1:]
    columns = 2 * hidden_units + expert_down.shape[2]
    gate_rows = gate_weight_enc.transpose(0, 2, 1)
    own, give, q, k, solved, cum, x_share, weights = call(
        delta_kernel,
        (
            sds((dim, HALF), f32),
            sds((dim, HALF), f32),
            sds((rows, HALF), f32),
            sds((rows, HALF), f32),
            sds((2, rows, HALF), f32),
            sds((rows, 2), f32),
            sds((rows, HALF), bf16),
            sds((depth, columns), bf16),
        ),
        (
            jnp.concatenate([core, spot]),
            x,
            norm_gain[None],
            qkv_weight,
            gate_rows,
            decay_rate[None],
            write_bias[None],
            expert_gate,
            expert_up,
            expert_down,
        ),
        scalars=1,
        scratch=(
            pltpu.VMEM((rows, width), bf16),
            pltpu.VMEM((1, width), f32),
            pltpu.VMEM(qkv_weight.shape, bf16),
            pltpu.VMEM(gate_rows.shape, bf16),
            pltpu.VMEM((1, 2), f32),
            pltpu.VMEM((1, 2), f32),
            pltpu.VMEM((8, dim, HALF), bf16),
            pltpu.VMEM((8, dim, dim), f32),
            pltpu.SemaphoreType.DMA((10,)),
        ),
        flops=2 * 10**9,
        megabytes=60,
        far_in=range(9),
    )

    swap = [(i, i ^ 1) for i in range(seq_total)]
    got = lax.ppermute(give, "seq", swap)
    local, ready = call(local_kernel, (sds((2, rows, HALF), f32), sds((8, dim), f32)), (q, k, solved, cum))
    rank = call(rank_kernel, sds((1, rows), jnp.int32), (boundaries,))
    take, weigh, routed = call(
        route_kernel,
        (
            sds((GROUP, pair_total, local_slots), bf16),
            sds((GROUP, pair_total, local_slots), f32),
            sds((8, dim), f32),
        ),
        (boundaries, choice),
    )
    message, first = call(
        pair_kernel, (sds((GROUP, dim, HALF), bf16), sds((dim, HALF), f32)), (core, own, got), scalars=1
    )
    half = depth // 2
    ring = [(i, (i + 1) % GROUP) for i in range(GROUP)]
    back = [(b, a) for a, b in ring]
    left = lax.ppermute(weights, "coarse", ring)
    right = lax.ppermute(weights, "coarse", back)
    facing = (lax.ppermute(left[:half], "coarse", ring), lax.ppermute(right[half:], "coarse", back))
    stride = 2 * GROUP
    groups = [
        [stride * g + 2 * i + c for i in range(GROUP)] for g in range(seq_total // stride) for c in range(2)
    ]
    chips = exchange(message, "seq", axis_index_groups=groups)
    before, total = call(
        group_kernel, (sds((dim, HALF), f32), sds((dim, HALF), f32)), (place, chips, ready), scalars=1
    )
    state = jnp.zeros((dim, dim), bf16)
    for hop in range(seq_total // stride - 1):
        if hop == 0:
            outgoing = total[:, dim:].astype(bf16)
        else:
            token = choice if hop == 1 else routed
            outgoing = call(hop_kernel, sds((dim, dim), bf16), (total, state, token))
        pairs = [(stride * hop + i, stride * (hop + 1) + i) for i in range(stride)]
        state = state + lax.ppermute(outgoing, "seq", pairs)
    states = call(enter_kernel, sds((2, dim, dim), f32), (core, before, first, state), scalars=1)
    others = lax.ppermute(states, "seq", swap)

    devices = lax.axis_size(everywhere)
    capacity = GROUP * pair_total // devices
    hidden, outgoing = call(
        finish_kernel,
        (sds((rows, HALF), bf16), sds((devices, capacity, HALF), bf16)),
        (core, local, states, others, x_share, head_gain[None], boundaries, rank, take, left, right),
        scalars=1,
        far_in=(8, 9),
    )
    received = exchange(outgoing, everywhere)
    parts = (sds((pair_total, 2 * hidden_units), f32), sds((16, 2 * hidden_units), f32))
    extra_rows = extension.reshape(width // HALF, 1, HALF)
    near = call(near_kernel, parts, (spot, received, extra_rows, weights, left, right), scalars=1)
    value = call(
        expert_kernel,
        sds((devices, capacity, HALF), bf16),
        (spot, received, extra_rows, *near, weights, left, right, *facing),
        scalars=1,
        scratch=tuple(pltpu.VMEM(part.shape, part.dtype) for part in parts),
    )
    returned = exchange(value, everywhere)
    stretch, last = call(
        combine_kernel,
        (sds((slot_total, HALF), f32), sds((1, HALF), f32)),
        (boundaries, weigh, returned),
    )
    previous = lax.ppermute(last, "seq", [(i, i + 1) for i in range(seq_total - 1)])
    mixed, early = call(
        spread_kernel, (sds((rows, HALF), bf16), sds((rows, dim), f32)), (hidden, rank, stretch), flops=10**9
    )
    mixed = call(entry_kernel, sds((rows, HALF), bf16), (hidden, mixed, early, previous))
    return mixed[None]


def solution(mesh):
    placed = (
        P("exp", "seq", None),
        P(),
        P(None, None, "coarse"),
        P(None, None, "coarse"),
        P("coarse"),
        P("coarse"),
        P("coarse"),
        P("exp", "seq"),
        P("exp", ("seq", "coarse"), None),
        P("exp", ("seq", "coarse"), None),
        P(),
        P(("seq", "exp"), "coarse", None),
        P(("seq", "exp"), "coarse", None),
        P(("seq", "exp"), None, "coarse"),
    )
    return jax.shard_map(
        shards, mesh=mesh, in_specs=placed, out_specs=P("exp", "seq", "coarse"), check_vma=False
    )
```

```python
import jax
import jax.numpy as jnp
from jax import lax
from jax.experimental import pallas as pl
from jax.experimental.pallas import tpu as pltpu
from jax.sharding import PartitionSpec as P

f32 = jnp.float32
bf16 = jnp.bfloat16
HALF = 256
GROUP = 4


def mm(a, b, dims=((1,), (0,))):
    return lax.dot_general(a, b, (dims, ((), ())), preferred_element_type=f32)


def split(x):
    high = x.astype(bf16)
    return high, (x - high.astype(f32)).astype(bf16)


def mm3(a, b, dims=((1,), (0,))):
    (ah, al), (bh, bl) = a, b
    return mm(ah, bh, dims) + (mm(ah, bl, dims) + mm(al, bh, dims))


def iota(shape, dim):
    return lax.broadcasted_iota(jnp.int32, shape, dim)


def as_row(column):
    size = column.shape[0]
    eye = iota((size, size), 0) == iota((size, size), 1)
    return jnp.sum(jnp.where(eye, column, 0.0), axis=0, keepdims=True)


def delta_kernel(
    x_far,
    gain_far,
    w_far,
    gw_far,
    rate_far,
    bias_far,
    egate_far,
    eup_far,
    edown_far,
    own_ref,
    give_ref,
    local_ref,
    share_ref,
    weights_ref,
    x_ref,
    gain_ref,
    w_ref,
    gw_ref,
    rate_ref,
    bias_ref,
    low,
    inv,
    sems,
):
    rows = x_ref.shape[0]
    dim = HALF // 2
    pairs = [(x_far, x_ref), (gain_far, gain_ref), (gw_far, gw_ref), (rate_far, rate_ref), (bias_far, bias_ref)]
    pairs.append((w_far, w_ref))
    start = 0
    for far in (egate_far, eup_far, edown_far):
        size = far.shape[2]
        pairs.append((far.at[0], weights_ref.at[:, pl.ds(start, size)]))
        start += size
    moves = [pltpu.make_async_copy(a, b, sems.at[n]) for n, (a, b) in enumerate(pairs)]
    for move in moves:
        move.start()
    for move in moves[:5]:
        move.wait()
    first = pl.multiple_of(lax.axis_index("coarse") * HALF, HALF)
    moves.append(pltpu.make_async_copy(x_ref.at[:, pl.ds(first, HALF)], share_ref, sems.at[9]))
    moves[9].start()

    x = x_ref[...].astype(f32)
    normed = (x * lax.rsqrt(jnp.mean(x * x, -1, keepdims=True) + 1e-05) * gain_ref[...]).astype(bf16)
    linear = mm(normed, jnp.concatenate([gw_ref[0], gw_ref[1]], axis=0), ((1,), (1,)))
    decay_in, write_in = linear[:, :2], linear[:, 2:]
    write = jax.nn.sigmoid(write_in + bias_ref[...])
    soft = jnp.maximum(decay_in, 0.0) + jnp.log1p(jnp.exp(-jnp.abs(decay_in)))
    log_decay = -rate_ref[...] * soft
    tri = jnp.where(iota((rows, rows), 0) >= iota((rows, rows), 1), 1.0, 0.0).astype(bf16)
    part_h = log_decay.astype(bf16)
    rest = log_decay - part_h.astype(f32)
    part_m = rest.astype(bf16)
    part_l = (rest - part_m.astype(f32)).astype(bf16)
    sums = mm(tri, jnp.concatenate([part_h, part_m, part_l], axis=1))
    cum = sums[:, 0:2] + (sums[:, 2:4] + sums[:, 4:6])

    moves[5].wait()

    def act(index):
        value = mm(normed, w_ref[index])
        return value / (1.0 + jnp.exp(-value))

    q_all, k_all, v_all = act(0), act(1), act(2)
    strict = iota((HALF, HALF), 0) > iota((HALF, HALF), 1)
    causal = iota((HALF, HALF), 0) >= iota((HALF, HALF), 1)
    pair = (iota((dim, dim), 0) >> 1) == (iota((dim, dim), 1) >> 1)
    eye = jnp.where(iota((dim, dim), 0) == iota((dim, dim), 1), 1.0, 0.0)
    keep = []
    for head in range(2):
        cols = slice(head * dim, (head + 1) * dim)
        q, k, v = q_all[:, cols], k_all[:, cols], v_all[:, cols]
        q = q * lax.rsqrt(jnp.sum(q * q, -1, keepdims=True) + 1e-06)
        k = k * lax.rsqrt(jnp.sum(k * k, -1, keepdims=True) + 1e-06)
        cum_col = cum[:, head : head + 1]
        cum_row = as_row(cum_col)
        beta = write[:, head : head + 1]
        kh, kl = split(k)
        deep = jnp.concatenate([kh, kl], axis=1)
        twice = jnp.concatenate([kh, kh], axis=1)
        cross = None
        inner = []
        for i, j in ((0, 0), (1, 1), (1, 0)):
            ri, rj = slice(i * HALF, (i + 1) * HALF), slice(j * HALF, (j + 1) * HALF)
            gram = mm(deep[ri], twice[rj], ((1,), (1,))) + mm(kh[ri], kl[rj], ((1,), (1,)))
            lower = beta[ri] * jnp.exp(jnp.minimum(cum_col[ri] - cum_row[:, rj], 0.0)) * gram
            if i == j:
                lower = jnp.where(strict, lower, 0.0)
                for sub in range(2):
                    rs = slice(sub * dim, (sub + 1) * dim)
                    block = 4 * head + 2 * i + sub
                    part = lower[rs, rs]
                    low[block] = jnp.concatenate(split(part), axis=1)
                    inv[block] = eye - jnp.where(pair, part, 0.0)
                inner.append(jnp.concatenate(split(lower[dim:, :dim]), axis=1))
            else:
                cross = split(lower)
        right = jnp.concatenate([(beta * jnp.exp(cum_col)) * k, beta * v], axis=1)
        last = cum_col[rows - 1 : rows]
        (qh, ql) = split(q)
        broad = jnp.concatenate([qh, ql], axis=1)
        attend = {}
        for i, j in ((0, 0), (1, 1), (1, 0)):
            ri, rj = slice(i * HALF, (i + 1) * HALF), slice(j * HALF, (j + 1) * HALF)
            gram = mm(broad[ri], twice[rj], ((1,), (1,))) + mm(qh[ri], kl[rj], ((1,), (1,)))
            gram = gram * jnp.exp(jnp.minimum(cum_col[ri] - cum_row[:, rj], 0.0))
            attend[i, j] = split(jnp.where(causal, gram, 0.0) if i == j else gram)
        grown = jnp.exp(cum_col) * q
        keep.append((cross, inner, right, k * jnp.exp(last - cum_col), jnp.exp(last), attend, grown))

    def packed(left, block):
        wide = jnp.concatenate(split(block), axis=1)
        out = mm(left, jnp.concatenate([wide, wide], axis=0))
        return out[:, :dim] + out[:, dim:]

    def level(step, carry):
        r, c = iota((dim, HALF), 0), iota((dim, HALF), 1) & (dim - 1)
        above = ((r >> (step + 1)) == (c >> (step + 1))) & ((r >> step) > (c >> step))
        zero = jnp.zeros((dim, HALF), bf16)
        blocks = [inv[m] for m in range(8)]
        inside = [packed(jnp.where(above, low[m], zero), blocks[m]) for m in range(8)]
        for m in range(8):
            inv[m] = blocks[m] - packed(jnp.concatenate(split(blocks[m]), axis=1), inside[m])
        return carry

    lax.fori_loop(1, 7, level, 0)
    for head in range(2):
        cross, inner, right, k_end, scale, attend, grown = keep[head]
        full = []
        for i in range(2):
            top, bottom = inv[4 * head + 2 * i], inv[4 * head + 2 * i + 1]
            corner = packed(jnp.concatenate(split(bottom), axis=1), packed(inner[i], top))
            upper = jnp.concatenate([top, jnp.zeros_like(top)], axis=1)
            full.append(split(jnp.concatenate([upper, jnp.concatenate([-corner, bottom], axis=1)], axis=0)))
        first = mm3(full[0], split(right[:HALF]))
        second = right[HALF:] - mm3(cross, split(first))
        second = mm3(full[1], split(second))
        solved = jnp.concatenate([first, second], axis=0)
        halves = (split(first), split(second))
        for i in range(2):
            ri = slice(i * HALF, (i + 1) * HALF)
            out = mm3(attend[i, i], halves[i])
            if i > 0:
                out = out + mm3(attend[1, 0], halves[0])
            local_ref[head, ri] = jnp.concatenate([grown[ri] - out[:, :dim], out[:, dim:]], axis=1)
        ends = mm3(split(k_end), split(solved), ((0,), (0,)))
        keep[head] = jnp.concatenate([scale * eye - ends[:, :dim], ends[:, dim:]], axis=1)
    lead = lax.rem(lax.axis_index("seq"), 2) == 0
    own_ref[...] = jnp.where(lead, keep[0], keep[1])
    give_ref[...] = jnp.where(lead, keep[1], keep[0])
    for move in moves[6:]:
        move.wait()


def compose(late, early):
    dim = late.shape[0]
    both = mm3(split(late[:, :dim]), split(early))
    return jnp.concatenate([both[:, :dim], both[:, dim:] + late[:, dim:]], axis=1)


def pair_kernel(core_ref, own_ref, got_ref, msg_ref, first_ref):
    dim = HALF // 2
    lead = core_ref[0] == 0
    own, got = own_ref[...], got_ref[...]
    early, late = jnp.where(lead, own, got), jnp.where(lead, got, own)
    first_ref[...] = early
    eye = jnp.where(iota((dim, HALF), 0) == iota((dim, HALF), 1), 1.0, 0.0)
    message = (compose(late, early) - eye).astype(bf16)
    for chip in range(GROUP):
        msg_ref[chip] = message


def group_kernel(place_ref, got_ref, token_ref, before_ref, total_ref):
    del token_ref
    dim = HALF // 2
    eye = jnp.where(iota((dim, HALF), 0) == iota((dim, HALF), 1), 1.0, 0.0)
    place = place_ref[0]
    running = eye
    before = eye
    for chip in range(GROUP):
        item = got_ref[chip].astype(f32) + eye
        running = item if chip == 0 else compose(item, running)
        if chip + 1 < GROUP:
            before = jnp.where(place == chip + 1, running, before)
    before_ref[...] = before
    total_ref[...] = running


def hop_kernel(total_ref, state_ref, token_ref, out_ref):
    del token_ref
    dim = HALF // 2
    moved = mm3(split(total_ref[:, :dim]), split(state_ref[...].astype(f32)))
    out_ref[...] = (moved + total_ref[:, dim:]).astype(bf16)


def enter_kernel(core_ref, before_ref, first_ref, state_ref, pair_ref):
    dim = HALF // 2
    state = mm3(split(before_ref[:, :dim]), split(state_ref[...].astype(f32))) + before_ref[:, dim:]
    after = mm3(split(first_ref[:, :dim]), split(state)) + first_ref[:, dim:]
    lead = core_ref[0] == 0
    pair_ref[0] = jnp.where(lead, state, after)
    pair_ref[1] = jnp.where(lead, after, state)


def finish_kernel(
    core_ref,
    local_ref,
    own_ref,
    got_ref,
    x_ref,
    gain_ref,
    mask_ref,
    rank_ref,
    take_ref,
    left_far,
    right_far,
    hidden_ref,
    send_ref,
):
    del left_far, right_far
    dim = HALF // 2
    lead = core_ref[0] == 0
    keep, got = own_ref[0], got_ref[1]
    states = (jnp.where(lead, keep, got), jnp.where(lead, got, keep))
    parts = []
    for head in range(2):
        out = local_ref[head, :, dim:] + mm3(split(local_ref[head, :, :dim]), split(states[head]))
        norm = out * lax.rsqrt(jnp.mean(out * out, -1, keepdims=True) + 1e-06)
        parts.append((norm * gain_ref[:, head * dim : (head + 1) * dim]).astype(bf16))
    normed = jnp.concatenate(parts, axis=1)
    hidden = (x_ref[...].astype(f32) + normed.astype(f32)).astype(bf16)
    hidden_ref[...] = hidden
    quarters, _, slots = take_ref.shape
    count = send_ref.shape[0] // quarters
    chosen = (iota((quarters * slots, hidden.shape[0]), 0) == rank_ref[...]) & (mask_ref[...] == 1)
    picked = mm(jnp.where(chosen, 1.0, 0.0).astype(bf16), hidden).astype(bf16)
    for quarter in range(quarters):
        rows = picked[quarter * slots : (quarter + 1) * slots]
        taken = mm(take_ref[quarter], rows).astype(bf16)
        send_ref[quarter * count : (quarter + 1) * count] = taken.reshape(count, *send_ref.shape[1:])


def rank_kernel(mask_ref, rank_ref):
    rows = mask_ref.shape[1]
    tri = jnp.where(iota((rows, rows), 0) <= iota((rows, rows), 1), 1.0, 0.0).astype(bf16)
    wide = jnp.broadcast_to(mask_ref[...].astype(f32), (16, rows)).astype(bf16)
    rank_ref[...] = mm(wide, tri)[:1].astype(jnp.int32) - 1


def route_kernel(coarse_ref, mask_ref, near_ref, far_ref, take_ref, weigh_ref, token_ref, choice_ref):
    here = coarse_ref[0]
    beside, facing = here + 1 - 2 * lax.rem(here, 2), GROUP - 1 - here
    choice_ref[here] = near_ref[0]
    choice_ref[beside] = near_ref[1]
    choice_ref[facing] = far_ref[0]
    choice_ref[GROUP - 1 - beside] = far_ref[1]
    token_ref[...] = jnp.zeros_like(token_ref)
    quarters, total, slots = take_ref.shape
    top = choice_ref.shape[1] // 2
    count = jnp.sum(mask_ref[...])
    line = iota((total, slots), 0)
    expert = (line >> 1).astype(f32)
    earlier = jnp.where(iota((slots, slots), 0) < iota((slots, slots), 1), 1.0, 0.0).astype(bf16)
    for quarter in range(quarters):
        live = quarter * slots + iota((total, slots), 1) < count
        hit = jnp.zeros((total, slots), f32)
        weight = jnp.zeros((total, slots), f32)
        for pick in range(top):
            same = (expert == choice_ref[quarter, pick : pick + 1, :slots]) & live
            hit = hit + jnp.where(same, 1.0, 0.0)
            weight = weight + jnp.where(same, choice_ref[quarter, top + pick : top + pick + 1, :slots], 0.0)
        arrival = mm(hit.astype(bf16), earlier).astype(jnp.int32)
        found = (hit > 0.0) & (arrival == (line & 1))
        take_ref[quarter] = jnp.where(found, 1.0, 0.0).astype(bf16)
        weigh_ref[quarter] = jnp.where(found, weight, 0.0)


def expert_part(coarse_ref, rows_ref, ext_ref, pieces, total, offset):
    width = rows_ref.shape[2]
    count = rows_ref.shape[0] // GROUP
    inner = total.shape[1]
    for ref, step, parts in pieces:
        c = lax.rem(coarse_ref[0] + step, GROUP)

        @pl.when(2 * c < GROUP)
        def _():
            for n, part in enumerate(parts):
                rows = rows_ref[pl.ds((2 * c + part) * count, count)].reshape(total.shape[0], width)
                total[...] += mm(rows, ref[n * width : (n + 1) * width, :inner])

        @pl.when(2 * c >= GROUP)
        def _():
            for n, part in enumerate(parts):
                ext = jnp.broadcast_to(ext_ref[2 * c + part - GROUP].astype(f32), (16, width)).astype(bf16)
                offset[...] += mm(ext, ref[n * width : (n + 1) * width, :inner])


def stage_kernel(weights_ref, hidden_far, out_ref):
    del hidden_far
    out_ref[...] = weights_ref[...]


def near_kernel(coarse_ref, rows_ref, ext_ref, own_ref, left_ref, right_ref, total_ref, offset_ref):
    total_ref[...] = jnp.zeros_like(total_ref)
    offset_ref[...] = jnp.zeros_like(offset_ref)
    pieces = ((own_ref, 0, (0, 1)), (left_ref, GROUP - 1, (0, 1)), (right_ref, 1, (0, 1)))
    expert_part(coarse_ref, rows_ref, ext_ref, pieces, total_ref, offset_ref)


def expert_kernel(
    coarse_ref,
    rows_ref,
    ext_ref,
    near_ref,
    near_offset_ref,
    own_ref,
    left_ref,
    right_ref,
    upper_ref,
    lower_ref,
    out_ref,
    total,
    offset,
):
    width = rows_ref.shape[2]
    count = rows_ref.shape[0] // GROUP
    inner = total.shape[1]
    hidden = inner // 2
    total[...] = near_ref[...]
    offset[...] = near_offset_ref[...]
    pieces = ((upper_ref, 2, (0,)), (lower_ref, 2, (1,)))
    expert_part(coarse_ref, rows_ref, ext_ref, pieces, total, offset)
    gate = total[:, :hidden] + offset[:1, :hidden]
    up = total[:, hidden:] + offset[:1, hidden:]
    act = (gate / (1.0 + jnp.exp(-gate)) * up).astype(bf16)

    def put(step, value):
        c = lax.rem(coarse_ref[0] + step, GROUP)
        out_ref[pl.ds(c * count, count)] = value.astype(bf16).reshape(count, *out_ref.shape[1:])

    for ref, step in ((own_ref, 0), (left_ref, GROUP - 1), (right_ref, 1)):
        put(step, mm(act, ref[:, inner:]))
    put(2, mm(act[:, :width], upper_ref[:, inner:]) + mm(act[:, width:], lower_ref[:, inner:]))


def combine_kernel(mask_ref, weigh_ref, back_ref, out_ref, last_ref):
    quarters, _, slots = weigh_ref.shape
    count, width = back_ref.shape[0] // quarters, back_ref.shape[2]
    bounds = jnp.sum(mask_ref[...])
    last = jnp.zeros(last_ref.shape, f32)
    for c in range(quarters):
        wh, wl = split(weigh_ref[c])
        back = back_ref[c * count : (c + 1) * count].reshape(weigh_ref.shape[1], width)
        part = mm(wh, back, ((0,), (0,))) + mm(wl, back, ((0,), (0,)))
        out_ref[c * slots : (c + 1) * slots] = part
        here = c * slots + iota((slots, 1), 0) == bounds - 1
        last = last + jnp.sum(jnp.where(here, part, 0.0), axis=0, keepdims=True)
    last_ref[...] = last


def spread_kernel(hidden_ref, rank_ref, stretch_ref, out_ref, before_ref):
    rows, slots = hidden_ref.shape[0], stretch_ref.shape[0]
    rank = rank_ref[...]
    chosen = jnp.where(iota((slots, rows), 0) == rank, 1.0, 0.0).astype(bf16)
    sh, sl = split(stretch_ref[...])
    spread = mm(chosen, sh, ((0,), (0,))) + mm(chosen, sl, ((0,), (0,)))
    eye = iota((rows, rows), 0) == iota((rows, rows), 1)
    before = jnp.sum(jnp.where(eye & (rank < 0), 1.0, 0.0), axis=1, keepdims=True)
    before_ref[...] = jnp.broadcast_to(before, before_ref.shape)
    out_ref[...] = (hidden_ref[...].astype(f32) + spread).astype(bf16)


def entry_kernel(hidden_ref, mixed_ref, before_ref, prev_ref, out_ref):
    entry = (hidden_ref[...].astype(f32) + prev_ref[...]).astype(bf16)
    out_ref[...] = jnp.where(before_ref[:, :1] > 0.0, entry, mixed_ref[...])


def sds(shape, dtype):
    return jax.ShapeDtypeStruct(shape, dtype)


def call(kernel, outs, args, scalars=0, scratch=(), flops=10**5, megabytes=16, far_in=(), far_out=()):
    def spec(far, index):
        space = pltpu.SMEM if index < 0 else pltpu.HBM if index in far else pltpu.VMEM
        return pl.BlockSpec(memory_space=space)

    many = isinstance(outs, tuple)
    places = tuple(spec(far_out, i) for i in range(len(outs))) if many else spec((), 0)
    return pl.pallas_call(
        kernel,
        out_shape=outs,
        in_specs=[spec(far_in, i - scalars) for i in range(len(args))],
        out_specs=places,
        scratch_shapes=list(scratch),
        compiler_params=pltpu.CompilerParams(vmem_limit_bytes=megabytes * 2**20),
        cost_estimate=pl.CostEstimate(flops=flops, bytes_accessed=flops // 100, transcendentals=0),
    )(*args)


def shards(
    bytes_in,
    norm_gain,
    qkv_weight,
    gate_weight_enc,
    decay_rate,
    write_bias,
    head_gain,
    boundaries,
    picks,
    pick_gates,
    extension,
    expert_gate,
    expert_up,
    expert_down,
):
    x = bytes_in[0]
    rows, width = x.shape
    dim = HALF // 2
    seq = lax.axis_index("seq")
    spot = lax.axis_index("coarse").astype(jnp.int32)[None]
    seq_total = lax.axis_size("seq")
    core = (seq % 2).astype(jnp.int32)[None]
    place = ((seq // 2) % GROUP).astype(jnp.int32)[None]
    local_slots = picks.shape[1]
    slot_total = local_slots * GROUP
    pair_total = local_slots * picks.shape[2]
    everywhere = ("coarse", "seq", "exp")

    def exchange(array, axes, **kwargs):
        return lax.all_to_all(array, axes, split_axis=0, concat_axis=0, tiled=True, **kwargs)

    choice = jnp.concatenate([picks[0].T.astype(f32), pick_gates[0].T], axis=0)
    choice = jnp.pad(choice, ((0, 0), (0, dim - local_slots)))
    choice = choice[None]
    paired = lax.ppermute(choice, "coarse", [(i, i ^ 1) for i in range(GROUP)])
    choice = jnp.concatenate([choice, paired])
    facing_choice = lax.ppermute(choice, "coarse", [(i, GROUP - 1 - i) for i in range(GROUP)])

    depth, hidden_units = expert_gate.shape[1:]
    columns = 2 * hidden_units + expert_down.shape[2]
    gate_rows = gate_weight_enc.transpose(0, 2, 1)
    own, give, local, x_share, weights = call(
        delta_kernel,
        (
            sds((dim, HALF), f32),
            sds((dim, HALF), f32),
            sds((2, rows, HALF), f32),
            sds((rows, HALF), bf16),
            sds((depth, columns), bf16),
        ),
        (
            x,
            norm_gain[None],
            qkv_weight,
            gate_rows,
            decay_rate[None],
            write_bias[None],
            expert_gate,
            expert_up,
            expert_down,
        ),
        scratch=(
            pltpu.VMEM((rows, width), bf16),
            pltpu.VMEM((1, width), f32),
            pltpu.VMEM(qkv_weight.shape, bf16),
            pltpu.VMEM(gate_rows.shape, bf16),
            pltpu.VMEM((1, 2), f32),
            pltpu.VMEM((1, 2), f32),
            pltpu.VMEM((8, dim, HALF), bf16),
            pltpu.VMEM((8, dim, dim), f32),
            pltpu.SemaphoreType.DMA((10,)),
        ),
        flops=2 * 10**9,
        megabytes=60,
        far_in=range(9),
    )

    swap = [(i, i ^ 1) for i in range(seq_total)]
    got = lax.ppermute(give, "seq", swap)
    rank = call(rank_kernel, sds((1, rows), jnp.int32), (boundaries,))
    take, weigh, routed = call(
        route_kernel,
        (
            sds((GROUP, pair_total, local_slots), bf16),
            sds((GROUP, pair_total, local_slots), f32),
            sds((8, dim), f32),
        ),
        (spot, boundaries, choice, facing_choice),
        scalars=1,
        scratch=(pltpu.VMEM((GROUP, 2 * picks.shape[2], dim), f32),),
    )
    message, first = call(
        pair_kernel, (sds((GROUP, dim, HALF), bf16), sds((dim, HALF), f32)), (core, own, got), scalars=1
    )
    half = depth // 2
    ring = [(i, (i + 1) % GROUP) for i in range(GROUP)]
    back = [(b, a) for a, b in ring]
    left = lax.ppermute(weights, "coarse", ring)
    right = lax.ppermute(weights, "coarse", back)
    facing = (lax.ppermute(left[:half], "coarse", ring), lax.ppermute(right[half:], "coarse", back))
    stride = 2 * GROUP
    groups = [
        [stride * g + 2 * i + c for i in range(GROUP)] for g in range(seq_total // stride) for c in range(2)
    ]
    chips = exchange(message, "seq", axis_index_groups=groups)
    before, total = call(
        group_kernel, (sds((dim, HALF), f32), sds((dim, HALF), f32)), (place, chips, facing_choice), scalars=1
    )
    state = jnp.zeros((dim, dim), bf16)
    for hop in range(seq_total // stride - 1):
        if hop == 0:
            outgoing = total[:, dim:].astype(bf16)
        else:
            outgoing = call(hop_kernel, sds((dim, dim), bf16), (total, state, routed))
        pairs = [(stride * hop + i, stride * (hop + 1) + i) for i in range(stride)]
        state = state + lax.ppermute(outgoing, "seq", pairs)
    states = call(enter_kernel, sds((2, dim, dim), f32), (core, before, first, state), scalars=1)
    others = lax.ppermute(states, "seq", swap)

    devices = lax.axis_size(everywhere)
    capacity = GROUP * pair_total // devices
    hidden, outgoing = call(
        finish_kernel,
        (sds((rows, HALF), bf16), sds((devices, capacity, HALF), bf16)),
        (core, local, states, others, x_share, head_gain[None], boundaries, rank, take, left, right),
        scalars=1,
        far_in=(8, 9),
    )
    received = exchange(outgoing, everywhere)
    parts = (sds((pair_total, 2 * hidden_units), f32), sds((16, 2 * hidden_units), f32))
    extra_rows = extension.reshape(width // HALF, 1, HALF)
    staged = call(stage_kernel, sds(weights.shape, bf16), (weights, hidden), far_in=(1,))
    near = call(near_kernel, parts, (spot, received, extra_rows, staged, left, right), scalars=1)
    value = call(
        expert_kernel,
        sds((devices, capacity, HALF), bf16),
        (spot, received, extra_rows, *near, staged, left, right, *facing),
        scalars=1,
        scratch=tuple(pltpu.VMEM(part.shape, part.dtype) for part in parts),
    )
    returned = exchange(value, everywhere)
    stretch, last = call(
        combine_kernel,
        (sds((slot_total, HALF), f32), sds((1, HALF), f32)),
        (boundaries, weigh, returned),
    )
    previous = lax.ppermute(last, "seq", [(i, i + 1) for i in range(seq_total - 1)])
    mixed, early = call(
        spread_kernel, (sds((rows, HALF), bf16), sds((rows, dim), f32)), (hidden, rank, stretch), flops=10**9
    )
    mixed = call(entry_kernel, sds((rows, HALF), bf16), (hidden, mixed, early, previous))
    return mixed[None]


def solution(mesh):
    placed = (
        P("exp", "seq", None),
        P(),
        P(None, None, "coarse"),
        P(None, None, "coarse"),
        P("coarse"),
        P("coarse"),
        P("coarse"),
        P("exp", "seq"),
        P("exp", ("seq", "coarse"), None),
        P("exp", ("seq", "coarse"), None),
        P(),
        P(("seq", "exp"), "coarse", None),
        P(("seq", "exp"), "coarse", None),
        P(("seq", "exp"), None, "coarse"),
    )
    return jax.shard_map(
        shards, mesh=mesh, in_specs=placed, out_specs=P("exp", "seq", "coarse"), check_vma=False
    )
```

```python
import jax
import jax.numpy as jnp
from jax import lax
from jax.experimental import pallas as pl
from jax.experimental.pallas import tpu as pltpu
from jax.sharding import PartitionSpec as P

f32 = jnp.float32
bf16 = jnp.bfloat16
HALF = 256
GROUP = 4


def mm(a, b, dims=((1,), (0,))):
    return lax.dot_general(a, b, (dims, ((), ())), preferred_element_type=f32)


def split(x):
    high = x.astype(bf16)
    return high, (x - high.astype(f32)).astype(bf16)


def mm3(a, b, dims=((1,), (0,))):
    (ah, al), (bh, bl) = a, b
    return mm(ah, bh, dims) + (mm(ah, bl, dims) + mm(al, bh, dims))


def iota(shape, dim):
    return lax.broadcasted_iota(jnp.int32, shape, dim)


def as_row(column):
    size = column.shape[0]
    eye = iota((size, size), 0) == iota((size, size), 1)
    return jnp.sum(jnp.where(eye, column, 0.0), axis=0, keepdims=True)


def choice_kernel(picks_ref, gates_ref, out_ref):
    top, slots = picks_ref.shape
    out_ref[...] = jnp.zeros_like(out_ref)
    for quarter in range(out_ref.shape[0]):
        out_ref[quarter, :top, :slots] = picks_ref[...].astype(f32)
        out_ref[quarter, top:, :slots] = gates_ref[...]


def after_kernel(choice_far, give_far, same_far):
    del choice_far, give_far, same_far


def delta_kernel(
    x_far,
    gain_far,
    w_far,
    gw_far,
    rate_far,
    bias_far,
    egate_far,
    eup_far,
    edown_far,
    own_ref,
    give_ref,
    local_ref,
    share_ref,
    weights_far,
    weights_ref,
    x_ref,
    gain_ref,
    w_ref,
    gw_ref,
    rate_ref,
    bias_ref,
    low,
    inv,
    sems,
):
    rows = x_ref.shape[0]
    dim = HALF // 2
    pairs = [(x_far, x_ref), (gain_far, gain_ref), (gw_far, gw_ref), (rate_far, rate_ref), (bias_far, bias_ref)]
    pairs.append((w_far, w_ref))
    start = 0
    for far in (egate_far, eup_far, edown_far):
        size = far.shape[2]
        pairs.append((far.at[0], weights_ref.at[:, pl.ds(start, size)]))
        start += size
    moves = [pltpu.make_async_copy(a, b, sems.at[n]) for n, (a, b) in enumerate(pairs)]
    for move in moves:
        move.start()
    for move in moves[:5]:
        move.wait()
    first = pl.multiple_of(lax.axis_index("coarse") * HALF, HALF)
    moves.append(pltpu.make_async_copy(x_ref.at[:, pl.ds(first, HALF)], share_ref, sems.at[9]))
    moves[9].start()

    x = x_ref[...].astype(f32)
    normed = (x * lax.rsqrt(jnp.mean(x * x, -1, keepdims=True) + 1e-05) * gain_ref[...]).astype(bf16)
    linear = mm(normed, jnp.concatenate([gw_ref[0], gw_ref[1]], axis=0), ((1,), (1,)))
    decay_in, write_in = linear[:, :2], linear[:, 2:]
    write = jax.nn.sigmoid(write_in + bias_ref[...])
    soft = jnp.maximum(decay_in, 0.0) + jnp.log1p(jnp.exp(-jnp.abs(decay_in)))
    log_decay = -rate_ref[...] * soft
    tri = jnp.where(iota((rows, rows), 0) >= iota((rows, rows), 1), 1.0, 0.0).astype(bf16)
    part_h = log_decay.astype(bf16)
    rest = log_decay - part_h.astype(f32)
    part_m = rest.astype(bf16)
    part_l = (rest - part_m.astype(f32)).astype(bf16)
    sums = mm(tri, jnp.concatenate([part_h, part_m, part_l], axis=1))
    cum = sums[:, 0:2] + (sums[:, 2:4] + sums[:, 4:6])

    moves[5].wait()

    def act(index):
        value = mm(normed, w_ref[index])
        return value / (1.0 + jnp.exp(-value))

    q_all, k_all, v_all = act(0), act(1), act(2)
    for move in moves[6:9]:
        move.wait()
    leave = pltpu.make_async_copy(weights_ref, weights_far, sems.at[10])
    leave.start()
    strict = iota((HALF, HALF), 0) > iota((HALF, HALF), 1)
    causal = iota((HALF, HALF), 0) >= iota((HALF, HALF), 1)
    pair = (iota((dim, dim), 0) >> 1) == (iota((dim, dim), 1) >> 1)
    eye = jnp.where(iota((dim, dim), 0) == iota((dim, dim), 1), 1.0, 0.0)
    keep = []
    for head in range(2):
        cols = slice(head * dim, (head + 1) * dim)
        q, k, v = q_all[:, cols], k_all[:, cols], v_all[:, cols]
        q = q * lax.rsqrt(jnp.sum(q * q, -1, keepdims=True) + 1e-06)
        k = k * lax.rsqrt(jnp.sum(k * k, -1, keepdims=True) + 1e-06)
        cum_col = cum[:, head : head + 1]
        cum_row = as_row(cum_col)
        beta = write[:, head : head + 1]
        kh, kl = split(k)
        deep = jnp.concatenate([kh, kl], axis=1)
        twice = jnp.concatenate([kh, kh], axis=1)
        cross = None
        inner = []
        for i, j in ((0, 0), (1, 1), (1, 0)):
            ri, rj = slice(i * HALF, (i + 1) * HALF), slice(j * HALF, (j + 1) * HALF)
            gram = mm(deep[ri], twice[rj], ((1,), (1,))) + mm(kh[ri], kl[rj], ((1,), (1,)))
            lower = beta[ri] * jnp.exp(jnp.minimum(cum_col[ri] - cum_row[:, rj], 0.0)) * gram
            if i == j:
                lower = jnp.where(strict, lower, 0.0)
                for sub in range(2):
                    rs = slice(sub * dim, (sub + 1) * dim)
                    block = 4 * head + 2 * i + sub
                    part = lower[rs, rs]
                    low[block] = jnp.concatenate(split(part), axis=1)
                    inv[block] = eye - jnp.where(pair, part, 0.0)
                inner.append(jnp.concatenate(split(lower[dim:, :dim]), axis=1))
            else:
                cross = split(lower)
        right = jnp.concatenate([(beta * jnp.exp(cum_col)) * k, beta * v], axis=1)
        last = cum_col[rows - 1 : rows]
        (qh, ql) = split(q)
        broad = jnp.concatenate([qh, ql], axis=1)
        attend = {}
        for i, j in ((0, 0), (1, 1), (1, 0)):
            ri, rj = slice(i * HALF, (i + 1) * HALF), slice(j * HALF, (j + 1) * HALF)
            gram = mm(broad[ri], twice[rj], ((1,), (1,))) + mm(qh[ri], kl[rj], ((1,), (1,)))
            gram = gram * jnp.exp(jnp.minimum(cum_col[ri] - cum_row[:, rj], 0.0))
            attend[i, j] = split(jnp.where(causal, gram, 0.0) if i == j else gram)
        grown = jnp.exp(cum_col) * q
        keep.append((cross, inner, right, k * jnp.exp(last - cum_col), jnp.exp(last), attend, grown))

    def packed(left, block):
        wide = jnp.concatenate(split(block), axis=1)
        out = mm(left, jnp.concatenate([wide, wide], axis=0))
        return out[:, :dim] + out[:, dim:]

    def level(step, carry):
        r, c = iota((dim, HALF), 0), iota((dim, HALF), 1) & (dim - 1)
        above = ((r >> (step + 1)) == (c >> (step + 1))) & ((r >> step) > (c >> step))
        zero = jnp.zeros((dim, HALF), bf16)
        blocks = [inv[m] for m in range(8)]
        inside = [packed(jnp.where(above, low[m], zero), blocks[m]) for m in range(8)]
        for m in range(8):
            inv[m] = blocks[m] - packed(jnp.concatenate(split(blocks[m]), axis=1), inside[m])
        return carry

    lax.fori_loop(1, 7, level, 0)
    for head in range(2):
        cross, inner, right, k_end, scale, attend, grown = keep[head]
        full = []
        for i in range(2):
            top, bottom = inv[4 * head + 2 * i], inv[4 * head + 2 * i + 1]
            corner = packed(jnp.concatenate(split(bottom), axis=1), packed(inner[i], top))
            upper = jnp.concatenate([top, jnp.zeros_like(top)], axis=1)
            full.append(split(jnp.concatenate([upper, jnp.concatenate([-corner, bottom], axis=1)], axis=0)))
        first = mm3(full[0], split(right[:HALF]))
        second = right[HALF:] - mm3(cross, split(first))
        second = mm3(full[1], split(second))
        solved = jnp.concatenate([first, second], axis=0)
        halves = (split(first), split(second))
        for i in range(2):
            ri = slice(i * HALF, (i + 1) * HALF)
            out = mm3(attend[i, i], halves[i])
            if i > 0:
                out = out + mm3(attend[1, 0], halves[0])
            local_ref[head, ri] = jnp.concatenate([grown[ri] - out[:, :dim], out[:, dim:]], axis=1)
        ends = mm3(split(k_end), split(solved), ((0,), (0,)))
        keep[head] = jnp.concatenate([scale * eye - ends[:, :dim], ends[:, dim:]], axis=1)
    lead = lax.rem(lax.axis_index("seq"), 2) == 0
    own_ref[...] = jnp.where(lead, keep[0], keep[1])
    give_ref[...] = jnp.where(lead, keep[1], keep[0])
    moves[9].wait()
    leave.wait()


def compose(late, early):
    dim = late.shape[0]
    both = mm3(split(late[:, :dim]), split(early))
    return jnp.concatenate([both[:, :dim], both[:, dim:] + late[:, dim:]], axis=1)


def pair_kernel(core_ref, own_ref, got_ref, msg_ref, first_ref):
    dim = HALF // 2
    lead = core_ref[0] == 0
    own, got = own_ref[...], got_ref[...]
    early, late = jnp.where(lead, own, got), jnp.where(lead, got, own)
    first_ref[...] = early
    eye = jnp.where(iota((dim, HALF), 0) == iota((dim, HALF), 1), 1.0, 0.0)
    message = (compose(late, early) - eye).astype(bf16)
    for chip in range(GROUP):
        msg_ref[chip] = message


def group_kernel(place_ref, got_ref, token_ref, before_ref, total_ref):
    del token_ref
    dim = HALF // 2
    eye = jnp.where(iota((dim, HALF), 0) == iota((dim, HALF), 1), 1.0, 0.0)
    place = place_ref[0]
    running = eye
    before = eye
    for chip in range(GROUP):
        item = got_ref[chip].astype(f32) + eye
        running = item if chip == 0 else compose(item, running)
        if chip + 1 < GROUP:
            before = jnp.where(place == chip + 1, running, before)
    before_ref[...] = before
    total_ref[...] = running


def hop_kernel(total_ref, state_ref, out_ref):
    dim = HALF // 2
    moved = mm3(split(total_ref[:, :dim]), split(state_ref[...].astype(f32)))
    out_ref[...] = (moved + total_ref[:, dim:]).astype(bf16)


def enter_kernel(core_ref, before_ref, first_ref, state_ref, pair_ref):
    dim = HALF // 2
    state = mm3(split(before_ref[:, :dim]), split(state_ref[...].astype(f32))) + before_ref[:, dim:]
    after = mm3(split(first_ref[:, :dim]), split(state)) + first_ref[:, dim:]
    lead = core_ref[0] == 0
    pair_ref[0] = jnp.where(lead, state, after)
    pair_ref[1] = jnp.where(lead, after, state)


def finish_kernel(
    core_ref,
    local_ref,
    own_ref,
    got_ref,
    x_ref,
    gain_ref,
    mask_ref,
    rank_ref,
    take_ref,
    left_far,
    right_far,
    hidden_ref,
    send_ref,
):
    del left_far, right_far
    dim = HALF // 2
    lead = core_ref[0] == 0
    keep, got = own_ref[0], got_ref[1]
    states = (jnp.where(lead, keep, got), jnp.where(lead, got, keep))
    parts = []
    for head in range(2):
        out = local_ref[head, :, dim:] + mm3(split(local_ref[head, :, :dim]), split(states[head]))
        norm = out * lax.rsqrt(jnp.mean(out * out, -1, keepdims=True) + 1e-06)
        parts.append((norm * gain_ref[:, head * dim : (head + 1) * dim]).astype(bf16))
    normed = jnp.concatenate(parts, axis=1)
    hidden = (x_ref[...].astype(f32) + normed.astype(f32)).astype(bf16)
    hidden_ref[...] = hidden
    quarters, _, slots = take_ref.shape
    count = send_ref.shape[0] // quarters
    chosen = (iota((quarters * slots, hidden.shape[0]), 0) == rank_ref[...]) & (mask_ref[...] == 1)
    picked = mm(jnp.where(chosen, 1.0, 0.0).astype(bf16), hidden).astype(bf16)
    for quarter in range(quarters):
        rows = picked[quarter * slots : (quarter + 1) * slots]
        taken = mm(take_ref[quarter], rows).astype(bf16)
        send_ref[quarter * count : (quarter + 1) * count] = taken.reshape(count, *send_ref.shape[1:])


def rank_kernel(mask_ref, rank_ref):
    rows = mask_ref.shape[1]
    tri = jnp.where(iota((rows, rows), 0) <= iota((rows, rows), 1), 1.0, 0.0).astype(bf16)
    wide = jnp.broadcast_to(mask_ref[...].astype(f32), (16, rows)).astype(bf16)
    rank_ref[...] = mm(wide, tri)[:1].astype(jnp.int32) - 1


def route_kernel(mask_ref, choice_ref, take_ref, weigh_ref, token_ref):
    quarters, total, slots = take_ref.shape
    top = choice_ref.shape[1] // 2
    count = jnp.sum(mask_ref[...])
    line = iota((total, slots), 0)
    expert = (line >> 1).astype(f32)
    earlier = jnp.where(iota((slots, slots), 0) < iota((slots, slots), 1), 1.0, 0.0).astype(bf16)
    for quarter in range(quarters):
        live = quarter * slots + iota((total, slots), 1) < count
        hit = jnp.zeros((total, slots), f32)
        weight = jnp.zeros((total, slots), f32)
        for pick in range(top):
            same = (expert == choice_ref[quarter, pick : pick + 1, :slots]) & live
            hit = hit + jnp.where(same, 1.0, 0.0)
            weight = weight + jnp.where(same, choice_ref[quarter, top + pick : top + pick + 1, :slots], 0.0)
        arrival = mm(hit.astype(bf16), earlier).astype(jnp.int32)
        found = (hit > 0.0) & (arrival == (line & 1))
        take_ref[quarter] = jnp.where(found, 1.0, 0.0).astype(bf16)
        weigh_ref[quarter] = jnp.where(found, weight, 0.0)


def expert_part(coarse_ref, rows_ref, ext_ref, pieces, total, offset):
    width = rows_ref.shape[2]
    count = rows_ref.shape[0] // GROUP
    inner = total.shape[1]
    for ref, step, parts in pieces:
        c = lax.rem(coarse_ref[0] + step, GROUP)

        @pl.when(2 * c < GROUP)
        def _():
            for n, part in enumerate(parts):
                rows = rows_ref[pl.ds((2 * c + part) * count, count)].reshape(total.shape[0], width)
                total[...] += mm(rows, ref[n * width : (n + 1) * width, :inner])

        @pl.when(2 * c >= GROUP)
        def _():
            for n, part in enumerate(parts):
                ext = jnp.broadcast_to(ext_ref[2 * c + part - GROUP].astype(f32), (16, width)).astype(bf16)
                offset[...] += mm(ext, ref[n * width : (n + 1) * width, :inner])


def near_kernel(coarse_ref, rows_ref, ext_ref, own_ref, left_ref, right_ref, total_ref, offset_ref):
    total_ref[...] = jnp.zeros_like(total_ref)
    offset_ref[...] = jnp.zeros_like(offset_ref)
    pieces = ((own_ref, 0, (0, 1)), (left_ref, GROUP - 1, (0, 1)), (right_ref, 1, (0, 1)))
    expert_part(coarse_ref, rows_ref, ext_ref, pieces, total_ref, offset_ref)


def expert_kernel(
    coarse_ref,
    rows_ref,
    ext_ref,
    near_ref,
    near_offset_ref,
    own_ref,
    left_ref,
    right_ref,
    upper_ref,
    lower_ref,
    out_ref,
    total,
    offset,
):
    width = rows_ref.shape[2]
    count = rows_ref.shape[0] // GROUP
    inner = total.shape[1]
    hidden = inner // 2
    total[...] = near_ref[...]
    offset[...] = near_offset_ref[...]
    pieces = ((upper_ref, 2, (0,)), (lower_ref, 2, (1,)))
    expert_part(coarse_ref, rows_ref, ext_ref, pieces, total, offset)
    gate = total[:, :hidden] + offset[:1, :hidden]
    up = total[:, hidden:] + offset[:1, hidden:]
    act = (gate / (1.0 + jnp.exp(-gate)) * up).astype(bf16)

    def put(step, value):
        c = lax.rem(coarse_ref[0] + step, GROUP)
        out_ref[pl.ds(c * count, count)] = value.astype(bf16).reshape(count, *out_ref.shape[1:])

    for ref, step in ((own_ref, 0), (left_ref, GROUP - 1), (right_ref, 1)):
        put(step, mm(act, ref[:, inner:]))
    put(2, mm(act[:, :width], upper_ref[:, inner:]) + mm(act[:, width:], lower_ref[:, inner:]))


def combine_kernel(mask_ref, weigh_ref, back_ref, out_ref, last_ref):
    quarters, _, slots = weigh_ref.shape
    count, width = back_ref.shape[0] // quarters, back_ref.shape[2]
    bounds = jnp.sum(mask_ref[...])
    last = jnp.zeros(last_ref.shape, f32)
    for c in range(quarters):
        wh, wl = split(weigh_ref[c])
        back = back_ref[c * count : (c + 1) * count].reshape(weigh_ref.shape[1], width)
        part = mm(wh, back, ((0,), (0,))) + mm(wl, back, ((0,), (0,)))
        out_ref[c * slots : (c + 1) * slots] = part
        here = c * slots + iota((slots, 1), 0) == bounds - 1
        last = last + jnp.sum(jnp.where(here, part, 0.0), axis=0, keepdims=True)
    last_ref[...] = last


def spread_kernel(hidden_ref, rank_ref, stretch_ref, out_ref, before_ref):
    rows, slots = hidden_ref.shape[0], stretch_ref.shape[0]
    rank = rank_ref[...]
    chosen = jnp.where(iota((slots, rows), 0) == rank, 1.0, 0.0).astype(bf16)
    sh, sl = split(stretch_ref[...])
    spread = mm(chosen, sh, ((0,), (0,))) + mm(chosen, sl, ((0,), (0,)))
    eye = iota((rows, rows), 0) == iota((rows, rows), 1)
    before = jnp.sum(jnp.where(eye & (rank < 0), 1.0, 0.0), axis=1, keepdims=True)
    before_ref[...] = jnp.broadcast_to(before, before_ref.shape)
    out_ref[...] = (hidden_ref[...].astype(f32) + spread).astype(bf16)


def entry_kernel(hidden_ref, mixed_ref, before_ref, prev_ref, out_ref):
    entry = (hidden_ref[...].astype(f32) + prev_ref[...]).astype(bf16)
    out_ref[...] = jnp.where(before_ref[:, :1] > 0.0, entry, mixed_ref[...])


def sds(shape, dtype):
    return jax.ShapeDtypeStruct(shape, dtype)


def call(kernel, outs, args, scalars=0, scratch=(), flops=10**5, megabytes=16, far_in=(), far_out=(), same=None):
    def spec(far, index):
        space = pltpu.SMEM if index < 0 else pltpu.HBM if index in far else pltpu.VMEM
        return pl.BlockSpec(memory_space=space)

    many = isinstance(outs, tuple)
    places = tuple(spec(far_out, i) for i in range(len(outs))) if many else spec(far_out, 0)
    return pl.pallas_call(
        kernel,
        out_shape=outs,
        in_specs=[spec(far_in, i - scalars) for i in range(len(args))],
        out_specs=places,
        scratch_shapes=list(scratch),
        input_output_aliases=same or {},
        compiler_params=pltpu.CompilerParams(vmem_limit_bytes=megabytes * 2**20),
        cost_estimate=pl.CostEstimate(flops=flops, bytes_accessed=flops // 100, transcendentals=0),
    )(*args)


def shards(
    bytes_in,
    norm_gain,
    qkv_weight,
    gate_weight_enc,
    decay_rate,
    write_bias,
    head_gain,
    boundaries,
    picks,
    pick_gates,
    extension,
    expert_gate,
    expert_up,
    expert_down,
):
    x = bytes_in[0]
    rows, width = x.shape
    dim = HALF // 2
    seq = lax.axis_index("seq")
    spot = lax.axis_index("coarse").astype(jnp.int32)[None]
    seq_total = lax.axis_size("seq")
    core = (seq % 2).astype(jnp.int32)[None]
    place = ((seq // 2) % GROUP).astype(jnp.int32)[None]
    local_slots = picks.shape[1]
    slot_total = local_slots * GROUP
    pair_total = local_slots * picks.shape[2]
    everywhere = ("coarse", "seq", "exp")

    def exchange(array, axes, **kwargs):
        return lax.all_to_all(array, axes, split_axis=0, concat_axis=0, tiled=True, **kwargs)

    top = picks.shape[2]
    choice = call(choice_kernel, sds((GROUP, 2 * top, dim), f32), (picks[0].T, pick_gates[0].T), megabytes=63)
    choice = exchange(choice, "coarse")

    depth, hidden_units = expert_gate.shape[1:]
    columns = 2 * hidden_units + expert_down.shape[2]
    gate_rows = gate_weight_enc.transpose(0, 2, 1)
    own, give, local, x_share, weights = call(
        delta_kernel,
        (
            sds((dim, HALF), f32),
            sds((dim, HALF), f32),
            sds((2, rows, HALF), f32),
            sds((rows, HALF), bf16),
            sds((depth, columns), bf16),
        ),
        (
            x,
            norm_gain[None],
            qkv_weight,
            gate_rows,
            decay_rate[None],
            write_bias[None],
            expert_gate,
            expert_up,
            expert_down,
        ),
        scratch=(
            pltpu.VMEM((depth, columns), bf16),
            pltpu.VMEM((rows, width), bf16),
            pltpu.VMEM((1, width), f32),
            pltpu.VMEM(qkv_weight.shape, bf16),
            pltpu.VMEM(gate_rows.shape, bf16),
            pltpu.VMEM((1, 2), f32),
            pltpu.VMEM((1, 2), f32),
            pltpu.VMEM((8, dim, HALF), bf16),
            pltpu.VMEM((8, dim, dim), f32),
            pltpu.SemaphoreType.DMA((11,)),
        ),
        flops=2 * 10**9,
        megabytes=60,
        far_in=range(9),
        far_out=(4,),
    )

    give = call(after_kernel, sds(give.shape, f32), (choice, give), far_in=(0, 1), far_out=(0,), same={1: 0})

    swap = [(i, i ^ 1) for i in range(seq_total)]
    got = lax.ppermute(give, "seq", swap)
    rank = call(rank_kernel, sds((1, rows), jnp.int32), (boundaries,))
    take, weigh, routed = call(
        route_kernel,
        (
            sds((GROUP, pair_total, local_slots), bf16),
            sds((GROUP, pair_total, local_slots), f32),
            sds((8, dim), f32),
        ),
        (boundaries, choice),
    )
    message, first = call(
        pair_kernel, (sds((GROUP, dim, HALF), bf16), sds((dim, HALF), f32)), (core, own, got), scalars=1
    )
    half = depth // 2
    ring = [(i, (i + 1) % GROUP) for i in range(GROUP)]
    back = [(b, a) for a, b in ring]
    left = lax.ppermute(weights, "coarse", ring)
    right = lax.ppermute(weights, "coarse", back)
    facing = (lax.ppermute(left[:half], "coarse", ring), lax.ppermute(right[half:], "coarse", back))
    stride = 2 * GROUP
    groups = [
        [stride * g + 2 * i + c for i in range(GROUP)] for g in range(seq_total // stride) for c in range(2)
    ]
    chips = exchange(message, "seq", axis_index_groups=groups)
    before, total = call(
        group_kernel, (sds((dim, HALF), f32), sds((dim, HALF), f32)), (place, chips, routed), scalars=1, flops=10**9
    )
    state = jnp.zeros((dim, dim), bf16)
    for hop in range(seq_total // stride - 1):
        if hop == 0:
            outgoing = total[:, dim:].astype(bf16)
        else:
            outgoing = call(hop_kernel, sds((dim, dim), bf16), (total, state), flops=10**9)
        pairs = [(stride * hop + i, stride * (hop + 1) + i) for i in range(stride)]
        state = state + lax.ppermute(outgoing, "seq", pairs)
    states = call(enter_kernel, sds((2, dim, dim), f32), (core, before, first, state), scalars=1, flops=10**9)
    others = lax.ppermute(states, "seq", swap)

    devices = lax.axis_size(everywhere)
    capacity = GROUP * pair_total // devices
    hidden, outgoing = call(
        finish_kernel,
        (sds((rows, HALF), bf16), sds((devices, capacity, HALF), bf16)),
        (core, local, states, others, x_share, head_gain[None], boundaries, rank, take, left, right),
        scalars=1,
        far_in=(8, 9),
    )
    received = exchange(outgoing, everywhere)
    parts = (sds((pair_total, 2 * hidden_units), f32), sds((16, 2 * hidden_units), f32))
    extra_rows = extension.reshape(width // HALF, 1, HALF)
    near = call(near_kernel, parts, (spot, received, extra_rows, weights, left, right), scalars=1)
    value = call(
        expert_kernel,
        sds((devices, capacity, HALF), bf16),
        (spot, received, extra_rows, *near, weights, left, right, *facing),
        scalars=1,
        scratch=tuple(pltpu.VMEM(part.shape, part.dtype) for part in parts),
    )
    returned = exchange(value, everywhere)
    stretch, last = call(
        combine_kernel,
        (sds((slot_total, HALF), f32), sds((1, HALF), f32)),
        (boundaries, weigh, returned),
    )
    previous = lax.ppermute(last, "seq", [(i, i + 1) for i in range(seq_total - 1)])
    mixed, early = call(
        spread_kernel, (sds((rows, HALF), bf16), sds((rows, dim), f32)), (hidden, rank, stretch), flops=10**9
    )
    mixed = call(entry_kernel, sds((rows, HALF), bf16), (hidden, mixed, early, previous))
    return mixed[None]


def solution(mesh):
    placed = (
        P("exp", "seq", None),
        P(),
        P(None, None, "coarse"),
        P(None, None, "coarse"),
        P("coarse"),
        P("coarse"),
        P("coarse"),
        P("exp", "seq"),
        P("exp", ("seq", "coarse"), None),
        P("exp", ("seq", "coarse"), None),
        P(),
        P(("seq", "exp"), "coarse", None),
        P(("seq", "exp"), "coarse", None),
        P(("seq", "exp"), None, "coarse"),
    )
    return jax.shard_map(
        shards, mesh=mesh, in_specs=placed, out_specs=P("exp", "seq", "coarse"), check_vma=False
    )
```

```python
import jax
import jax.numpy as jnp
from jax import lax
from jax.experimental import pallas as pl
from jax.experimental.pallas import tpu as pltpu
from jax.sharding import PartitionSpec as P

f32 = jnp.float32
bf16 = jnp.bfloat16
HALF = 256
GROUP = 4


def mm(a, b, dims=((1,), (0,))):
    return lax.dot_general(a, b, (dims, ((), ())), preferred_element_type=f32)


def split(x):
    high = x.astype(bf16)
    return high, (x - high.astype(f32)).astype(bf16)


def mm3(a, b, dims=((1,), (0,))):
    (ah, al), (bh, bl) = a, b
    return mm(ah, bh, dims) + (mm(ah, bl, dims) + mm(al, bh, dims))


def iota(shape, dim):
    return lax.broadcasted_iota(jnp.int32, shape, dim)


def as_row(column):
    size = column.shape[0]
    eye = iota((size, size), 0) == iota((size, size), 1)
    return jnp.sum(jnp.where(eye, column, 0.0), axis=0, keepdims=True)


def choice_kernel(picks_ref, gates_ref, out_ref):
    top, slots = picks_ref.shape
    out_ref[...] = jnp.zeros_like(out_ref)
    for quarter in range(out_ref.shape[0]):
        out_ref[quarter, :top, :slots] = picks_ref[...].astype(f32)
        out_ref[quarter, top:, :slots] = gates_ref[...]


def after_kernel(choice_far, give_far, same_far):
    del choice_far, give_far, same_far


def delta_kernel(
    x_far,
    gain_far,
    w_far,
    gw_far,
    rate_far,
    bias_far,
    egate_far,
    eup_far,
    edown_far,
    own_ref,
    give_ref,
    local_ref,
    share_ref,
    weights_far,
    weights_ref,
    x_ref,
    gain_ref,
    w_ref,
    gw_ref,
    rate_ref,
    bias_ref,
    low,
    inv,
    sems,
):
    rows = x_ref.shape[0]
    dim = HALF // 2
    pairs = [(x_far, x_ref), (gain_far, gain_ref), (gw_far, gw_ref), (rate_far, rate_ref), (bias_far, bias_ref)]
    pairs.append((w_far, w_ref))
    start = 0
    for far in (egate_far, eup_far, edown_far):
        size = far.shape[2]
        pairs.append((far.at[0], weights_ref.at[:, pl.ds(start, size)]))
        start += size
    moves = [pltpu.make_async_copy(a, b, sems.at[n]) for n, (a, b) in enumerate(pairs)]
    for move in moves:
        move.start()
    for move in moves[:5]:
        move.wait()
    first = pl.multiple_of(lax.axis_index("coarse") * HALF, HALF)
    moves.append(pltpu.make_async_copy(x_ref.at[:, pl.ds(first, HALF)], share_ref, sems.at[9]))
    moves[9].start()

    x = x_ref[...].astype(f32)
    normed = (x * lax.rsqrt(jnp.mean(x * x, -1, keepdims=True) + 1e-05) * gain_ref[...]).astype(bf16)
    linear = mm(normed, jnp.concatenate([gw_ref[0], gw_ref[1]], axis=0), ((1,), (1,)))
    decay_in, write_in = linear[:, :2], linear[:, 2:]
    write = jax.nn.sigmoid(write_in + bias_ref[...])
    soft = jnp.maximum(decay_in, 0.0) + jnp.log1p(jnp.exp(-jnp.abs(decay_in)))
    log_decay = -rate_ref[...] * soft
    tri = jnp.where(iota((rows, rows), 0) >= iota((rows, rows), 1), 1.0, 0.0).astype(bf16)
    part_h = log_decay.astype(bf16)
    rest = log_decay - part_h.astype(f32)
    part_m = rest.astype(bf16)
    part_l = (rest - part_m.astype(f32)).astype(bf16)
    sums = mm(tri, jnp.concatenate([part_h, part_m, part_l], axis=1))
    cum = sums[:, 0:2] + (sums[:, 2:4] + sums[:, 4:6])

    moves[5].wait()

    def act(index):
        value = mm(normed, w_ref[index])
        return value / (1.0 + jnp.exp(-value))

    q_all, k_all, v_all = act(0), act(1), act(2)
    for move in moves[6:9]:
        move.wait()
    leave = pltpu.make_async_copy(weights_ref, weights_far, sems.at[10])
    leave.start()
    strict = iota((HALF, HALF), 0) > iota((HALF, HALF), 1)
    causal = iota((HALF, HALF), 0) >= iota((HALF, HALF), 1)
    pair = (iota((dim, dim), 0) >> 1) == (iota((dim, dim), 1) >> 1)
    eye = jnp.where(iota((dim, dim), 0) == iota((dim, dim), 1), 1.0, 0.0)
    keep = []
    for head in range(2):
        cols = slice(head * dim, (head + 1) * dim)
        q, k, v = q_all[:, cols], k_all[:, cols], v_all[:, cols]
        q = q * lax.rsqrt(jnp.sum(q * q, -1, keepdims=True) + 1e-06)
        k = k * lax.rsqrt(jnp.sum(k * k, -1, keepdims=True) + 1e-06)
        cum_col = cum[:, head : head + 1]
        cum_row = as_row(cum_col)
        beta = write[:, head : head + 1]
        kh, kl = split(k)
        deep = jnp.concatenate([kh, kl], axis=1)
        twice = jnp.concatenate([kh, kh], axis=1)
        cross = None
        inner = []
        for i, j in ((0, 0), (1, 1), (1, 0)):
            ri, rj = slice(i * HALF, (i + 1) * HALF), slice(j * HALF, (j + 1) * HALF)
            gram = mm(deep[ri], twice[rj], ((1,), (1,))) + mm(kh[ri], kl[rj], ((1,), (1,)))
            lower = beta[ri] * jnp.exp(jnp.minimum(cum_col[ri] - cum_row[:, rj], 0.0)) * gram
            if i == j:
                lower = jnp.where(strict, lower, 0.0)
                for sub in range(2):
                    rs = slice(sub * dim, (sub + 1) * dim)
                    block = 4 * head + 2 * i + sub
                    part = lower[rs, rs]
                    low[block] = jnp.concatenate(split(part), axis=1)
                    inv[block] = eye - jnp.where(pair, part, 0.0)
                inner.append(jnp.concatenate(split(lower[dim:, :dim]), axis=1))
            else:
                cross = split(lower)
        right = jnp.concatenate([(beta * jnp.exp(cum_col)) * k, beta * v], axis=1)
        last = cum_col[rows - 1 : rows]
        (qh, ql) = split(q)
        broad = jnp.concatenate([qh, ql], axis=1)
        attend = {}
        for i, j in ((0, 0), (1, 1), (1, 0)):
            ri, rj = slice(i * HALF, (i + 1) * HALF), slice(j * HALF, (j + 1) * HALF)
            gram = mm(broad[ri], twice[rj], ((1,), (1,))) + mm(qh[ri], kl[rj], ((1,), (1,)))
            gram = gram * jnp.exp(jnp.minimum(cum_col[ri] - cum_row[:, rj], 0.0))
            attend[i, j] = split(jnp.where(causal, gram, 0.0) if i == j else gram)
        grown = jnp.exp(cum_col) * q
        keep.append((cross, inner, right, k * jnp.exp(last - cum_col), jnp.exp(last), attend, grown))

    def packed(left, block):
        wide = jnp.concatenate(split(block), axis=1)
        out = mm(left, jnp.concatenate([wide, wide], axis=0))
        return out[:, :dim] + out[:, dim:]

    def level(step):
        r, c = iota((dim, HALF), 0), iota((dim, HALF), 1) & (dim - 1)
        above = ((r >> (step + 1)) == (c >> (step + 1))) & ((r >> step) > (c >> step))
        zero = jnp.zeros((dim, HALF), bf16)
        blocks = [inv[m] for m in range(8)]
        inside = [packed(jnp.where(above, low[m], zero), blocks[m]) for m in range(8)]
        for m in range(8):
            inv[m] = blocks[m] - packed(jnp.concatenate(split(blocks[m]), axis=1), inside[m])

    for step in range(1, 7):
        level(step)
    for head in range(2):
        cross, inner, right, k_end, scale, attend, grown = keep[head]
        full = []
        for i in range(2):
            top, bottom = inv[4 * head + 2 * i], inv[4 * head + 2 * i + 1]
            corner = packed(jnp.concatenate(split(bottom), axis=1), packed(inner[i], top))
            upper = jnp.concatenate([top, jnp.zeros_like(top)], axis=1)
            full.append(split(jnp.concatenate([upper, jnp.concatenate([-corner, bottom], axis=1)], axis=0)))
        first = mm3(full[0], split(right[:HALF]))
        second = right[HALF:] - mm3(cross, split(first))
        second = mm3(full[1], split(second))
        solved = jnp.concatenate([first, second], axis=0)
        halves = (split(first), split(second))
        for i in range(2):
            ri = slice(i * HALF, (i + 1) * HALF)
            out = mm3(attend[i, i], halves[i])
            if i > 0:
                out = out + mm3(attend[1, 0], halves[0])
            local_ref[head, ri] = jnp.concatenate([grown[ri] - out[:, :dim], out[:, dim:]], axis=1)
        ends = mm3(split(k_end), split(solved), ((0,), (0,)))
        keep[head] = jnp.concatenate([scale * eye - ends[:, :dim], ends[:, dim:]], axis=1)
    lead = lax.rem(lax.axis_index("seq"), 2) == 0
    own_ref[...] = jnp.where(lead, keep[0], keep[1])
    give_ref[...] = jnp.where(lead, keep[1], keep[0])
    moves[9].wait()
    leave.wait()


def compose(late, early):
    dim = late.shape[0]
    both = mm3(split(late[:, :dim]), split(early))
    return jnp.concatenate([both[:, :dim], both[:, dim:] + late[:, dim:]], axis=1)


def pair_kernel(core_ref, own_ref, got_ref, msg_ref, first_ref):
    dim = HALF // 2
    lead = core_ref[0] == 0
    own, got = own_ref[...], got_ref[...]
    early, late = jnp.where(lead, own, got), jnp.where(lead, got, own)
    first_ref[...] = early
    eye = jnp.where(iota((dim, HALF), 0) == iota((dim, HALF), 1), 1.0, 0.0)
    message = (compose(late, early) - eye).astype(bf16)
    for chip in range(GROUP):
        msg_ref[chip] = message


def group_kernel(place_ref, got_ref, before_ref, total_ref):
    dim = HALF // 2
    eye = jnp.where(iota((dim, HALF), 0) == iota((dim, HALF), 1), 1.0, 0.0)
    place = place_ref[0]
    running = eye
    before = eye
    for chip in range(GROUP):
        item = got_ref[chip].astype(f32) + eye
        running = item if chip == 0 else compose(item, running)
        if chip + 1 < GROUP:
            before = jnp.where(place == chip + 1, running, before)
    before_ref[...] = before
    total_ref[...] = running


def hop_kernel(total_ref, state_ref, token_ref, out_ref):
    del token_ref
    dim = HALF // 2
    moved = mm3(split(total_ref[:, :dim]), split(state_ref[...].astype(f32)))
    out_ref[...] = (moved + total_ref[:, dim:]).astype(bf16)


def enter_kernel(core_ref, before_ref, first_ref, state_ref, pair_ref):
    dim = HALF // 2
    state = mm3(split(before_ref[:, :dim]), split(state_ref[...].astype(f32))) + before_ref[:, dim:]
    after = mm3(split(first_ref[:, :dim]), split(state)) + first_ref[:, dim:]
    lead = core_ref[0] == 0
    pair_ref[0] = jnp.where(lead, state, after)
    pair_ref[1] = jnp.where(lead, after, state)


def finish_kernel(
    core_ref,
    local_ref,
    own_ref,
    got_ref,
    x_ref,
    gain_ref,
    mask_ref,
    rank_ref,
    take_ref,
    left_far,
    right_far,
    hidden_ref,
    send_ref,
):
    del left_far, right_far
    dim = HALF // 2
    lead = core_ref[0] == 0
    keep, got = own_ref[0], got_ref[1]
    states = (jnp.where(lead, keep, got), jnp.where(lead, got, keep))
    parts = []
    for head in range(2):
        out = local_ref[head, :, dim:] + mm3(split(local_ref[head, :, :dim]), split(states[head]))
        norm = out * lax.rsqrt(jnp.mean(out * out, -1, keepdims=True) + 1e-06)
        parts.append((norm * gain_ref[:, head * dim : (head + 1) * dim]).astype(bf16))
    normed = jnp.concatenate(parts, axis=1)
    hidden = (x_ref[...].astype(f32) + normed.astype(f32)).astype(bf16)
    hidden_ref[...] = hidden
    quarters, _, slots = take_ref.shape
    count = send_ref.shape[0] // quarters
    chosen = (iota((quarters * slots, hidden.shape[0]), 0) == rank_ref[...]) & (mask_ref[...] == 1)
    picked = mm(jnp.where(chosen, 1.0, 0.0).astype(bf16), hidden).astype(bf16)
    for quarter in range(quarters):
        rows = picked[quarter * slots : (quarter + 1) * slots]
        taken = mm(take_ref[quarter], rows).astype(bf16)
        send_ref[quarter * count : (quarter + 1) * count] = taken.reshape(count, *send_ref.shape[1:])


def rank_kernel(mask_ref, rank_ref):
    rows = mask_ref.shape[1]
    tri = jnp.where(iota((rows, rows), 0) <= iota((rows, rows), 1), 1.0, 0.0).astype(bf16)
    wide = jnp.broadcast_to(mask_ref[...].astype(f32), (16, rows)).astype(bf16)
    rank_ref[...] = mm(wide, tri)[:1].astype(jnp.int32) - 1


def route_kernel(mask_ref, choice_ref, take_ref, weigh_ref, token_ref):
    quarters, total, slots = take_ref.shape
    top = choice_ref.shape[1] // 2
    count = jnp.sum(mask_ref[...])
    line = iota((total, slots), 0)
    expert = (line >> 1).astype(f32)
    earlier = jnp.where(iota((slots, slots), 0) < iota((slots, slots), 1), 1.0, 0.0).astype(bf16)
    for quarter in range(quarters):
        live = quarter * slots + iota((total, slots), 1) < count
        hit = jnp.zeros((total, slots), f32)
        weight = jnp.zeros((total, slots), f32)
        for pick in range(top):
            same = (expert == choice_ref[quarter, pick : pick + 1, :slots]) & live
            hit = hit + jnp.where(same, 1.0, 0.0)
            weight = weight + jnp.where(same, choice_ref[quarter, top + pick : top + pick + 1, :slots], 0.0)
        arrival = mm(hit.astype(bf16), earlier).astype(jnp.int32)
        found = (hit > 0.0) & (arrival == (line & 1))
        take_ref[quarter] = jnp.where(found, 1.0, 0.0).astype(bf16)
        weigh_ref[quarter] = jnp.where(found, weight, 0.0)


def expert_part(coarse_ref, rows_ref, ext_ref, pieces, total, offset):
    width = rows_ref.shape[2]
    count = rows_ref.shape[0] // GROUP
    inner = total.shape[1]
    for ref, step, parts in pieces:
        c = lax.rem(coarse_ref[0] + step, GROUP)

        @pl.when(2 * c < GROUP)
        def _():
            for n, part in enumerate(parts):
                rows = rows_ref[pl.ds((2 * c + part) * count, count)].reshape(total.shape[0], width)
                total[...] += mm(rows, ref[n * width : (n + 1) * width, :inner])

        @pl.when(2 * c >= GROUP)
        def _():
            for n, part in enumerate(parts):
                ext = jnp.broadcast_to(ext_ref[2 * c + part - GROUP].astype(f32), (16, width)).astype(bf16)
                offset[...] += mm(ext, ref[n * width : (n + 1) * width, :inner])


def near_kernel(coarse_ref, rows_ref, ext_ref, own_ref, left_ref, right_ref, total_ref, offset_ref):
    total_ref[...] = jnp.zeros_like(total_ref)
    offset_ref[...] = jnp.zeros_like(offset_ref)
    pieces = ((own_ref, 0, (0, 1)), (left_ref, GROUP - 1, (0, 1)), (right_ref, 1, (0, 1)))
    expert_part(coarse_ref, rows_ref, ext_ref, pieces, total_ref, offset_ref)


def expert_kernel(
    coarse_ref,
    rows_ref,
    ext_ref,
    near_ref,
    near_offset_ref,
    own_ref,
    left_ref,
    right_ref,
    upper_ref,
    lower_ref,
    out_ref,
    total,
    offset,
):
    width = rows_ref.shape[2]
    count = rows_ref.shape[0] // GROUP
    inner = total.shape[1]
    hidden = inner // 2
    total[...] = near_ref[...]
    offset[...] = near_offset_ref[...]
    pieces = ((upper_ref, 2, (0,)), (lower_ref, 2, (1,)))
    expert_part(coarse_ref, rows_ref, ext_ref, pieces, total, offset)
    gate = total[:, :hidden] + offset[:1, :hidden]
    up = total[:, hidden:] + offset[:1, hidden:]
    act = (gate / (1.0 + jnp.exp(-gate)) * up).astype(bf16)

    def put(step, value):
        c = lax.rem(coarse_ref[0] + step, GROUP)
        out_ref[pl.ds(c * count, count)] = value.astype(bf16).reshape(count, *out_ref.shape[1:])

    for ref, step in ((own_ref, 0), (left_ref, GROUP - 1), (right_ref, 1)):
        put(step, mm(act, ref[:, inner:]))
    put(2, mm(act[:, :width], upper_ref[:, inner:]) + mm(act[:, width:], lower_ref[:, inner:]))


def combine_kernel(mask_ref, weigh_ref, back_ref, out_ref, last_ref):
    quarters, _, slots = weigh_ref.shape
    count, width = back_ref.shape[0] // quarters, back_ref.shape[2]
    bounds = jnp.sum(mask_ref[...])
    last = jnp.zeros(last_ref.shape, f32)
    for c in range(quarters):
        wh, wl = split(weigh_ref[c])
        back = back_ref[c * count : (c + 1) * count].reshape(weigh_ref.shape[1], width)
        part = mm(wh, back, ((0,), (0,))) + mm(wl, back, ((0,), (0,)))
        out_ref[c * slots : (c + 1) * slots] = part
        here = c * slots + iota((slots, 1), 0) == bounds - 1
        last = last + jnp.sum(jnp.where(here, part, 0.0), axis=0, keepdims=True)
    last_ref[...] = last


def spread_kernel(hidden_ref, rank_ref, stretch_ref, out_ref, before_ref):
    rows, slots = hidden_ref.shape[0], stretch_ref.shape[0]
    rank = rank_ref[...]
    chosen = jnp.where(iota((slots, rows), 0) == rank, 1.0, 0.0).astype(bf16)
    sh, sl = split(stretch_ref[...])
    spread = mm(chosen, sh, ((0,), (0,))) + mm(chosen, sl, ((0,), (0,)))
    eye = iota((rows, rows), 0) == iota((rows, rows), 1)
    before = jnp.sum(jnp.where(eye & (rank < 0), 1.0, 0.0), axis=1, keepdims=True)
    before_ref[...] = jnp.broadcast_to(before, before_ref.shape)
    out_ref[...] = (hidden_ref[...].astype(f32) + spread).astype(bf16)


def entry_kernel(hidden_ref, mixed_ref, before_ref, prev_ref, out_ref):
    entry = (hidden_ref[...].astype(f32) + prev_ref[...]).astype(bf16)
    out_ref[...] = jnp.where(before_ref[:, :1] > 0.0, entry, mixed_ref[...])


def sds(shape, dtype):
    return jax.ShapeDtypeStruct(shape, dtype)


def call(kernel, outs, args, scalars=0, scratch=(), flops=10**5, megabytes=16, far_in=(), far_out=(), same=None):
    def spec(far, index):
        space = pltpu.SMEM if index < 0 else pltpu.HBM if index in far else pltpu.VMEM
        return pl.BlockSpec(memory_space=space)

    many = isinstance(outs, tuple)
    places = tuple(spec(far_out, i) for i in range(len(outs))) if many else spec(far_out, 0)
    return pl.pallas_call(
        kernel,
        out_shape=outs,
        in_specs=[spec(far_in, i - scalars) for i in range(len(args))],
        out_specs=places,
        scratch_shapes=list(scratch),
        input_output_aliases=same or {},
        compiler_params=pltpu.CompilerParams(vmem_limit_bytes=megabytes * 2**20),
        cost_estimate=pl.CostEstimate(flops=flops, bytes_accessed=flops // 100, transcendentals=0),
    )(*args)


def shards(
    bytes_in,
    norm_gain,
    qkv_weight,
    gate_weight_enc,
    decay_rate,
    write_bias,
    head_gain,
    boundaries,
    picks,
    pick_gates,
    extension,
    expert_gate,
    expert_up,
    expert_down,
):
    x = bytes_in[0]
    rows, width = x.shape
    dim = HALF // 2
    seq = lax.axis_index("seq")
    spot = lax.axis_index("coarse").astype(jnp.int32)[None]
    seq_total = lax.axis_size("seq")
    core = (seq % 2).astype(jnp.int32)[None]
    place = ((seq // 2) % GROUP).astype(jnp.int32)[None]
    local_slots = picks.shape[1]
    slot_total = local_slots * GROUP
    pair_total = local_slots * picks.shape[2]
    everywhere = ("coarse", "seq", "exp")

    def exchange(array, axes, **kwargs):
        return lax.all_to_all(array, axes, split_axis=0, concat_axis=0, tiled=True, **kwargs)

    top = picks.shape[2]
    choice = call(choice_kernel, sds((GROUP, 2 * top, dim), f32), (picks[0].T, pick_gates[0].T), megabytes=63)
    choice = exchange(choice, "coarse")

    depth, hidden_units = expert_gate.shape[1:]
    columns = 2 * hidden_units + expert_down.shape[2]
    gate_rows = gate_weight_enc.transpose(0, 2, 1)
    own, give, local, x_share, weights = call(
        delta_kernel,
        (
            sds((dim, HALF), f32),
            sds((dim, HALF), f32),
            sds((2, rows, HALF), f32),
            sds((rows, HALF), bf16),
            sds((depth, columns), bf16),
        ),
        (
            x,
            norm_gain[None],
            qkv_weight,
            gate_rows,
            decay_rate[None],
            write_bias[None],
            expert_gate,
            expert_up,
            expert_down,
        ),
        scratch=(
            pltpu.VMEM((depth, columns), bf16),
            pltpu.VMEM((rows, width), bf16),
            pltpu.VMEM((1, width), f32),
            pltpu.VMEM(qkv_weight.shape, bf16),
            pltpu.VMEM(gate_rows.shape, bf16),
            pltpu.VMEM((1, 2), f32),
            pltpu.VMEM((1, 2), f32),
            pltpu.VMEM((8, dim, HALF), bf16),
            pltpu.VMEM((8, dim, dim), f32),
            pltpu.SemaphoreType.DMA((11,)),
        ),
        flops=2 * 10**9,
        megabytes=60,
        far_in=range(9),
        far_out=(4,),
    )

    give = call(after_kernel, sds(give.shape, f32), (choice, give), far_in=(0, 1), far_out=(0,), same={1: 0})

    swap = [(i, i ^ 1) for i in range(seq_total)]
    got = lax.ppermute(give, "seq", swap)
    rank = call(rank_kernel, sds((1, rows), jnp.int32), (boundaries,))
    take, weigh, routed = call(
        route_kernel,
        (
            sds((GROUP, pair_total, local_slots), bf16),
            sds((GROUP, pair_total, local_slots), f32),
            sds((8, dim), f32),
        ),
        (boundaries, choice),
    )
    message, first = call(
        pair_kernel, (sds((GROUP, dim, HALF), bf16), sds((dim, HALF), f32)), (core, own, got), scalars=1
    )
    half = depth // 2
    ring = [(i, (i + 1) % GROUP) for i in range(GROUP)]
    back = [(b, a) for a, b in ring]
    left = lax.ppermute(weights, "coarse", ring)
    right = lax.ppermute(weights, "coarse", back)
    facing = (lax.ppermute(left[:half], "coarse", ring), lax.ppermute(right[half:], "coarse", back))
    stride = 2 * GROUP
    groups = [
        [stride * g + 2 * i + c for i in range(GROUP)] for g in range(seq_total // stride) for c in range(2)
    ]
    chips = exchange(message, "seq", axis_index_groups=groups)
    before, total = call(
        group_kernel, (sds((dim, HALF), f32), sds((dim, HALF), f32)), (place, chips), scalars=1, flops=10**9
    )
    state = jnp.zeros((dim, dim), bf16)
    for hop in range(seq_total // stride - 1):
        if hop == 0:
            outgoing = total[:, dim:].astype(bf16)
        else:
            outgoing = call(hop_kernel, sds((dim, dim), bf16), (total, state, routed), flops=10**9)
        pairs = [(stride * hop + i, stride * (hop + 1) + i) for i in range(stride)]
        state = state + lax.ppermute(outgoing, "seq", pairs)
    states = call(enter_kernel, sds((2, dim, dim), f32), (core, before, first, state), scalars=1, flops=10**9)
    others = lax.ppermute(states, "seq", swap)

    devices = lax.axis_size(everywhere)
    capacity = GROUP * pair_total // devices
    hidden, outgoing = call(
        finish_kernel,
        (sds((rows, HALF), bf16), sds((devices, capacity, HALF), bf16)),
        (core, local, states, others, x_share, head_gain[None], boundaries, rank, take, left, right),
        scalars=1,
        far_in=(8, 9),
    )
    received = exchange(outgoing, everywhere)
    parts = (sds((pair_total, 2 * hidden_units), f32), sds((16, 2 * hidden_units), f32))
    extra_rows = extension.reshape(width // HALF, 1, HALF)
    near = call(near_kernel, parts, (spot, received, extra_rows, weights, left, right), scalars=1)
    value = call(
        expert_kernel,
        sds((devices, capacity, HALF), bf16),
        (spot, received, extra_rows, *near, weights, left, right, *facing),
        scalars=1,
        scratch=tuple(pltpu.VMEM(part.shape, part.dtype) for part in parts),
    )
    returned = exchange(value, everywhere)
    stretch, last = call(
        combine_kernel,
        (sds((slot_total, HALF), f32), sds((1, HALF), f32)),
        (boundaries, weigh, returned),
    )
    previous = lax.ppermute(last, "seq", [(i, i + 1) for i in range(seq_total - 1)])
    mixed, early = call(
        spread_kernel, (sds((rows, HALF), bf16), sds((rows, dim), f32)), (hidden, rank, stretch), flops=10**9
    )
    mixed = call(entry_kernel, sds((rows, HALF), bf16), (hidden, mixed, early, previous))
    return mixed[None]


def solution(mesh):
    placed = (
        P("exp", "seq", None),
        P(),
        P(None, None, "coarse"),
        P(None, None, "coarse"),
        P("coarse"),
        P("coarse"),
        P("coarse"),
        P("exp", "seq"),
        P("exp", ("seq", "coarse"), None),
        P("exp", ("seq", "coarse"), None),
        P(),
        P(("seq", "exp"), "coarse", None),
        P(("seq", "exp"), "coarse", None),
        P(("seq", "exp"), None, "coarse"),
    )
    return jax.shard_map(
        shards, mesh=mesh, in_specs=placed, out_specs=P("exp", "seq", "coarse"), check_vma=False
    )
```

```python
import jax
import jax.numpy as jnp
from jax import lax
from jax.experimental import pallas as pl
from jax.experimental.pallas import tpu as pltpu
from jax.sharding import PartitionSpec as P

f32 = jnp.float32
bf16 = jnp.bfloat16
HALF = 256
GROUP = 4
PIECES = 4


def mm(a, b, dims=((1,), (0,))):
    return lax.dot_general(a, b, (dims, ((), ())), preferred_element_type=f32)


def split(x):
    high = x.astype(bf16)
    return high, (x - high.astype(f32)).astype(bf16)


def mm3(a, b, dims=((1,), (0,))):
    (ah, al), (bh, bl) = a, b
    return mm(ah, bh, dims) + (mm(ah, bl, dims) + mm(al, bh, dims))


def iota(shape, dim):
    return lax.broadcasted_iota(jnp.int32, shape, dim)


def as_row(column):
    size = column.shape[0]
    eye = iota((size, size), 0) == iota((size, size), 1)
    return jnp.sum(jnp.where(eye, column, 0.0), axis=0, keepdims=True)


def choice_kernel(picks_ref, gates_ref, out_ref):
    top, slots = picks_ref.shape
    out_ref[...] = jnp.zeros_like(out_ref)
    for quarter in range(out_ref.shape[0]):
        out_ref[quarter, :top, :slots] = picks_ref[...].astype(f32)
        out_ref[quarter, top:, :slots] = gates_ref[...]


def after_kernel(choice_far, give_far, same_far):
    del choice_far, give_far, same_far


def delta_kernel(
    x_far,
    gain_far,
    w_far,
    gw_far,
    rate_far,
    bias_far,
    egate_far,
    eup_far,
    edown_far,
    own_ref,
    give_ref,
    local_ref,
    share_ref,
    weights_far,
    weights_ref,
    x_ref,
    gain_ref,
    w_ref,
    gw_ref,
    rate_ref,
    bias_ref,
    low,
    inv,
    sems,
):
    rows = x_ref.shape[0]
    dim = HALF // 2
    pairs = [(gain_far, gain_ref), (gw_far, gw_ref), (rate_far, rate_ref), (bias_far, bias_ref), (w_far, w_ref)]
    start = 0
    for far in (egate_far, eup_far, edown_far):
        size = far.shape[2]
        pairs.append((far.at[0], weights_ref.at[:, pl.ds(start, size)]))
        start += size
    moves = [pltpu.make_async_copy(a, b, sems.at[n]) for n, (a, b) in enumerate(pairs)]
    size = rows // PIECES
    bytes_in = []
    for n in range(PIECES):
        spot = pl.ds(n * size, size)
        bytes_in.append(pltpu.make_async_copy(x_far.at[spot], x_ref.at[spot], sems.at[10 + n]))
    for move in bytes_in + moves:
        move.start()
    for move in moves[:4]:
        move.wait()
    gain = gain_ref[...]
    parts = []
    for n in range(PIECES):
        bytes_in[n].wait()
        x = x_ref[n * size : (n + 1) * size].astype(f32)
        parts.append((x * lax.rsqrt(jnp.mean(x * x, -1, keepdims=True) + 1e-05) * gain).astype(bf16))
    normed = jnp.concatenate(parts, axis=0)
    first = pl.multiple_of(lax.axis_index("coarse") * HALF, HALF)
    moves.append(pltpu.make_async_copy(x_ref.at[:, pl.ds(first, HALF)], share_ref, sems.at[8]))
    moves[8].start()

    linear = mm(normed, jnp.concatenate([gw_ref[0], gw_ref[1]], axis=0), ((1,), (1,)))
    decay_in, write_in = linear[:, :2], linear[:, 2:]
    write = jax.nn.sigmoid(write_in + bias_ref[...])
    soft = jnp.maximum(decay_in, 0.0) + jnp.log1p(jnp.exp(-jnp.abs(decay_in)))
    log_decay = -rate_ref[...] * soft
    tri = jnp.where(iota((rows, rows), 0) >= iota((rows, rows), 1), 1.0, 0.0).astype(bf16)
    part_h = log_decay.astype(bf16)
    rest = log_decay - part_h.astype(f32)
    part_m = rest.astype(bf16)
    part_l = (rest - part_m.astype(f32)).astype(bf16)
    sums = mm(tri, jnp.concatenate([part_h, part_m, part_l], axis=1))
    cum = sums[:, 0:2] + (sums[:, 2:4] + sums[:, 4:6])

    moves[4].wait()

    def act(index):
        value = mm(normed, w_ref[index])
        return value / (1.0 + jnp.exp(-value))

    q_all, k_all, v_all = act(0), act(1), act(2)
    for move in moves[5:8]:
        move.wait()
    leave = pltpu.make_async_copy(weights_ref, weights_far, sems.at[9])
    leave.start()
    strict = iota((HALF, HALF), 0) > iota((HALF, HALF), 1)
    causal = iota((HALF, HALF), 0) >= iota((HALF, HALF), 1)
    pair = (iota((dim, dim), 0) >> 1) == (iota((dim, dim), 1) >> 1)
    eye = jnp.where(iota((dim, dim), 0) == iota((dim, dim), 1), 1.0, 0.0)
    keep = []
    for head in range(2):
        cols = slice(head * dim, (head + 1) * dim)
        q, k, v = q_all[:, cols], k_all[:, cols], v_all[:, cols]
        q = q * lax.rsqrt(jnp.sum(q * q, -1, keepdims=True) + 1e-06)
        k = k * lax.rsqrt(jnp.sum(k * k, -1, keepdims=True) + 1e-06)
        cum_col = cum[:, head : head + 1]
        cum_row = as_row(cum_col)
        beta = write[:, head : head + 1]
        kh, kl = split(k)
        deep = jnp.concatenate([kh, kl], axis=1)
        twice = jnp.concatenate([kh, kh], axis=1)
        cross = None
        inner = []
        for i, j in ((0, 0), (1, 1), (1, 0)):
            ri, rj = slice(i * HALF, (i + 1) * HALF), slice(j * HALF, (j + 1) * HALF)
            gram = mm(deep[ri], twice[rj], ((1,), (1,))) + mm(kh[ri], kl[rj], ((1,), (1,)))
            lower = beta[ri] * jnp.exp(jnp.minimum(cum_col[ri] - cum_row[:, rj], 0.0)) * gram
            if i == j:
                lower = jnp.where(strict, lower, 0.0)
                for sub in range(2):
                    rs = slice(sub * dim, (sub + 1) * dim)
                    block = 4 * head + 2 * i + sub
                    part = lower[rs, rs]
                    low[block] = jnp.concatenate(split(part), axis=1)
                    inv[block] = eye - jnp.where(pair, part, 0.0)
                inner.append(jnp.concatenate(split(lower[dim:, :dim]), axis=1))
            else:
                cross = split(lower)
        right = jnp.concatenate([(beta * jnp.exp(cum_col)) * k, beta * v], axis=1)
        last = cum_col[rows - 1 : rows]
        (qh, ql) = split(q)
        broad = jnp.concatenate([qh, ql], axis=1)
        attend = {}
        for i, j in ((0, 0), (1, 1), (1, 0)):
            ri, rj = slice(i * HALF, (i + 1) * HALF), slice(j * HALF, (j + 1) * HALF)
            gram = mm(broad[ri], twice[rj], ((1,), (1,))) + mm(qh[ri], kl[rj], ((1,), (1,)))
            gram = gram * jnp.exp(jnp.minimum(cum_col[ri] - cum_row[:, rj], 0.0))
            attend[i, j] = split(jnp.where(causal, gram, 0.0) if i == j else gram)
        grown = jnp.exp(cum_col) * q
        keep.append((cross, inner, right, k * jnp.exp(last - cum_col), jnp.exp(last), attend, grown))

    def packed(left, block):
        wide = jnp.concatenate(split(block), axis=1)
        out = mm(left, jnp.concatenate([wide, wide], axis=0))
        return out[:, :dim] + out[:, dim:]

    def level(step):
        r, c = iota((dim, HALF), 0), iota((dim, HALF), 1) & (dim - 1)
        above = ((r >> (step + 1)) == (c >> (step + 1))) & ((r >> step) > (c >> step))
        zero = jnp.zeros((dim, HALF), bf16)
        blocks = [inv[m] for m in range(8)]
        inside = [packed(jnp.where(above, low[m], zero), blocks[m]) for m in range(8)]
        for m in range(8):
            inv[m] = blocks[m] - packed(jnp.concatenate(split(blocks[m]), axis=1), inside[m])

    for step in range(1, 7):
        level(step)
    for head in range(2):
        cross, inner, right, k_end, scale, attend, grown = keep[head]
        full = []
        for i in range(2):
            top, bottom = inv[4 * head + 2 * i], inv[4 * head + 2 * i + 1]
            corner = packed(jnp.concatenate(split(bottom), axis=1), packed(inner[i], top))
            upper = jnp.concatenate([top, jnp.zeros_like(top)], axis=1)
            full.append(split(jnp.concatenate([upper, jnp.concatenate([-corner, bottom], axis=1)], axis=0)))
        first = mm3(full[0], split(right[:HALF]))
        second = right[HALF:] - mm3(cross, split(first))
        second = mm3(full[1], split(second))
        solved = jnp.concatenate([first, second], axis=0)
        halves = (split(first), split(second))
        for i in range(2):
            ri = slice(i * HALF, (i + 1) * HALF)
            out = mm3(attend[i, i], halves[i])
            if i > 0:
                out = out + mm3(attend[1, 0], halves[0])
            local_ref[head, ri] = jnp.concatenate([grown[ri] - out[:, :dim], out[:, dim:]], axis=1)
        ends = mm3(split(k_end), split(solved), ((0,), (0,)))
        keep[head] = jnp.concatenate([scale * eye - ends[:, :dim], ends[:, dim:]], axis=1)
    lead = lax.rem(lax.axis_index("seq"), 2) == 0
    own_ref[...] = jnp.where(lead, keep[0], keep[1])
    give_ref[...] = jnp.where(lead, keep[1], keep[0])
    moves[8].wait()
    leave.wait()


def compose(late, early):
    dim = late.shape[0]
    both = mm3(split(late[:, :dim]), split(early))
    return jnp.concatenate([both[:, :dim], both[:, dim:] + late[:, dim:]], axis=1)


def stage_kernel(own_ref, out_ref):
    out_ref[...] = own_ref[...]


def pair_kernel(core_ref, own_ref, got_ref, msg_ref, first_ref):
    dim = HALF // 2
    lead = core_ref[0] == 0
    own, got = own_ref[...], got_ref[...]
    early, late = jnp.where(lead, own, got), jnp.where(lead, got, own)
    first_ref[...] = early
    eye = jnp.where(iota((dim, HALF), 0) == iota((dim, HALF), 1), 1.0, 0.0)
    message = (compose(late, early) - eye).astype(bf16)
    for chip in range(GROUP):
        msg_ref[chip] = message


def group_kernel(place_ref, got_ref, before_ref, total_ref):
    dim = HALF // 2
    eye = jnp.where(iota((dim, HALF), 0) == iota((dim, HALF), 1), 1.0, 0.0)
    place = place_ref[0]
    running = eye
    before = eye
    for chip in range(GROUP):
        item = got_ref[chip].astype(f32) + eye
        running = item if chip == 0 else compose(item, running)
        if chip + 1 < GROUP:
            before = jnp.where(place == chip + 1, running, before)
    before_ref[...] = before
    total_ref[...] = running


def hop_kernel(total_ref, state_ref, token_ref, out_ref):
    del token_ref
    dim = HALF // 2
    moved = mm3(split(total_ref[:, :dim]), split(state_ref[...].astype(f32)))
    out_ref[...] = (moved + total_ref[:, dim:]).astype(bf16)


def enter_kernel(core_ref, before_ref, first_ref, state_ref, pair_ref):
    dim = HALF // 2
    state = mm3(split(before_ref[:, :dim]), split(state_ref[...].astype(f32))) + before_ref[:, dim:]
    after = mm3(split(first_ref[:, :dim]), split(state)) + first_ref[:, dim:]
    lead = core_ref[0] == 0
    pair_ref[0] = jnp.where(lead, state, after)
    pair_ref[1] = jnp.where(lead, after, state)


def finish_kernel(
    core_ref,
    local_ref,
    own_ref,
    got_ref,
    x_ref,
    gain_ref,
    mask_ref,
    rank_ref,
    take_ref,
    left_far,
    right_far,
    hidden_ref,
    send_ref,
    token_ref,
):
    token_ref[...] = jnp.zeros_like(token_ref)
    del left_far, right_far
    dim = HALF // 2
    lead = core_ref[0] == 0
    keep, got = own_ref[0], got_ref[1]
    states = (jnp.where(lead, keep, got), jnp.where(lead, got, keep))
    parts = []
    for head in range(2):
        out = local_ref[head, :, dim:] + mm3(split(local_ref[head, :, :dim]), split(states[head]))
        norm = out * lax.rsqrt(jnp.mean(out * out, -1, keepdims=True) + 1e-06)
        parts.append((norm * gain_ref[:, head * dim : (head + 1) * dim]).astype(bf16))
    normed = jnp.concatenate(parts, axis=1)
    hidden = (x_ref[...].astype(f32) + normed.astype(f32)).astype(bf16)
    hidden_ref[...] = hidden
    quarters, _, slots = take_ref.shape
    count = send_ref.shape[0] // quarters
    chosen = (iota((quarters * slots, hidden.shape[0]), 0) == rank_ref[...]) & (mask_ref[...] == 1)
    picked = mm(jnp.where(chosen, 1.0, 0.0).astype(bf16), hidden).astype(bf16)
    for quarter in range(quarters):
        rows = picked[quarter * slots : (quarter + 1) * slots]
        taken = mm(take_ref[quarter], rows).astype(bf16)
        send_ref[quarter * count : (quarter + 1) * count] = taken.reshape(count, *send_ref.shape[1:])


def rank_kernel(mask_ref, rank_ref):
    rows = mask_ref.shape[1]
    tri = jnp.where(iota((rows, rows), 0) <= iota((rows, rows), 1), 1.0, 0.0).astype(bf16)
    wide = jnp.broadcast_to(mask_ref[...].astype(f32), (16, rows)).astype(bf16)
    rank_ref[...] = mm(wide, tri)[:1].astype(jnp.int32) - 1


def placed_rows(mask_ref, choice_ref, quarter, shape):
    total, slots = shape
    top = choice_ref.shape[1] // 2
    line = iota(shape, 0)
    expert = (line >> 1).astype(f32)
    earlier = jnp.where(iota((slots, slots), 0) < iota((slots, slots), 1), 1.0, 0.0).astype(bf16)
    live = quarter * slots + iota(shape, 1) < jnp.sum(mask_ref[...])
    hit = jnp.zeros(shape, f32)
    weight = jnp.zeros(shape, f32)
    for pick in range(top):
        same = (expert == choice_ref[quarter, pick : pick + 1, :slots]) & live
        hit = hit + jnp.where(same, 1.0, 0.0)
        weight = weight + jnp.where(same, choice_ref[quarter, top + pick : top + pick + 1, :slots], 0.0)
    arrival = mm(hit.astype(bf16), earlier).astype(jnp.int32)
    return (hit > 0.0) & (arrival == (line & 1)), weight


def route_kernel(mask_ref, choice_ref, take_ref, token_ref):
    token_ref[...] = jnp.zeros_like(token_ref)
    for quarter in range(take_ref.shape[0]):
        found, _ = placed_rows(mask_ref, choice_ref, quarter, take_ref.shape[1:])
        take_ref[quarter] = jnp.where(found, 1.0, 0.0).astype(bf16)


def weigh_kernel(mask_ref, choice_ref, token_ref, weigh_ref, done_ref):
    done_ref[...] = token_ref[...]
    for quarter in range(weigh_ref.shape[0]):
        found, weight = placed_rows(mask_ref, choice_ref, quarter, weigh_ref.shape[1:])
        weigh_ref[quarter] = jnp.where(found, weight, 0.0)


def expert_part(coarse_ref, rows_ref, ext_ref, pieces, total, offset):
    width = rows_ref.shape[2]
    count = rows_ref.shape[0] // GROUP
    inner = total.shape[1]
    for ref, step, parts in pieces:
        c = lax.rem(coarse_ref[0] + step, GROUP)

        @pl.when(2 * c < GROUP)
        def _():
            for n, part in enumerate(parts):
                rows = rows_ref[pl.ds((2 * c + part) * count, count)].reshape(total.shape[0], width)
                total[...] += mm(rows, ref[n * width : (n + 1) * width, :inner])

        @pl.when(2 * c >= GROUP)
        def _():
            for n, part in enumerate(parts):
                ext = jnp.broadcast_to(ext_ref[2 * c + part - GROUP].astype(f32), (16, width)).astype(bf16)
                offset[...] += mm(ext, ref[n * width : (n + 1) * width, :inner])


def expert_kernel(
    coarse_ref,
    rows_ref,
    ext_ref,
    own_ref,
    left_ref,
    right_ref,
    upper_ref,
    lower_ref,
    token_ref,
    out_ref,
    total,
    offset,
):
    del token_ref
    width = rows_ref.shape[2]
    count = rows_ref.shape[0] // GROUP
    inner = total.shape[1]
    hidden = inner // 2
    total[...] = jnp.zeros_like(total)
    offset[...] = jnp.zeros_like(offset)
    pieces = [(own_ref, 0, (0, 1)), (left_ref, GROUP - 1, (0, 1)), (right_ref, 1, (0, 1))]
    pieces += [(upper_ref, 2, (0,)), (lower_ref, 2, (1,))]
    expert_part(coarse_ref, rows_ref, ext_ref, pieces, total, offset)
    gate = total[:, :hidden] + offset[:1, :hidden]
    up = total[:, hidden:] + offset[:1, hidden:]
    act = (gate / (1.0 + jnp.exp(-gate)) * up).astype(bf16)

    def put(step, value):
        c = lax.rem(coarse_ref[0] + step, GROUP)
        out_ref[pl.ds(c * count, count)] = value.astype(bf16).reshape(count, *out_ref.shape[1:])

    for ref, step in ((own_ref, 0), (left_ref, GROUP - 1), (right_ref, 1)):
        put(step, mm(act, ref[:, inner:]))
    put(2, mm(act[:, :width], upper_ref[:, inner:]) + mm(act[:, width:], lower_ref[:, inner:]))


def combine_kernel(mask_ref, weigh_ref, back_ref, out_ref, last_ref):
    quarters, _, slots = weigh_ref.shape
    count, width = back_ref.shape[0] // quarters, back_ref.shape[2]
    bounds = jnp.sum(mask_ref[...])
    last = jnp.zeros(last_ref.shape, f32)
    for c in range(quarters):
        wh, wl = split(weigh_ref[c])
        back = back_ref[c * count : (c + 1) * count].reshape(weigh_ref.shape[1], width)
        part = mm(wh, back, ((0,), (0,))) + mm(wl, back, ((0,), (0,)))
        out_ref[c * slots : (c + 1) * slots] = part
        here = c * slots + iota((slots, 1), 0) == bounds - 1
        last = last + jnp.sum(jnp.where(here, part, 0.0), axis=0, keepdims=True)
    last_ref[...] = last


def spread_kernel(hidden_ref, rank_ref, stretch_ref, out_ref, before_ref):
    rows, slots = hidden_ref.shape[0], stretch_ref.shape[0]
    rank = rank_ref[...]
    chosen = jnp.where(iota((slots, rows), 0) == rank, 1.0, 0.0).astype(bf16)
    sh, sl = split(stretch_ref[...])
    spread = mm(chosen, sh, ((0,), (0,))) + mm(chosen, sl, ((0,), (0,)))
    eye = iota((rows, rows), 0) == iota((rows, rows), 1)
    before = jnp.sum(jnp.where(eye & (rank < 0), 1.0, 0.0), axis=1, keepdims=True)
    before_ref[...] = jnp.broadcast_to(before, before_ref.shape)
    out_ref[...] = (hidden_ref[...].astype(f32) + spread).astype(bf16)


def entry_kernel(hidden_ref, mixed_ref, before_ref, prev_ref, out_ref):
    entry = (hidden_ref[...].astype(f32) + prev_ref[...]).astype(bf16)
    out_ref[...] = jnp.where(before_ref[:, :1] > 0.0, entry, mixed_ref[...])


def sds(shape, dtype):
    return jax.ShapeDtypeStruct(shape, dtype)


def call(kernel, outs, args, scalars=0, scratch=(), flops=10**5, megabytes=16, far_in=(), far_out=(), same=None):
    def spec(far, index):
        space = pltpu.SMEM if index < 0 else pltpu.HBM if index in far else pltpu.VMEM
        return pl.BlockSpec(memory_space=space)

    many = isinstance(outs, tuple)
    places = tuple(spec(far_out, i) for i in range(len(outs))) if many else spec(far_out, 0)
    return pl.pallas_call(
        kernel,
        out_shape=outs,
        in_specs=[spec(far_in, i - scalars) for i in range(len(args))],
        out_specs=places,
        scratch_shapes=list(scratch),
        input_output_aliases=same or {},
        compiler_params=pltpu.CompilerParams(vmem_limit_bytes=megabytes * 2**20),
        cost_estimate=pl.CostEstimate(flops=flops, bytes_accessed=flops // 100, transcendentals=0),
    )(*args)


def shards(
    bytes_in,
    norm_gain,
    qkv_weight,
    gate_weight_enc,
    decay_rate,
    write_bias,
    head_gain,
    boundaries,
    picks,
    pick_gates,
    extension,
    expert_gate,
    expert_up,
    expert_down,
):
    x = bytes_in[0]
    rows, width = x.shape
    dim = HALF // 2
    seq = lax.axis_index("seq")
    spot = lax.axis_index("coarse").astype(jnp.int32)[None]
    seq_total = lax.axis_size("seq")
    core = (seq % 2).astype(jnp.int32)[None]
    place = ((seq // 2) % GROUP).astype(jnp.int32)[None]
    local_slots = picks.shape[1]
    slot_total = local_slots * GROUP
    pair_total = local_slots * picks.shape[2]
    everywhere = ("coarse", "seq", "exp")

    def exchange(array, axes, **kwargs):
        return lax.all_to_all(array, axes, split_axis=0, concat_axis=0, tiled=True, **kwargs)

    top = picks.shape[2]
    choice = call(choice_kernel, sds((GROUP, 2 * top, dim), f32), (picks[0].T, pick_gates[0].T), megabytes=63)
    choice = exchange(choice, "coarse")

    depth, hidden_units = expert_gate.shape[1:]
    columns = 2 * hidden_units + expert_down.shape[2]
    gate_rows = gate_weight_enc.transpose(0, 2, 1)
    own, give, local, x_share, weights = call(
        delta_kernel,
        (
            sds((dim, HALF), f32),
            sds((dim, HALF), f32),
            sds((2, rows, HALF), f32),
            sds((rows, HALF), bf16),
            sds((depth, columns), bf16),
        ),
        (
            x,
            norm_gain[None],
            qkv_weight,
            gate_rows,
            decay_rate[None],
            write_bias[None],
            expert_gate,
            expert_up,
            expert_down,
        ),
        scratch=(
            pltpu.VMEM((depth, columns), bf16),
            pltpu.VMEM((rows, width), bf16),
            pltpu.VMEM((1, width), f32),
            pltpu.VMEM(qkv_weight.shape, bf16),
            pltpu.VMEM(gate_rows.shape, bf16),
            pltpu.VMEM((1, 2), f32),
            pltpu.VMEM((1, 2), f32),
            pltpu.VMEM((8, dim, HALF), bf16),
            pltpu.VMEM((8, dim, dim), f32),
            pltpu.SemaphoreType.DMA((10 + PIECES,)),
        ),
        flops=2 * 10**9,
        megabytes=60,
        far_in=range(9),
        far_out=(4,),
    )

    give = call(after_kernel, sds(give.shape, f32), (choice, give), far_in=(0, 1), far_out=(0,), same={1: 0})

    swap = [(i, i ^ 1) for i in range(seq_total)]
    got = lax.ppermute(give, "seq", swap)
    own = call(stage_kernel, sds(own.shape, f32), (own,))
    rank = call(rank_kernel, sds((1, rows), jnp.int32), (boundaries,))
    take, routed = call(
        route_kernel,
        (
            sds((GROUP, pair_total, local_slots), bf16),
            sds((8, dim), f32),
        ),
        (boundaries, choice),
    )
    message, first = call(
        pair_kernel, (sds((GROUP, dim, HALF), bf16), sds((dim, HALF), f32)), (core, own, got), scalars=1
    )
    half = depth // 2
    ring = [(i, (i + 1) % GROUP) for i in range(GROUP)]
    back = [(b, a) for a, b in ring]
    left = lax.ppermute(weights, "coarse", ring)
    right = lax.ppermute(weights, "coarse", back)
    facing = (lax.ppermute(left[:half], "coarse", ring), lax.ppermute(right[half:], "coarse", back))
    stride = 2 * GROUP
    groups = [
        [stride * g + 2 * i + c for i in range(GROUP)] for g in range(seq_total // stride) for c in range(2)
    ]
    chips = exchange(message, "seq", axis_index_groups=groups)
    before, total = call(
        group_kernel, (sds((dim, HALF), f32), sds((dim, HALF), f32)), (place, chips), scalars=1, flops=10**9
    )
    state = jnp.zeros((dim, dim), bf16)
    for hop in range(seq_total // stride - 1):
        if hop == 0:
            outgoing = total[:, dim:].astype(bf16)
        else:
            outgoing = call(hop_kernel, sds((dim, dim), bf16), (total, state, routed), flops=10**9)
        pairs = [(stride * hop + i, stride * (hop + 1) + i) for i in range(stride)]
        state = state + lax.ppermute(outgoing, "seq", pairs)
    states = call(enter_kernel, sds((2, dim, dim), f32), (core, before, first, state), scalars=1, flops=10**9)
    others = lax.ppermute(states, "seq", swap)

    devices = lax.axis_size(everywhere)
    capacity = GROUP * pair_total // devices
    hidden, outgoing, picked = call(
        finish_kernel,
        (sds((rows, HALF), bf16), sds((devices, capacity, HALF), bf16), sds((8, dim), f32)),
        (core, local, states, others, x_share, head_gain[None], boundaries, rank, take, left, right),
        scalars=1,
        far_in=(8, 9),
    )
    received = exchange(outgoing, everywhere)
    weigh, weighed = call(
        weigh_kernel,
        (sds((GROUP, pair_total, local_slots), f32), sds((8, dim), f32)),
        (boundaries, choice, picked),
    )
    value = call(
        expert_kernel,
        sds((devices, capacity, HALF), bf16),
        (spot, received, extension.reshape(width // HALF, 1, HALF), weights, left, right, *facing, weighed),
        scalars=1,
        scratch=(pltpu.VMEM((pair_total, 2 * hidden_units), f32), pltpu.VMEM((16, 2 * hidden_units), f32)),
    )
    returned = exchange(value, everywhere)
    stretch, last = call(
        combine_kernel,
        (sds((slot_total, HALF), f32), sds((1, HALF), f32)),
        (boundaries, weigh, returned),
    )
    previous = lax.ppermute(last, "seq", [(i, i + 1) for i in range(seq_total - 1)])
    mixed, early = call(
        spread_kernel, (sds((rows, HALF), bf16), sds((rows, dim), f32)), (hidden, rank, stretch), flops=10**9
    )
    mixed = call(entry_kernel, sds((rows, HALF), bf16), (hidden, mixed, early, previous))
    return mixed[None]


def solution(mesh):
    placed = (
        P("exp", "seq", None),
        P(),
        P(None, None, "coarse"),
        P(None, None, "coarse"),
        P("coarse"),
        P("coarse"),
        P("coarse"),
        P("exp", "seq"),
        P("exp", ("seq", "coarse"), None),
        P("exp", ("seq", "coarse"), None),
        P(),
        P(("seq", "exp"), "coarse", None),
        P(("seq", "exp"), "coarse", None),
        P(("seq", "exp"), None, "coarse"),
    )
    return jax.shard_map(
        shards, mesh=mesh, in_specs=placed, out_specs=P("exp", "seq", "coarse"), check_vma=False
    )
```

```python
import jax
import jax.numpy as jnp
from jax import lax
from jax.experimental import pallas as pl
from jax.experimental.pallas import tpu as pltpu
from jax.sharding import PartitionSpec as P

f32 = jnp.float32
bf16 = jnp.bfloat16
HALF = 256
GROUP = 4
PIECES = 1


def mm(a, b, dims=((1,), (0,))):
    return lax.dot_general(a, b, (dims, ((), ())), preferred_element_type=f32)


def split(x):
    high = x.astype(bf16)
    return high, (x - high.astype(f32)).astype(bf16)


def mm3(a, b, dims=((1,), (0,))):
    (ah, al), (bh, bl) = a, b
    return mm(ah, bh, dims) + (mm(ah, bl, dims) + mm(al, bh, dims))


def iota(shape, dim):
    return lax.broadcasted_iota(jnp.int32, shape, dim)


def as_row(column):
    size = column.shape[0]
    eye = iota((size, size), 0) == iota((size, size), 1)
    return jnp.sum(jnp.where(eye, column, 0.0), axis=0, keepdims=True)


def choice_kernel(picks_ref, gates_ref, edown_far, out_ref, build, sems):
    top, slots = picks_ref.shape
    depth = edown_far.shape[1]
    moves = [
        pltpu.make_async_copy(edown_far.at[0], out_ref.at[n, pl.ds(0, depth)], sems.at[n]) for n in range(GROUP)
    ]
    for move in moves:
        move.start()
    build[...] = jnp.zeros_like(build)
    gates = gates_ref[...]
    high = gates.astype(bf16).astype(f32)
    half = build.shape[1] // 2
    build[:top, :slots] = picks_ref[...].astype(f32)
    build[:top, half : half + slots] = high
    build[top:, half : half + slots] = gates - high
    for n in range(GROUP):
        out_ref[n, depth:] = build[...].astype(bf16)
    for move in moves:
        move.wait()


def after_kernel(choice_far, give_far, same_far):
    del choice_far, give_far, same_far


def delta_kernel(
    x_far,
    gain_far,
    w_far,
    gw_far,
    rate_far,
    bias_far,
    egate_far,
    eup_far,
    own_ref,
    give_ref,
    local_ref,
    share_ref,
    weights_far,
    weights_ref,
    x_ref,
    gain_ref,
    w_ref,
    gw_ref,
    rate_ref,
    bias_ref,
    low,
    inv,
    sems,
):
    rows = x_ref.shape[0]
    dim = HALF // 2
    pairs = [(gain_far, gain_ref), (gw_far, gw_ref), (rate_far, rate_ref), (bias_far, bias_ref), (w_far, w_ref)]
    start = 0
    for far in (egate_far, eup_far):
        size = far.shape[2]
        pairs.append((far.at[0], weights_ref.at[:, pl.ds(start, size)]))
        start += size
    moves = [pltpu.make_async_copy(a, b, sems.at[n]) for n, (a, b) in enumerate(pairs)]
    size = rows // PIECES
    bytes_in = []
    for n in range(PIECES):
        spot = pl.ds(n * size, size)
        bytes_in.append(pltpu.make_async_copy(x_far.at[spot], x_ref.at[spot], sems.at[10 + n]))
    for move in bytes_in + moves:
        move.start()
    for move in moves[:4]:
        move.wait()
    gain = gain_ref[...]
    parts = []
    for n in range(PIECES):
        bytes_in[n].wait()
        x = x_ref[n * size : (n + 1) * size].astype(f32)
        parts.append((x * lax.rsqrt(jnp.mean(x * x, -1, keepdims=True) + 1e-05) * gain).astype(bf16))
    normed = jnp.concatenate(parts, axis=0)
    first = pl.multiple_of(lax.axis_index("coarse") * HALF, HALF)
    moves.append(pltpu.make_async_copy(x_ref.at[:, pl.ds(first, HALF)], share_ref, sems.at[8]))
    moves[7].start()

    linear = mm(normed, jnp.concatenate([gw_ref[0], gw_ref[1]], axis=0), ((1,), (1,)))
    decay_in, write_in = linear[:, :2], linear[:, 2:]
    write = jax.nn.sigmoid(write_in + bias_ref[...])
    soft = jnp.maximum(decay_in, 0.0) + jnp.log1p(jnp.exp(-jnp.abs(decay_in)))
    log_decay = -rate_ref[...] * soft
    tri = jnp.where(iota((rows, rows), 0) >= iota((rows, rows), 1), 1.0, 0.0).astype(bf16)
    part_h = log_decay.astype(bf16)
    rest = log_decay - part_h.astype(f32)
    part_m = rest.astype(bf16)
    part_l = (rest - part_m.astype(f32)).astype(bf16)
    sums = mm(tri, jnp.concatenate([part_h, part_m, part_l], axis=1))
    cum = sums[:, 0:2] + (sums[:, 2:4] + sums[:, 4:6])

    moves[4].wait()

    def act(index):
        value = mm(normed, w_ref[index])
        return value / (1.0 + jnp.exp(-value))

    q_all, k_all, v_all = act(0), act(1), act(2)
    for move in moves[5:7]:
        move.wait()
    leave = pltpu.make_async_copy(weights_ref, weights_far, sems.at[9])
    leave.start()
    strict = iota((HALF, HALF), 0) > iota((HALF, HALF), 1)
    causal = iota((HALF, HALF), 0) >= iota((HALF, HALF), 1)
    pair = (iota((dim, dim), 0) >> 1) == (iota((dim, dim), 1) >> 1)
    eye = jnp.where(iota((dim, dim), 0) == iota((dim, dim), 1), 1.0, 0.0)
    keep = []
    for head in range(2):
        cols = slice(head * dim, (head + 1) * dim)
        q, k, v = q_all[:, cols], k_all[:, cols], v_all[:, cols]
        q = q * lax.rsqrt(jnp.sum(q * q, -1, keepdims=True) + 1e-06)
        k = k * lax.rsqrt(jnp.sum(k * k, -1, keepdims=True) + 1e-06)
        cum_col = cum[:, head : head + 1]
        cum_row = as_row(cum_col)
        beta = write[:, head : head + 1]
        kh, kl = split(k)
        deep = jnp.concatenate([kh, kl], axis=1)
        twice = jnp.concatenate([kh, kh], axis=1)
        cross = None
        inner = []
        for i, j in ((0, 0), (1, 1), (1, 0)):
            ri, rj = slice(i * HALF, (i + 1) * HALF), slice(j * HALF, (j + 1) * HALF)
            gram = mm(deep[ri], twice[rj], ((1,), (1,))) + mm(kh[ri], kl[rj], ((1,), (1,)))
            lower = beta[ri] * jnp.exp(jnp.minimum(cum_col[ri] - cum_row[:, rj], 0.0)) * gram
            if i == j:
                lower = jnp.where(strict, lower, 0.0)
                for sub in range(2):
                    rs = slice(sub * dim, (sub + 1) * dim)
                    block = 4 * head + 2 * i + sub
                    part = lower[rs, rs]
                    low[block] = jnp.concatenate(split(part), axis=1)
                    inv[block] = eye - jnp.where(pair, part, 0.0)
                inner.append(jnp.concatenate(split(lower[dim:, :dim]), axis=1))
            else:
                cross = split(lower)
        right = jnp.concatenate([(beta * jnp.exp(cum_col)) * k, beta * v], axis=1)
        last = cum_col[rows - 1 : rows]
        (qh, ql) = split(q)
        broad = jnp.concatenate([qh, ql], axis=1)
        attend = {}
        for i, j in ((0, 0), (1, 1), (1, 0)):
            ri, rj = slice(i * HALF, (i + 1) * HALF), slice(j * HALF, (j + 1) * HALF)
            gram = mm(broad[ri], twice[rj], ((1,), (1,))) + mm(qh[ri], kl[rj], ((1,), (1,)))
            gram = gram * jnp.exp(jnp.minimum(cum_col[ri] - cum_row[:, rj], 0.0))
            attend[i, j] = split(jnp.where(causal, gram, 0.0) if i == j else gram)
        grown = jnp.exp(cum_col) * q
        keep.append((cross, inner, right, k * jnp.exp(last - cum_col), jnp.exp(last), attend, grown))

    def packed(left, block):
        wide = jnp.concatenate(split(block), axis=1)
        out = mm(left, jnp.concatenate([wide, wide], axis=0))
        return out[:, :dim] + out[:, dim:]

    def level(step):
        r, c = iota((dim, HALF), 0), iota((dim, HALF), 1) & (dim - 1)
        above = ((r >> (step + 1)) == (c >> (step + 1))) & ((r >> step) > (c >> step))
        zero = jnp.zeros((dim, HALF), bf16)
        blocks = [inv[m] for m in range(8)]
        inside = [packed(jnp.where(above, low[m], zero), blocks[m]) for m in range(8)]
        for m in range(8):
            inv[m] = blocks[m] - packed(jnp.concatenate(split(blocks[m]), axis=1), inside[m])

    for step in range(1, 7):
        level(step)
    for head in range(2):
        cross, inner, right, k_end, scale, attend, grown = keep[head]
        full = []
        for i in range(2):
            top, bottom = inv[4 * head + 2 * i], inv[4 * head + 2 * i + 1]
            corner = packed(jnp.concatenate(split(bottom), axis=1), packed(inner[i], top))
            upper = jnp.concatenate([top, jnp.zeros_like(top)], axis=1)
            full.append(split(jnp.concatenate([upper, jnp.concatenate([-corner, bottom], axis=1)], axis=0)))
        first = mm3(full[0], split(right[:HALF]))
        second = right[HALF:] - mm3(cross, split(first))
        second = mm3(full[1], split(second))
        solved = jnp.concatenate([first, second], axis=0)
        halves = (split(first), split(second))
        for i in range(2):
            ri = slice(i * HALF, (i + 1) * HALF)
            out = mm3(attend[i, i], halves[i])
            if i > 0:
                out = out + mm3(attend[1, 0], halves[0])
            local_ref[head, ri] = jnp.concatenate([grown[ri] - out[:, :dim], out[:, dim:]], axis=1)
        ends = mm3(split(k_end), split(solved), ((0,), (0,)))
        keep[head] = jnp.concatenate([scale * eye - ends[:, :dim], ends[:, dim:]], axis=1)
    lead = lax.rem(lax.axis_index("seq"), 2) == 0
    own_ref[...] = jnp.where(lead, keep[0], keep[1])
    give_ref[...] = jnp.where(lead, keep[1], keep[0])
    moves[7].wait()
    leave.wait()


def compose(late, early):
    dim = late.shape[0]
    both = mm3(split(late[:, :dim]), split(early))
    return jnp.concatenate([both[:, :dim], both[:, dim:] + late[:, dim:]], axis=1)


def stage_kernel(own_ref, out_ref):
    out_ref[...] = own_ref[...]


def pair_kernel(core_ref, own_ref, got_ref, msg_ref, first_ref):
    dim = HALF // 2
    lead = core_ref[0] == 0
    own, got = own_ref[...], got_ref[...]
    early, late = jnp.where(lead, own, got), jnp.where(lead, got, own)
    first_ref[...] = early
    eye = jnp.where(iota((dim, HALF), 0) == iota((dim, HALF), 1), 1.0, 0.0)
    message = (compose(late, early) - eye).astype(bf16)
    for chip in range(GROUP):
        msg_ref[chip] = message


def group_kernel(place_ref, got_ref, before_ref, total_ref):
    dim = HALF // 2
    eye = jnp.where(iota((dim, HALF), 0) == iota((dim, HALF), 1), 1.0, 0.0)
    place = place_ref[0]
    running = eye
    before = eye
    for chip in range(GROUP):
        item = got_ref[chip].astype(f32) + eye
        running = item if chip == 0 else compose(item, running)
        if chip + 1 < GROUP:
            before = jnp.where(place == chip + 1, running, before)
    before_ref[...] = before
    total_ref[...] = running


def hop_kernel(total_ref, state_ref, token_ref, out_ref):
    del token_ref
    dim = HALF // 2
    moved = mm3(split(total_ref[:, :dim]), split(state_ref[...].astype(f32)))
    out_ref[...] = (moved + total_ref[:, dim:]).astype(bf16)


def enter_kernel(core_ref, before_ref, first_ref, state_ref, pair_ref):
    dim = HALF // 2
    state = mm3(split(before_ref[:, :dim]), split(state_ref[...].astype(f32))) + before_ref[:, dim:]
    after = mm3(split(first_ref[:, :dim]), split(state)) + first_ref[:, dim:]
    lead = core_ref[0] == 0
    pair_ref[0] = jnp.where(lead, state, after)
    pair_ref[1] = jnp.where(lead, after, state)


def finish_kernel(
    core_ref,
    local_ref,
    own_ref,
    got_ref,
    x_ref,
    gain_ref,
    mask_ref,
    rank_ref,
    take_ref,
    left_far,
    right_far,
    hidden_ref,
    send_ref,
    token_ref,
):
    token_ref[...] = jnp.zeros_like(token_ref)
    del left_far, right_far
    dim = HALF // 2
    lead = core_ref[0] == 0
    keep, got = own_ref[0], got_ref[1]
    states = (jnp.where(lead, keep, got), jnp.where(lead, got, keep))
    parts = []
    for head in range(2):
        out = local_ref[head, :, dim:] + mm3(split(local_ref[head, :, :dim]), split(states[head]))
        norm = out * lax.rsqrt(jnp.mean(out * out, -1, keepdims=True) + 1e-06)
        parts.append((norm * gain_ref[:, head * dim : (head + 1) * dim]).astype(bf16))
    normed = jnp.concatenate(parts, axis=1)
    hidden = (x_ref[...].astype(f32) + normed.astype(f32)).astype(bf16)
    hidden_ref[...] = hidden
    quarters, _, slots = take_ref.shape
    count = send_ref.shape[0] // quarters
    chosen = (iota((quarters * slots, hidden.shape[0]), 0) == rank_ref[...]) & (mask_ref[...] == 1)
    picked = mm(jnp.where(chosen, 1.0, 0.0).astype(bf16), hidden).astype(bf16)
    for quarter in range(quarters):
        rows = picked[quarter * slots : (quarter + 1) * slots]
        taken = mm(take_ref[quarter], rows).astype(bf16)
        send_ref[quarter * count : (quarter + 1) * count] = taken.reshape(count, *send_ref.shape[1:])


def rank_kernel(mask_ref, rank_ref):
    rows = mask_ref.shape[1]
    tri = jnp.where(iota((rows, rows), 0) <= iota((rows, rows), 1), 1.0, 0.0).astype(bf16)
    wide = jnp.broadcast_to(mask_ref[...].astype(f32), (16, rows)).astype(bf16)
    rank_ref[...] = mm(wide, tri)[:1].astype(jnp.int32) - 1


def fetch(shared_far, table, sem):
    depth = shared_far.shape[1] - table.shape[1]
    move = pltpu.make_async_copy(shared_far.at[:, pl.ds(depth, table.shape[1])], table, sem)
    move.start()
    move.wait()


def placed_rows(mask_ref, choice_ref, quarter, shape):
    total, slots = shape
    top = choice_ref.shape[1] // 2
    line = iota(shape, 0)
    expert = (line >> 1).astype(f32)
    earlier = jnp.where(iota((slots, slots), 0) < iota((slots, slots), 1), 1.0, 0.0).astype(bf16)
    live = quarter * slots + iota(shape, 1) < jnp.sum(mask_ref[...])
    hit = jnp.zeros(shape, f32)
    weight = jnp.zeros(shape, f32)
    table = choice_ref[quarter].astype(f32)
    half = table.shape[1] // 2
    names = table[:top, :slots]
    gates = table[:top, half : half + slots] + table[top:, half : half + slots]
    for pick in range(top):
        same = (expert == names[pick : pick + 1]) & live
        hit = hit + jnp.where(same, 1.0, 0.0)
        weight = weight + jnp.where(same, gates[pick : pick + 1], 0.0)
    arrival = mm(hit.astype(bf16), earlier).astype(jnp.int32)
    return (hit > 0.0) & (arrival == (line & 1)), weight


def route_kernel(mask_ref, shared_far, take_ref, token_ref, choice_ref, sem):
    fetch(shared_far, choice_ref, sem)
    token_ref[...] = jnp.zeros_like(token_ref)
    for quarter in range(take_ref.shape[0]):
        found, _ = placed_rows(mask_ref, choice_ref, quarter, take_ref.shape[1:])
        take_ref[quarter] = jnp.where(found, 1.0, 0.0).astype(bf16)


def weigh_kernel(mask_ref, shared_far, token_ref, weigh_ref, done_ref, choice_ref, sem):
    fetch(shared_far, choice_ref, sem)
    done_ref[...] = token_ref[...]
    for quarter in range(weigh_ref.shape[0]):
        found, weight = placed_rows(mask_ref, choice_ref, quarter, weigh_ref.shape[1:])
        weigh_ref[quarter] = jnp.where(found, weight, 0.0)


def expert_part(coarse_ref, rows_ref, ext_ref, pieces, total, offset):
    width = rows_ref.shape[2]
    count = rows_ref.shape[0] // GROUP
    inner = total.shape[1]
    for ref, step, parts in pieces:
        c = lax.rem(coarse_ref[0] + step, GROUP)

        @pl.when(2 * c < GROUP)
        def _():
            for n, part in enumerate(parts):
                rows = rows_ref[pl.ds((2 * c + part) * count, count)].reshape(total.shape[0], width)
                total[...] += mm(rows, ref[n * width : (n + 1) * width, :inner])

        @pl.when(2 * c >= GROUP)
        def _():
            for n, part in enumerate(parts):
                ext = jnp.broadcast_to(ext_ref[2 * c + part - GROUP].astype(f32), (16, width)).astype(bf16)
                offset[...] += mm(ext, ref[n * width : (n + 1) * width, :inner])


def expert_kernel(
    coarse_ref,
    rows_ref,
    ext_ref,
    own_ref,
    left_ref,
    right_ref,
    upper_ref,
    lower_ref,
    down_ref,
    token_ref,
    out_ref,
    total,
    offset,
):
    del token_ref
    width = rows_ref.shape[2]
    count = rows_ref.shape[0] // GROUP
    inner = total.shape[1]
    hidden = inner // 2
    total[...] = jnp.zeros_like(total)
    offset[...] = jnp.zeros_like(offset)
    pieces = [(own_ref, 0, (0, 1)), (left_ref, GROUP - 1, (0, 1)), (right_ref, 1, (0, 1))]
    pieces += [(upper_ref, 2, (0,)), (lower_ref, 2, (1,))]
    expert_part(coarse_ref, rows_ref, ext_ref, pieces, total, offset)
    gate = total[:, :hidden] + offset[:1, :hidden]
    up = total[:, hidden:] + offset[:1, hidden:]
    act = (gate / (1.0 + jnp.exp(-gate)) * up).astype(bf16)

    for c in range(GROUP):
        value = mm(act, down_ref[c, :hidden]).astype(bf16)
        out_ref[c * count : (c + 1) * count] = value.reshape(count, *out_ref.shape[1:])


def combine_kernel(mask_ref, weigh_ref, back_ref, out_ref, last_ref):
    quarters, _, slots = weigh_ref.shape
    count, width = back_ref.shape[0] // quarters, back_ref.shape[2]
    bounds = jnp.sum(mask_ref[...])
    last = jnp.zeros(last_ref.shape, f32)
    for c in range(quarters):
        wh, wl = split(weigh_ref[c])
        back = back_ref[c * count : (c + 1) * count].reshape(weigh_ref.shape[1], width)
        part = mm(wh, back, ((0,), (0,))) + mm(wl, back, ((0,), (0,)))
        out_ref[c * slots : (c + 1) * slots] = part
        here = c * slots + iota((slots, 1), 0) == bounds - 1
        last = last + jnp.sum(jnp.where(here, part, 0.0), axis=0, keepdims=True)
    last_ref[...] = last


def spread_kernel(hidden_ref, rank_ref, stretch_ref, out_ref, before_ref):
    rows, slots = hidden_ref.shape[0], stretch_ref.shape[0]
    rank = rank_ref[...]
    chosen = jnp.where(iota((slots, rows), 0) == rank, 1.0, 0.0).astype(bf16)
    sh, sl = split(stretch_ref[...])
    spread = mm(chosen, sh, ((0,), (0,))) + mm(chosen, sl, ((0,), (0,)))
    eye = iota((rows, rows), 0) == iota((rows, rows), 1)
    before = jnp.sum(jnp.where(eye & (rank < 0), 1.0, 0.0), axis=1, keepdims=True)
    before_ref[...] = jnp.broadcast_to(before, before_ref.shape)
    out_ref[...] = (hidden_ref[...].astype(f32) + spread).astype(bf16)


def entry_kernel(hidden_ref, mixed_ref, before_ref, prev_ref, out_ref):
    entry = (hidden_ref[...].astype(f32) + prev_ref[...]).astype(bf16)
    out_ref[...] = jnp.where(before_ref[:, :1] > 0.0, entry, mixed_ref[...])


def sds(shape, dtype):
    return jax.ShapeDtypeStruct(shape, dtype)


def call(kernel, outs, args, scalars=0, scratch=(), flops=10**5, megabytes=16, far_in=(), far_out=(), same=None):
    def spec(far, index):
        space = pltpu.SMEM if index < 0 else pltpu.HBM if index in far else pltpu.VMEM
        return pl.BlockSpec(memory_space=space)

    many = isinstance(outs, tuple)
    places = tuple(spec(far_out, i) for i in range(len(outs))) if many else spec(far_out, 0)
    return pl.pallas_call(
        kernel,
        out_shape=outs,
        in_specs=[spec(far_in, i - scalars) for i in range(len(args))],
        out_specs=places,
        scratch_shapes=list(scratch),
        input_output_aliases=same or {},
        compiler_params=pltpu.CompilerParams(vmem_limit_bytes=megabytes * 2**20),
        cost_estimate=pl.CostEstimate(flops=flops, bytes_accessed=flops // 100, transcendentals=0),
    )(*args)


def shards(
    bytes_in,
    norm_gain,
    qkv_weight,
    gate_weight_enc,
    decay_rate,
    write_bias,
    head_gain,
    boundaries,
    picks,
    pick_gates,
    extension,
    expert_gate,
    expert_up,
    expert_down,
):
    x = bytes_in[0]
    rows, width = x.shape
    dim = HALF // 2
    seq = lax.axis_index("seq")
    spot = lax.axis_index("coarse").astype(jnp.int32)[None]
    seq_total = lax.axis_size("seq")
    core = (seq % 2).astype(jnp.int32)[None]
    place = ((seq // 2) % GROUP).astype(jnp.int32)[None]
    local_slots = picks.shape[1]
    slot_total = local_slots * GROUP
    pair_total = local_slots * picks.shape[2]
    everywhere = ("coarse", "seq", "exp")

    def exchange(array, axes, **kwargs):
        return lax.all_to_all(array, axes, split_axis=0, concat_axis=0, tiled=True, **kwargs)

    top = picks.shape[2]
    shared = call(
        choice_kernel,
        sds((GROUP, expert_down.shape[1] + 2 * top, HALF), bf16),
        (picks[0].T, pick_gates[0].T, expert_down),
        scratch=(pltpu.VMEM((2 * top, HALF), f32), pltpu.SemaphoreType.DMA((GROUP,))),
        megabytes=63,
        far_in=(2,),
    )
    shared = exchange(shared, "coarse")
    table = (pltpu.VMEM((GROUP, 2 * top, HALF), bf16), pltpu.SemaphoreType.DMA)

    depth, hidden_units = expert_gate.shape[1:]
    columns = 2 * hidden_units
    gate_rows = gate_weight_enc.transpose(0, 2, 1)
    own, give, local, x_share, weights = call(
        delta_kernel,
        (
            sds((dim, HALF), f32),
            sds((dim, HALF), f32),
            sds((2, rows, HALF), f32),
            sds((rows, HALF), bf16),
            sds((depth, columns), bf16),
        ),
        (
            x,
            norm_gain[None],
            qkv_weight,
            gate_rows,
            decay_rate[None],
            write_bias[None],
            expert_gate,
            expert_up,
        ),
        scratch=(
            pltpu.VMEM((depth, columns), bf16),
            pltpu.VMEM((rows, width), bf16),
            pltpu.VMEM((1, width), f32),
            pltpu.VMEM(qkv_weight.shape, bf16),
            pltpu.VMEM(gate_rows.shape, bf16),
            pltpu.VMEM((1, 2), f32),
            pltpu.VMEM((1, 2), f32),
            pltpu.VMEM((8, dim, HALF), bf16),
            pltpu.VMEM((8, dim, dim), f32),
            pltpu.SemaphoreType.DMA((10 + PIECES,)),
        ),
        flops=2 * 10**9,
        megabytes=60,
        far_in=range(8),
        far_out=(4,),
    )

    give = call(after_kernel, sds(give.shape, f32), (shared, give), far_in=(0, 1), far_out=(0,), same={1: 0})

    swap = [(i, i ^ 1) for i in range(seq_total)]
    got = lax.ppermute(give, "seq", swap)
    own = call(stage_kernel, sds(own.shape, f32), (own,))
    rank = call(rank_kernel, sds((1, rows), jnp.int32), (boundaries,))
    take, routed = call(
        route_kernel,
        (
            sds((GROUP, pair_total, local_slots), bf16),
            sds((8, dim), f32),
        ),
        (boundaries, shared),
        scratch=table,
        far_in=(1,),
    )
    message, first = call(
        pair_kernel, (sds((GROUP, dim, HALF), bf16), sds((dim, HALF), f32)), (core, own, got), scalars=1
    )
    half = depth // 2
    ring = [(i, (i + 1) % GROUP) for i in range(GROUP)]
    back = [(b, a) for a, b in ring]
    left = lax.ppermute(weights, "coarse", ring)
    right = lax.ppermute(weights, "coarse", back)
    facing = (lax.ppermute(left[:half], "coarse", ring), lax.ppermute(right[half:], "coarse", back))
    stride = 2 * GROUP
    groups = [
        [stride * g + 2 * i + c for i in range(GROUP)] for g in range(seq_total // stride) for c in range(2)
    ]
    chips = exchange(message, "seq", axis_index_groups=groups)
    before, total = call(
        group_kernel, (sds((dim, HALF), f32), sds((dim, HALF), f32)), (place, chips), scalars=1, flops=10**9
    )
    state = jnp.zeros((dim, dim), bf16)
    for hop in range(seq_total // stride - 1):
        if hop == 0:
            outgoing = total[:, dim:].astype(bf16)
        else:
            outgoing = call(hop_kernel, sds((dim, dim), bf16), (total, state, routed), flops=10**9)
        pairs = [(stride * hop + i, stride * (hop + 1) + i) for i in range(stride)]
        state = state + lax.ppermute(outgoing, "seq", pairs)
    states = call(enter_kernel, sds((2, dim, dim), f32), (core, before, first, state), scalars=1, flops=10**9)
    others = lax.ppermute(states, "seq", swap)

    devices = lax.axis_size(everywhere)
    capacity = GROUP * pair_total // devices
    hidden, outgoing, picked = call(
        finish_kernel,
        (sds((rows, HALF), bf16), sds((devices, capacity, HALF), bf16), sds((8, dim), f32)),
        (core, local, states, others, x_share, head_gain[None], boundaries, rank, take, left, right),
        scalars=1,
        far_in=(8, 9),
    )
    received = exchange(outgoing, everywhere)
    weigh, weighed = call(
        weigh_kernel,
        (sds((GROUP, pair_total, local_slots), f32), sds((8, dim), f32)),
        (boundaries, shared, picked),
        scratch=table,
        far_in=(1,),
    )
    value = call(
        expert_kernel,
        sds((devices, capacity, HALF), bf16),
        (spot, received, extension.reshape(width // HALF, 1, HALF), weights, left, right, *facing, shared, weighed),
        scalars=1,
        scratch=(pltpu.VMEM((pair_total, 2 * hidden_units), f32), pltpu.VMEM((16, 2 * hidden_units), f32)),
    )
    returned = exchange(value, everywhere)
    stretch, last = call(
        combine_kernel,
        (sds((slot_total, HALF), f32), sds((1, HALF), f32)),
        (boundaries, weigh, returned),
    )
    previous = lax.ppermute(last, "seq", [(i, i + 1) for i in range(seq_total - 1)])
    mixed, early = call(
        spread_kernel, (sds((rows, HALF), bf16), sds((rows, dim), f32)), (hidden, rank, stretch), flops=10**9
    )
    mixed = call(entry_kernel, sds((rows, HALF), bf16), (hidden, mixed, early, previous))
    return mixed[None]


def solution(mesh):
    placed = (
        P("exp", "seq", None),
        P(),
        P(None, None, "coarse"),
        P(None, None, "coarse"),
        P("coarse"),
        P("coarse"),
        P("coarse"),
        P("exp", "seq"),
        P("exp", ("seq", "coarse"), None),
        P("exp", ("seq", "coarse"), None),
        P(),
        P(("seq", "exp"), "coarse", None),
        P(("seq", "exp"), "coarse", None),
        P(("seq", "exp"), None, "coarse"),
    )
    return jax.shard_map(
        shards, mesh=mesh, in_specs=placed, out_specs=P("exp", "seq", "coarse"), check_vma=False
    )
```

```python
import jax
import jax.numpy as jnp
from jax import lax
from jax.experimental import pallas as pl
from jax.experimental.pallas import tpu as pltpu
from jax.sharding import PartitionSpec as P

f32 = jnp.float32
bf16 = jnp.bfloat16
HALF = 256
GROUP = 4
PIECES = 1


def mm(a, b, dims=((1,), (0,))):
    return lax.dot_general(a, b, (dims, ((), ())), preferred_element_type=f32)


def split(x):
    high = x.astype(bf16)
    return high, (x - high.astype(f32)).astype(bf16)


def mm3(a, b, dims=((1,), (0,))):
    (ah, al), (bh, bl) = a, b
    return mm(ah, bh, dims) + (mm(ah, bl, dims) + mm(al, bh, dims))


def iota(shape, dim):
    return lax.broadcasted_iota(jnp.int32, shape, dim)


def as_row(column):
    size = column.shape[0]
    eye = iota((size, size), 0) == iota((size, size), 1)
    return jnp.sum(jnp.where(eye, column, 0.0), axis=0, keepdims=True)


def choice_kernel(picks_ref, gates_ref, edown_far, out_far, build, tile, sems):
    top, slots = picks_ref.shape
    depth = edown_far.shape[1]
    arrive = pltpu.make_async_copy(edown_far.at[0], tile.at[pl.ds(0, depth)], sems.at[GROUP])
    arrive.start()
    build[...] = jnp.zeros_like(build)
    gates = gates_ref[...]
    high = gates.astype(bf16).astype(f32)
    half = build.shape[1] // 2
    build[:top, :slots] = picks_ref[...].astype(f32)
    build[:top, half : half + slots] = high
    build[top:, half : half + slots] = gates - high
    tile[depth:] = build[...].astype(bf16)
    arrive.wait()
    moves = [pltpu.make_async_copy(tile, out_far.at[n], sems.at[n]) for n in range(GROUP)]
    for move in moves:
        move.start()
    for move in moves:
        move.wait()


def after_kernel(choice_far, give_far, same_far):
    del choice_far, give_far, same_far


def delta_kernel(
    x_far,
    gain_far,
    w_far,
    gw_far,
    rate_far,
    bias_far,
    egate_far,
    eup_far,
    own_ref,
    give_ref,
    local_ref,
    share_ref,
    weights_far,
    weights_ref,
    x_ref,
    gain_ref,
    w_ref,
    gw_ref,
    rate_ref,
    bias_ref,
    low,
    inv,
    sems,
):
    rows = x_ref.shape[0]
    dim = HALF // 2
    pairs = [(gain_far, gain_ref), (gw_far, gw_ref), (rate_far, rate_ref), (bias_far, bias_ref), (w_far, w_ref)]
    start = 0
    for far in (egate_far, eup_far):
        size = far.shape[2]
        pairs.append((far.at[0], weights_ref.at[:, pl.ds(start, size)]))
        start += size
    moves = [pltpu.make_async_copy(a, b, sems.at[n]) for n, (a, b) in enumerate(pairs)]
    size = rows // PIECES
    bytes_in = []
    for n in range(PIECES):
        spot = pl.ds(n * size, size)
        bytes_in.append(pltpu.make_async_copy(x_far.at[spot], x_ref.at[spot], sems.at[10 + n]))
    for move in bytes_in + moves:
        move.start()
    for move in moves[:4]:
        move.wait()
    gain = gain_ref[...]
    parts = []
    for n in range(PIECES):
        bytes_in[n].wait()
        x = x_ref[n * size : (n + 1) * size].astype(f32)
        parts.append((x * lax.rsqrt(jnp.mean(x * x, -1, keepdims=True) + 1e-05) * gain).astype(bf16))
    normed = jnp.concatenate(parts, axis=0)
    first = pl.multiple_of(lax.axis_index("coarse") * HALF, HALF)
    moves.append(pltpu.make_async_copy(x_ref.at[:, pl.ds(first, HALF)], share_ref, sems.at[8]))
    moves[7].start()

    linear = mm(normed, jnp.concatenate([gw_ref[0], gw_ref[1]], axis=0), ((1,), (1,)))
    decay_in, write_in = linear[:, :2], linear[:, 2:]
    write = jax.nn.sigmoid(write_in + bias_ref[...])
    soft = jnp.maximum(decay_in, 0.0) + jnp.log1p(jnp.exp(-jnp.abs(decay_in)))
    log_decay = -rate_ref[...] * soft
    tri = jnp.where(iota((rows, rows), 0) >= iota((rows, rows), 1), 1.0, 0.0).astype(bf16)
    part_h = log_decay.astype(bf16)
    rest = log_decay - part_h.astype(f32)
    part_m = rest.astype(bf16)
    part_l = (rest - part_m.astype(f32)).astype(bf16)
    sums = mm(tri, jnp.concatenate([part_h, part_m, part_l], axis=1))
    cum = sums[:, 0:2] + (sums[:, 2:4] + sums[:, 4:6])

    moves[4].wait()

    def act(index):
        value = mm(normed, w_ref[index])
        return value / (1.0 + jnp.exp(-value))

    q_all, k_all, v_all = act(0), act(1), act(2)
    for move in moves[5:7]:
        move.wait()
    leave = pltpu.make_async_copy(weights_ref, weights_far, sems.at[9])
    leave.start()
    strict = iota((HALF, HALF), 0) > iota((HALF, HALF), 1)
    causal = iota((HALF, HALF), 0) >= iota((HALF, HALF), 1)
    pair = (iota((dim, dim), 0) >> 1) == (iota((dim, dim), 1) >> 1)
    eye = jnp.where(iota((dim, dim), 0) == iota((dim, dim), 1), 1.0, 0.0)
    keep = []
    for head in range(2):
        cols = slice(head * dim, (head + 1) * dim)
        q, k, v = q_all[:, cols], k_all[:, cols], v_all[:, cols]
        q = q * lax.rsqrt(jnp.sum(q * q, -1, keepdims=True) + 1e-06)
        k = k * lax.rsqrt(jnp.sum(k * k, -1, keepdims=True) + 1e-06)
        cum_col = cum[:, head : head + 1]
        cum_row = as_row(cum_col)
        beta = write[:, head : head + 1]
        kh, kl = split(k)
        deep = jnp.concatenate([kh, kl], axis=1)
        twice = jnp.concatenate([kh, kh], axis=1)
        cross = None
        inner = []
        for i, j in ((0, 0), (1, 1), (1, 0)):
            ri, rj = slice(i * HALF, (i + 1) * HALF), slice(j * HALF, (j + 1) * HALF)
            gram = mm(deep[ri], twice[rj], ((1,), (1,))) + mm(kh[ri], kl[rj], ((1,), (1,)))
            lower = beta[ri] * jnp.exp(jnp.minimum(cum_col[ri] - cum_row[:, rj], 0.0)) * gram
            if i == j:
                lower = jnp.where(strict, lower, 0.0)
                for sub in range(2):
                    rs = slice(sub * dim, (sub + 1) * dim)
                    block = 4 * head + 2 * i + sub
                    part = lower[rs, rs]
                    low[block] = jnp.concatenate(split(part), axis=1)
                    inv[block] = eye - jnp.where(pair, part, 0.0)
                inner.append(jnp.concatenate(split(lower[dim:, :dim]), axis=1))
            else:
                cross = split(lower)
        right = jnp.concatenate([(beta * jnp.exp(cum_col)) * k, beta * v], axis=1)
        last = cum_col[rows - 1 : rows]
        (qh, ql) = split(q)
        broad = jnp.concatenate([qh, ql], axis=1)
        attend = {}
        for i, j in ((0, 0), (1, 1), (1, 0)):
            ri, rj = slice(i * HALF, (i + 1) * HALF), slice(j * HALF, (j + 1) * HALF)
            gram = mm(broad[ri], twice[rj], ((1,), (1,))) + mm(qh[ri], kl[rj], ((1,), (1,)))
            gram = gram * jnp.exp(jnp.minimum(cum_col[ri] - cum_row[:, rj], 0.0))
            attend[i, j] = split(jnp.where(causal, gram, 0.0) if i == j else gram)
        grown = jnp.exp(cum_col) * q
        keep.append((cross, inner, right, k * jnp.exp(last - cum_col), jnp.exp(last), attend, grown))

    def packed(left, block):
        wide = jnp.concatenate(split(block), axis=1)
        out = mm(left, jnp.concatenate([wide, wide], axis=0))
        return out[:, :dim] + out[:, dim:]

    def level(step):
        r, c = iota((dim, HALF), 0), iota((dim, HALF), 1) & (dim - 1)
        above = ((r >> (step + 1)) == (c >> (step + 1))) & ((r >> step) > (c >> step))
        zero = jnp.zeros((dim, HALF), bf16)
        blocks = [inv[m] for m in range(8)]
        inside = [packed(jnp.where(above, low[m], zero), blocks[m]) for m in range(8)]
        for m in range(8):
            inv[m] = blocks[m] - packed(jnp.concatenate(split(blocks[m]), axis=1), inside[m])

    for step in range(1, 7):
        level(step)
    for head in range(2):
        cross, inner, right, k_end, scale, attend, grown = keep[head]
        full = []
        for i in range(2):
            top, bottom = inv[4 * head + 2 * i], inv[4 * head + 2 * i + 1]
            corner = packed(jnp.concatenate(split(bottom), axis=1), packed(inner[i], top))
            upper = jnp.concatenate([top, jnp.zeros_like(top)], axis=1)
            full.append(split(jnp.concatenate([upper, jnp.concatenate([-corner, bottom], axis=1)], axis=0)))
        first = mm3(full[0], split(right[:HALF]))
        second = right[HALF:] - mm3(cross, split(first))
        second = mm3(full[1], split(second))
        solved = jnp.concatenate([first, second], axis=0)
        halves = (split(first), split(second))
        for i in range(2):
            ri = slice(i * HALF, (i + 1) * HALF)
            out = mm3(attend[i, i], halves[i])
            if i > 0:
                out = out + mm3(attend[1, 0], halves[0])
            local_ref[head, ri] = jnp.concatenate([grown[ri] - out[:, :dim], out[:, dim:]], axis=1)
        ends = mm3(split(k_end), split(solved), ((0,), (0,)))
        keep[head] = jnp.concatenate([scale * eye - ends[:, :dim], ends[:, dim:]], axis=1)
    lead = lax.rem(lax.axis_index("seq"), 2) == 0
    own_ref[...] = jnp.where(lead, keep[0], keep[1])
    give_ref[...] = jnp.where(lead, keep[1], keep[0])
    moves[7].wait()
    leave.wait()


def compose(late, early):
    dim = late.shape[0]
    both = mm3(split(late[:, :dim]), split(early))
    return jnp.concatenate([both[:, :dim], both[:, dim:] + late[:, dim:]], axis=1)


def stage_kernel(own_ref, out_ref):
    out_ref[...] = own_ref[...]


def pair_kernel(core_ref, own_ref, got_ref, msg_ref, first_ref):
    dim = HALF // 2
    lead = core_ref[0] == 0
    own, got = own_ref[...], got_ref[...]
    early, late = jnp.where(lead, own, got), jnp.where(lead, got, own)
    first_ref[...] = early
    eye = jnp.where(iota((dim, HALF), 0) == iota((dim, HALF), 1), 1.0, 0.0)
    message = (compose(late, early) - eye).astype(bf16)
    for chip in range(GROUP):
        msg_ref[chip] = message


def group_kernel(place_ref, got_ref, before_ref, total_ref):
    dim = HALF // 2
    eye = jnp.where(iota((dim, HALF), 0) == iota((dim, HALF), 1), 1.0, 0.0)
    place = place_ref[0]
    running = eye
    before = eye
    for chip in range(GROUP):
        item = got_ref[chip].astype(f32) + eye
        running = item if chip == 0 else compose(item, running)
        if chip + 1 < GROUP:
            before = jnp.where(place == chip + 1, running, before)
    before_ref[...] = before
    total_ref[...] = running


def hop_kernel(total_ref, state_ref, token_ref, out_ref):
    del token_ref
    dim = HALF // 2
    moved = mm3(split(total_ref[:, :dim]), split(state_ref[...].astype(f32)))
    out_ref[...] = (moved + total_ref[:, dim:]).astype(bf16)


def enter_kernel(core_ref, before_ref, first_ref, state_ref, pair_ref):
    dim = HALF // 2
    state = mm3(split(before_ref[:, :dim]), split(state_ref[...].astype(f32))) + before_ref[:, dim:]
    after = mm3(split(first_ref[:, :dim]), split(state)) + first_ref[:, dim:]
    lead = core_ref[0] == 0
    pair_ref[0] = jnp.where(lead, state, after)
    pair_ref[1] = jnp.where(lead, after, state)


def finish_kernel(
    core_ref,
    local_ref,
    own_ref,
    got_ref,
    x_ref,
    gain_ref,
    mask_ref,
    rank_ref,
    take_ref,
    left_far,
    right_far,
    hidden_ref,
    send_ref,
    token_ref,
):
    token_ref[...] = jnp.zeros_like(token_ref)
    del left_far, right_far
    dim = HALF // 2
    lead = core_ref[0] == 0
    keep, got = own_ref[0], got_ref[1]
    states = (jnp.where(lead, keep, got), jnp.where(lead, got, keep))
    parts = []
    for head in range(2):
        out = local_ref[head, :, dim:] + mm3(split(local_ref[head, :, :dim]), split(states[head]))
        norm = out * lax.rsqrt(jnp.mean(out * out, -1, keepdims=True) + 1e-06)
        parts.append((norm * gain_ref[:, head * dim : (head + 1) * dim]).astype(bf16))
    normed = jnp.concatenate(parts, axis=1)
    hidden = (x_ref[...].astype(f32) + normed.astype(f32)).astype(bf16)
    hidden_ref[...] = hidden
    quarters, _, slots = take_ref.shape
    count = send_ref.shape[0] // quarters
    chosen = (iota((quarters * slots, hidden.shape[0]), 0) == rank_ref[...]) & (mask_ref[...] == 1)
    picked = mm(jnp.where(chosen, 1.0, 0.0).astype(bf16), hidden).astype(bf16)
    for quarter in range(quarters):
        rows = picked[quarter * slots : (quarter + 1) * slots]
        taken = mm(take_ref[quarter], rows).astype(bf16)
        send_ref[quarter * count : (quarter + 1) * count] = taken.reshape(count, *send_ref.shape[1:])


def rank_kernel(mask_ref, rank_ref):
    rows = mask_ref.shape[1]
    tri = jnp.where(iota((rows, rows), 0) <= iota((rows, rows), 1), 1.0, 0.0).astype(bf16)
    wide = jnp.broadcast_to(mask_ref[...].astype(f32), (16, rows)).astype(bf16)
    rank_ref[...] = mm(wide, tri)[:1].astype(jnp.int32) - 1


def fetch(shared_far, table, sem):
    depth = shared_far.shape[1] - table.shape[1]
    move = pltpu.make_async_copy(shared_far.at[:, pl.ds(depth, table.shape[1])], table, sem)
    move.start()
    move.wait()


def placed_rows(mask_ref, choice_ref, quarter, shape):
    total, slots = shape
    top = choice_ref.shape[1] // 2
    line = iota(shape, 0)
    expert = (line >> 1).astype(f32)
    earlier = jnp.where(iota((slots, slots), 0) < iota((slots, slots), 1), 1.0, 0.0).astype(bf16)
    live = quarter * slots + iota(shape, 1) < jnp.sum(mask_ref[...])
    hit = jnp.zeros(shape, f32)
    weight = jnp.zeros(shape, f32)
    table = choice_ref[quarter].astype(f32)
    half = table.shape[1] // 2
    names = table[:top, :slots]
    gates = table[:top, half : half + slots] + table[top:, half : half + slots]
    for pick in range(top):
        same = (expert == names[pick : pick + 1]) & live
        hit = hit + jnp.where(same, 1.0, 0.0)
        weight = weight + jnp.where(same, gates[pick : pick + 1], 0.0)
    arrival = mm(hit.astype(bf16), earlier).astype(jnp.int32)
    return (hit > 0.0) & (arrival == (line & 1)), weight


def route_kernel(mask_ref, shared_far, take_ref, token_ref, choice_ref, sem):
    fetch(shared_far, choice_ref, sem)
    token_ref[...] = jnp.zeros_like(token_ref)
    for quarter in range(take_ref.shape[0]):
        found, _ = placed_rows(mask_ref, choice_ref, quarter, take_ref.shape[1:])
        take_ref[quarter] = jnp.where(found, 1.0, 0.0).astype(bf16)


def weigh_kernel(mask_ref, shared_far, token_ref, weigh_ref, done_ref, choice_ref, sem):
    fetch(shared_far, choice_ref, sem)
    done_ref[...] = token_ref[...]
    for quarter in range(weigh_ref.shape[0]):
        found, weight = placed_rows(mask_ref, choice_ref, quarter, weigh_ref.shape[1:])
        weigh_ref[quarter] = jnp.where(found, weight, 0.0)


def expert_part(coarse_ref, rows_ref, ext_ref, pieces, total, offset):
    width = rows_ref.shape[2]
    count = rows_ref.shape[0] // GROUP
    inner = total.shape[1]
    for ref, step, parts in pieces:
        c = lax.rem(coarse_ref[0] + step, GROUP)

        @pl.when(2 * c < GROUP)
        def _():
            for n, part in enumerate(parts):
                rows = rows_ref[pl.ds((2 * c + part) * count, count)].reshape(total.shape[0], width)
                total[...] += mm(rows, ref[n * width : (n + 1) * width, :inner])

        @pl.when(2 * c >= GROUP)
        def _():
            for n, part in enumerate(parts):
                ext = jnp.broadcast_to(ext_ref[2 * c + part - GROUP].astype(f32), (16, width)).astype(bf16)
                offset[...] += mm(ext, ref[n * width : (n + 1) * width, :inner])


def expert_kernel(
    coarse_ref,
    rows_ref,
    ext_ref,
    own_ref,
    left_ref,
    right_ref,
    upper_ref,
    lower_ref,
    down_ref,
    token_ref,
    out_ref,
    total,
    offset,
):
    del token_ref
    width = rows_ref.shape[2]
    count = rows_ref.shape[0] // GROUP
    inner = total.shape[1]
    hidden = inner // 2
    total[...] = jnp.zeros_like(total)
    offset[...] = jnp.zeros_like(offset)
    pieces = [(own_ref, 0, (0, 1)), (left_ref, GROUP - 1, (0, 1)), (right_ref, 1, (0, 1))]
    pieces += [(upper_ref, 2, (0,)), (lower_ref, 2, (1,))]
    expert_part(coarse_ref, rows_ref, ext_ref, pieces, total, offset)
    gate = total[:, :hidden] + offset[:1, :hidden]
    up = total[:, hidden:] + offset[:1, hidden:]
    act = (gate / (1.0 + jnp.exp(-gate)) * up).astype(bf16)

    for c in range(GROUP):
        value = mm(act, down_ref[c, :hidden]).astype(bf16)
        out_ref[c * count : (c + 1) * count] = value.reshape(count, *out_ref.shape[1:])


def combine_kernel(mask_ref, weigh_ref, back_ref, out_ref, last_ref):
    quarters, _, slots = weigh_ref.shape
    count, width = back_ref.shape[0] // quarters, back_ref.shape[2]
    bounds = jnp.sum(mask_ref[...])
    last = jnp.zeros(last_ref.shape, f32)
    for c in range(quarters):
        wh, wl = split(weigh_ref[c])
        back = back_ref[c * count : (c + 1) * count].reshape(weigh_ref.shape[1], width)
        part = mm(wh, back, ((0,), (0,))) + mm(wl, back, ((0,), (0,)))
        out_ref[c * slots : (c + 1) * slots] = part
        here = c * slots + iota((slots, 1), 0) == bounds - 1
        last = last + jnp.sum(jnp.where(here, part, 0.0), axis=0, keepdims=True)
    last_ref[...] = last


def spread_kernel(hidden_ref, rank_ref, stretch_ref, out_ref, before_ref):
    rows, slots = hidden_ref.shape[0], stretch_ref.shape[0]
    rank = rank_ref[...]
    chosen = jnp.where(iota((slots, rows), 0) == rank, 1.0, 0.0).astype(bf16)
    sh, sl = split(stretch_ref[...])
    spread = mm(chosen, sh, ((0,), (0,))) + mm(chosen, sl, ((0,), (0,)))
    eye = iota((rows, rows), 0) == iota((rows, rows), 1)
    before = jnp.sum(jnp.where(eye & (rank < 0), 1.0, 0.0), axis=1, keepdims=True)
    before_ref[...] = jnp.broadcast_to(before, before_ref.shape)
    out_ref[...] = (hidden_ref[...].astype(f32) + spread).astype(bf16)


def entry_kernel(hidden_ref, mixed_ref, before_ref, prev_ref, out_ref):
    entry = (hidden_ref[...].astype(f32) + prev_ref[...]).astype(bf16)
    out_ref[...] = jnp.where(before_ref[:, :1] > 0.0, entry, mixed_ref[...])


def sds(shape, dtype):
    return jax.ShapeDtypeStruct(shape, dtype)


def call(kernel, outs, args, scalars=0, scratch=(), flops=10**5, megabytes=16, far_in=(), far_out=(), same=None):
    def spec(far, index):
        space = pltpu.SMEM if index < 0 else pltpu.HBM if index in far else pltpu.VMEM
        return pl.BlockSpec(memory_space=space)

    many = isinstance(outs, tuple)
    places = tuple(spec(far_out, i) for i in range(len(outs))) if many else spec(far_out, 0)
    return pl.pallas_call(
        kernel,
        out_shape=outs,
        in_specs=[spec(far_in, i - scalars) for i in range(len(args))],
        out_specs=places,
        scratch_shapes=list(scratch),
        input_output_aliases=same or {},
        compiler_params=pltpu.CompilerParams(vmem_limit_bytes=megabytes * 2**20),
        cost_estimate=pl.CostEstimate(flops=flops, bytes_accessed=flops // 100, transcendentals=0),
    )(*args)


def shards(
    bytes_in,
    norm_gain,
    qkv_weight,
    gate_weight_enc,
    decay_rate,
    write_bias,
    head_gain,
    boundaries,
    picks,
    pick_gates,
    extension,
    expert_gate,
    expert_up,
    expert_down,
):
    x = bytes_in[0]
    rows, width = x.shape
    dim = HALF // 2
    seq = lax.axis_index("seq")
    spot = lax.axis_index("coarse").astype(jnp.int32)[None]
    seq_total = lax.axis_size("seq")
    core = (seq % 2).astype(jnp.int32)[None]
    place = ((seq // 2) % GROUP).astype(jnp.int32)[None]
    local_slots = picks.shape[1]
    slot_total = local_slots * GROUP
    pair_total = local_slots * picks.shape[2]
    everywhere = ("coarse", "seq", "exp")

    def exchange(array, axes, **kwargs):
        return lax.all_to_all(array, axes, split_axis=0, concat_axis=0, tiled=True, **kwargs)

    top = picks.shape[2]
    shared = call(
        choice_kernel,
        sds((GROUP, expert_down.shape[1] + 2 * top, HALF), bf16),
        (picks[0].T, pick_gates[0].T, expert_down),
        scratch=(
            pltpu.VMEM((2 * top, HALF), f32),
            pltpu.VMEM((expert_down.shape[1] + 2 * top, HALF), bf16),
            pltpu.SemaphoreType.DMA((GROUP + 1,)),
        ),
        megabytes=63,
        far_in=(2,),
        far_out=(0,),
    )
    shared = exchange(shared, "coarse")
    table = (pltpu.VMEM((GROUP, 2 * top, HALF), bf16), pltpu.SemaphoreType.DMA)

    depth, hidden_units = expert_gate.shape[1:]
    columns = 2 * hidden_units
    gate_rows = gate_weight_enc.transpose(0, 2, 1)
    own, give, local, x_share, weights = call(
        delta_kernel,
        (
            sds((dim, HALF), f32),
            sds((dim, HALF), f32),
            sds((2, rows, HALF), f32),
            sds((rows, HALF), bf16),
            sds((depth, columns), bf16),
        ),
        (
            x,
            norm_gain[None],
            qkv_weight,
            gate_rows,
            decay_rate[None],
            write_bias[None],
            expert_gate,
            expert_up,
        ),
        scratch=(
            pltpu.VMEM((depth, columns), bf16),
            pltpu.VMEM((rows, width), bf16),
            pltpu.VMEM((1, width), f32),
            pltpu.VMEM(qkv_weight.shape, bf16),
            pltpu.VMEM(gate_rows.shape, bf16),
            pltpu.VMEM((1, 2), f32),
            pltpu.VMEM((1, 2), f32),
            pltpu.VMEM((8, dim, HALF), bf16),
            pltpu.VMEM((8, dim, dim), f32),
            pltpu.SemaphoreType.DMA((10 + PIECES,)),
        ),
        flops=2 * 10**9,
        megabytes=60,
        far_in=range(8),
        far_out=(4,),
    )

    give = call(after_kernel, sds(give.shape, f32), (shared, give), far_in=(0, 1), far_out=(0,), same={1: 0})

    swap = [(i, i ^ 1) for i in range(seq_total)]
    got = lax.ppermute(give, "seq", swap)
    own = call(stage_kernel, sds(own.shape, f32), (own,))
    rank = call(rank_kernel, sds((1, rows), jnp.int32), (boundaries,))
    take, routed = call(
        route_kernel,
        (
            sds((GROUP, pair_total, local_slots), bf16),
            sds((8, dim), f32),
        ),
        (boundaries, shared),
        scratch=table,
        far_in=(1,),
    )
    message, first = call(
        pair_kernel, (sds((GROUP, dim, HALF), bf16), sds((dim, HALF), f32)), (core, own, got), scalars=1
    )
    half = depth // 2
    ring = [(i, (i + 1) % GROUP) for i in range(GROUP)]
    back = [(b, a) for a, b in ring]
    left = lax.ppermute(weights, "coarse", ring)
    right = lax.ppermute(weights, "coarse", back)
    facing = (lax.ppermute(left[:half], "coarse", ring), lax.ppermute(right[half:], "coarse", back))
    stride = 2 * GROUP
    groups = [
        [stride * g + 2 * i + c for i in range(GROUP)] for g in range(seq_total // stride) for c in range(2)
    ]
    chips = exchange(message, "seq", axis_index_groups=groups)
    before, total = call(
        group_kernel, (sds((dim, HALF), f32), sds((dim, HALF), f32)), (place, chips), scalars=1, flops=10**9
    )
    state = jnp.zeros((dim, dim), bf16)
    for hop in range(seq_total // stride - 1):
        if hop == 0:
            outgoing = total[:, dim:].astype(bf16)
        else:
            outgoing = call(hop_kernel, sds((dim, dim), bf16), (total, state, routed), flops=10**9)
        pairs = [(stride * hop + i, stride * (hop + 1) + i) for i in range(stride)]
        state = state + lax.ppermute(outgoing, "seq", pairs)
    states = call(enter_kernel, sds((2, dim, dim), f32), (core, before, first, state), scalars=1, flops=10**9)
    others = lax.ppermute(states, "seq", swap)

    devices = lax.axis_size(everywhere)
    capacity = GROUP * pair_total // devices
    hidden, outgoing, picked = call(
        finish_kernel,
        (sds((rows, HALF), bf16), sds((devices, capacity, HALF), bf16), sds((8, dim), f32)),
        (core, local, states, others, x_share, head_gain[None], boundaries, rank, take, left, right),
        scalars=1,
        far_in=(8, 9),
    )
    received = exchange(outgoing, everywhere)
    weigh, weighed = call(
        weigh_kernel,
        (sds((GROUP, pair_total, local_slots), f32), sds((8, dim), f32)),
        (boundaries, shared, picked),
        scratch=table,
        far_in=(1,),
    )
    value = call(
        expert_kernel,
        sds((devices, capacity, HALF), bf16),
        (spot, received, extension.reshape(width // HALF, 1, HALF), weights, left, right, *facing, shared, weighed),
        scalars=1,
        scratch=(pltpu.VMEM((pair_total, 2 * hidden_units), f32), pltpu.VMEM((16, 2 * hidden_units), f32)),
    )
    returned = exchange(value, everywhere)
    stretch, last = call(
        combine_kernel,
        (sds((slot_total, HALF), f32), sds((1, HALF), f32)),
        (boundaries, weigh, returned),
    )
    previous = lax.ppermute(last, "seq", [(i, i + 1) for i in range(seq_total - 1)])
    mixed, early = call(
        spread_kernel, (sds((rows, HALF), bf16), sds((rows, dim), f32)), (hidden, rank, stretch), flops=10**9
    )
    mixed = call(entry_kernel, sds((rows, HALF), bf16), (hidden, mixed, early, previous))
    return mixed[None]


def solution(mesh):
    placed = (
        P("exp", "seq", None),
        P(),
        P(None, None, "coarse"),
        P(None, None, "coarse"),
        P("coarse"),
        P("coarse"),
        P("coarse"),
        P("exp", "seq"),
        P("exp", ("seq", "coarse"), None),
        P("exp", ("seq", "coarse"), None),
        P(),
        P(("seq", "exp"), "coarse", None),
        P(("seq", "exp"), "coarse", None),
        P(("seq", "exp"), None, "coarse"),
    )
    return jax.shard_map(
        shards, mesh=mesh, in_specs=placed, out_specs=P("exp", "seq", "coarse"), check_vma=False
    )
```
